512 devices in a mesh: lon: 32 (over z_lo, x, core), lat: 16 (over z_hi, y).
Axes of the slice: x: 4, y: 8, z: 8 (z_hi: 2, z_lo: 4; z = z_hi * 4 + z_lo), core: 2. Of those that a mesh axis runs over, the one named last changes fastest.
Arguments:
- tokens: bfloat16 [96, 768, 512], P('lat', 'lon'), may hold values from -10 to 10
- land_mask: int32 [96, 768], P('lat', 'lon'), may hold values 0 or 1
- keep_rows: int32 [96], replicated, may hold values from 0 to 1, as said below
- land_embed: float32 [2, 512], replicated, may hold values from -4 to 4
- norm_gains: float32 [2, 512], replicated, may hold values from 0.1 to 1.9
- w_qkv: bfloat16 [2, 512, 768], replicated, may hold values from -0.25 to 0.25
- w_proj: bfloat16 [2, 256, 512], replicated, may hold values from -0.375 to 0.375
- rel_bias: float32 [2, 8, 253], replicated, may hold values from -6 to 330
- cotangent: bfloat16 [96, 768, 512], P('lat', 'lon'), may hold values from -6 to 6
Outputs:
- output: float32 [96, 768, 512], P('lat', 'lon')
- grad_tokens: bfloat16 [96, 768, 512], P('lat', 'lon')
- grad_proj: bfloat16 [2, 256, 512], replicated
- grad_gains: float32 [2, 512], replicated
The draws below stay inside these ranges and needn't reach their ends.
Inputs may be any that keep to these rules, and one draw needn't show every extreme that they name: keep_rows[i] = 1 wherever i % 3 == 1, and wherever 96 // 4 <= i < 72.
All inputs are finite; a program needn't handle non-finite values. No bound on the sum of `land_mask` on one device may be relied on, other than what follows from the above.
Results may differ from the reference program's by a relative error of at most 0.015.
Values may be sent and summed in bfloat16 or wider, within the bound.
No kernel may reach another device: no remote copies, remote signals or barrier semaphores. Data moves between devices by JAX's collectives and lax.ppermute only.
A program may use at most 64 MiB of HBM per device.

```python
import jax
import jax.numpy as jnp
from jax import lax

D = 512
HEAD_DIM = 32
HEADS = 8
WIN_LAT = 6
WIN_LON = 12
INNER = 256
NREL = 253
NLAT = 96
NLON = 768
TOKENS = 73728


def draw_tokens(key, part):
    key = jax.random.fold_in(key, 11)
    scale_key, sample_key = jax.random.split(key, 2)
    feature_scale = jnp.exp(jax.random.uniform(scale_key, (D,), jnp.float32, jnp.log(0.25), jnp.log(2.5)))
    samples = jax.random.truncated_normal(sample_key, -4.0, 4.0, (NLAT, NLON, D), jnp.float32)
    return (samples * feature_scale).astype(jnp.bfloat16)


def draw_keep_rows(key, part):
    key = jax.random.fold_in(key, 23)
    rows_all = jnp.arange(NLAT, dtype=jnp.int32)
    coin_flip = jax.random.randint(key, (NLAT,), 0, 2, jnp.int32)
    polar_rows = (rows_all < NLAT // 4) | (rows_all >= NLAT - NLAT // 4)
    always_kept = rows_all % 3 == 1
    return jnp.where(polar_rows & jnp.logical_not(always_kept), coin_flip, 1).astype(jnp.int32)


def draw_rel_bias(key, part):
    key = jax.random.fold_in(key, 37)
    base_key = jax.random.fold_in(key, 0)
    table = 1.5 * jax.random.truncated_normal(base_key, -4.0, 4.0, (2, HEADS, NREL), jnp.float32)
    return table.astype(jnp.float32)


def touch_ends(array, stream_key, low, largest):
    place = [jax.random.randint(jax.random.fold_in(stream_key, axis), (), 0, length) for axis, length in enumerate(array.shape)]
    main_axis = array.shape.index(max(array.shape))
    next_to = place[:main_axis] + [(place[main_axis] + 1) % array.shape[main_axis]] + place[main_axis + 1:]
    return array.at[tuple(place)].set(low).at[tuple(next_to)].set(largest)


def block_levels(rng, shape, cuts, smallest, top_value):
    def one(dim, shards_of):
        steps = jax.random.uniform(jax.random.fold_in(jax.random.fold_in(rng, 6), dim), (shards_of,), jnp.float32, smallest / len(cuts), top_value / len(cuts))
        return jnp.repeat(jnp.exp(steps), shape[dim] // shards_of).reshape((-1,) + (1,) * (len(shape) - dim - 1))

    gain = one(*cuts[0])
    for cut in cuts[1:]:
        gain = gain * one(*cut)
    return gain


def scatter_about(stream_key, extent, width, most, cuts=(), held_as=jnp.bfloat16):
    array = jax.random.normal(stream_key, extent, jnp.float32) * width
    if len(cuts) > 0:
        array = block_levels(stream_key, extent, cuts, -0.22, 0.18) * array
    return jnp.clip(array, min=-most, max=most).astype(held_as)


def setup_inputs(seed: int = 0) -> dict:
    arg_keys = jax.random.split(jax.random.key(seed), 10)
    return {
        "tokens": draw_tokens(jax.random.fold_in(arg_keys[9], 71), 0),
        "land_mask": touch_ends((jax.random.randint(arg_keys[1], (NLAT, NLON), 0, 10) < 3).astype(jnp.int32), jax.random.fold_in(arg_keys[1], 1), 0, 1),
        "keep_rows": draw_keep_rows(jax.random.fold_in(arg_keys[9], 71), 0),
        "land_embed": scatter_about(arg_keys[3], (2, D), 1.0, 4.0, (), jnp.float32),
        "norm_gains": jnp.clip(1.0 + 0.18 * jax.random.normal(arg_keys[4], (2, D), jnp.float32), 0.1, 1.9),
        "w_qkv": scatter_about(arg_keys[5], (2, D, 3 * INNER), D ** -0.5, 0.25),
        "w_proj": scatter_about(arg_keys[6], (2, INNER, D), INNER ** -0.5, 0.375),
        "rel_bias": draw_rel_bias(jax.random.fold_in(arg_keys[9], 71), 0),
        "cotangent": scatter_about(arg_keys[8], (NLAT, NLON, D), 1.0, 6.0, ((0, 16), (1, 32))),
    }


NORM_EPS = 1e-05

def layer_norm(values, gain_row):
    row_mean = lax.optimization_barrier(jnp.mean(values, axis=-1, keepdims=True))
    centred = values - row_mean
    row_var = lax.optimization_barrier(jnp.mean(centred * centred, axis=-1, keepdims=True))
    inv_std = lax.rsqrt(row_var + NORM_EPS)
    unit_rows = centred * inv_std
    return ((unit_rows * gain_row).astype(jnp.bfloat16), unit_rows, inv_std)

def norm_back(d_normed, unit_rows, inv_std, gain_row):
    d_float = d_normed.astype(jnp.float32)
    d_unit = d_float * gain_row
    mean_grad = lax.optimization_barrier(jnp.mean(d_unit, axis=-1, keepdims=True))
    mean_proj = lax.optimization_barrier(jnp.mean(d_unit * unit_rows, axis=-1, keepdims=True))
    d_input = inv_std * (d_unit - mean_grad - unit_rows * mean_proj)
    token_axes = tuple(range(unit_rows.ndim - 1))
    return (d_input, lax.optimization_barrier(jnp.sum(d_float * unit_rows, axis=token_axes)))

def to_windows(field_grid):
    rows_all, cols_all = (field_grid.shape[0], field_grid.shape[1])
    trailing = tuple(field_grid.shape[2:])
    blocked = field_grid.reshape((rows_all // WIN_LAT, WIN_LAT, cols_all // WIN_LON, WIN_LON) + trailing)
    blocked = jnp.swapaxes(blocked, 1, 2)
    return blocked.reshape((rows_all // WIN_LAT, cols_all // WIN_LON, WIN_LAT * WIN_LON) + trailing)

def from_windows(blocked, rows_all, cols_all):
    trailing = tuple(blocked.shape[3:])
    reshaped = blocked.reshape((rows_all // WIN_LAT, cols_all // WIN_LON, WIN_LAT, WIN_LON) + trailing)
    reshaped = jnp.swapaxes(reshaped, 1, 2)
    return reshaped.reshape((rows_all, cols_all) + trailing)

def relative_table(rel_bias):
    positions = jnp.arange(WIN_LAT * WIN_LON, dtype=jnp.int32)
    rows_in = positions // WIN_LON
    cols_in = positions % WIN_LON
    table_index = (rows_in[:, None] - rows_in[None, :] + WIN_LAT - 1) * (2 * WIN_LON - 1) + cols_in[:, None] - cols_in[None, :] + WIN_LON - 1
    return rel_bias[:, :, table_index]

def key_allowed(keep_win, region_win):
    same_region = region_win[:, :, None] == region_win[:, None, :]
    return same_region & (keep_win[:, None, :] == 1)

def split_heads(qkv_win):
    pieces = qkv_win.reshape(qkv_win.shape[0], qkv_win.shape[1], 3, HEADS, HEAD_DIM)
    return (pieces[:, :, 0], pieces[:, :, 1], pieces[:, :, 2])

def attend(qkv_win, pos_bias, allowed):
    queries, keys_in, values = split_heads(qkv_win)
    scores = jnp.einsum('wqhd,wkhd->whqk', queries.astype(jnp.float32), keys_in.astype(jnp.float32)) * HEAD_DIM ** (-0.5) + pos_bias[None]
    scores = jnp.where(allowed[:, None], scores, -jnp.inf)
    row_max = lax.optimization_barrier(jnp.max(scores, axis=-1, keepdims=True))
    exp_scores = jnp.exp(scores - row_max)
    attn_probs = exp_scores / lax.optimization_barrier(jnp.sum(exp_scores, axis=-1, keepdims=True))
    probs_low = lax.optimization_barrier(attn_probs.astype(jnp.bfloat16)).astype(jnp.float32)
    head_out = jnp.einsum('whqk,wkhd->wqhd', probs_low, values.astype(jnp.float32))
    head_out = head_out.astype(jnp.bfloat16)
    return (head_out.reshape(qkv_win.shape[0], qkv_win.shape[1], HEADS * HEAD_DIM), attn_probs)

def attend_back(d_out, qkv_win, attn_probs):
    queries, keys_in, values = split_heads(qkv_win)
    window_count, win_size = (qkv_win.shape[0], qkv_win.shape[1])
    d_heads = d_out.reshape(window_count, win_size, HEADS, HEAD_DIM).astype(jnp.float32)
    probs_low = lax.optimization_barrier(attn_probs.astype(jnp.bfloat16)).astype(jnp.float32)
    d_values = jnp.einsum('whqk,wqhd->wkhd', probs_low, d_heads).astype(jnp.bfloat16)
    d_probs = jnp.einsum('wqhd,wkhd->whqk', d_heads, values.astype(jnp.float32))
    d_scores = attn_probs * (d_probs - lax.optimization_barrier(jnp.sum(d_probs * attn_probs, axis=-1, keepdims=True))) * HEAD_DIM ** (-0.5)
    d_low = lax.optimization_barrier(d_scores.astype(jnp.bfloat16)).astype(jnp.float32)
    d_queries = jnp.einsum('whqk,wkhd->wqhd', d_low, keys_in.astype(jnp.float32)).astype(jnp.bfloat16)
    d_keys = jnp.einsum('whqk,wqhd->wkhd', d_low, queries.astype(jnp.float32)).astype(jnp.bfloat16)
    stacked = jnp.stack([d_queries, d_keys, d_values], axis=2)
    return stacked.reshape(window_count, win_size, 3 * HEADS * HEAD_DIM)

def attention_grid(qkv_grid, pos_bias, keep_grid, region_grid):

    def one_band(band_in):
        qkv_band, keep_band, region_band = band_in
        head_out, unused = attend(qkv_band, pos_bias, key_allowed(keep_band, region_band))
        return head_out
    out_win = lax.map(one_band, (to_windows(qkv_grid), to_windows(keep_grid), to_windows(region_grid)))
    return from_windows(out_win, NLAT, NLON)

def attention_grid_back(d_grid, qkv_grid, pos_bias, keep_grid, region_grid):

    def one_band(band_in):
        d_band, qkv_band, keep_band, region_band = band_in
        unused, attn_probs = attend(qkv_band, pos_bias, key_allowed(keep_band, region_band))
        return attend_back(d_band, qkv_band, attn_probs)
    out_win = lax.map(one_band, (to_windows(d_grid), to_windows(qkv_grid), to_windows(keep_grid), to_windows(region_grid)))
    return from_windows(out_win, NLAT, NLON)

def project(field_grid, weight):
    return jnp.dot(field_grid, weight, preferred_element_type=jnp.float32).astype(jnp.bfloat16)

def outer_sum(left_grid, right_grid):
    left_flat = left_grid.reshape(-1, left_grid.shape[-1])
    right_flat = right_grid.reshape(-1, right_grid.shape[-1])
    return jnp.dot(left_flat.T, right_flat, preferred_element_type=jnp.float32)

def roll_in(field_grid):
    return jnp.roll(field_grid, (-(WIN_LAT // 2), -(WIN_LON // 2)), axis=(0, 1))

def roll_out(field_grid):
    return jnp.roll(field_grid, (WIN_LAT // 2, WIN_LON // 2), axis=(0, 1))

def reference(tokens, land_mask, keep_rows, land_embed, norm_gains, w_qkv, w_proj, rel_bias, cotangent):
    half_lat = WIN_LAT // 2
    pos_bias = relative_table(rel_bias)
    row_ids = jnp.arange(NLAT, dtype=jnp.int32)
    keep_one = jnp.broadcast_to(keep_rows[:, None], (NLAT, NLON))
    region_one = jnp.zeros((NLAT, NLON), jnp.int32)
    keep_two = jnp.broadcast_to(jnp.roll(keep_rows, -half_lat)[:, None], (NLAT, NLON))
    region_two = jnp.broadcast_to((row_ids >= NLAT - half_lat).astype(jnp.int32)[:, None], (NLAT, NLON))
    embedded = tokens.astype(jnp.float32) + jnp.where(land_mask[:, :, None] == 1, land_embed[1], land_embed[0])
    normed_one, unit_one, inv_one = layer_norm(embedded, norm_gains[0])
    qkv_one = project(normed_one, w_qkv[0])
    heads_one = attention_grid(qkv_one, pos_bias[0], keep_one, region_one)
    branch_one = project(heads_one, w_proj[0])
    stream = embedded + branch_one.astype(jnp.float32)
    normed_two, unit_two, inv_two = layer_norm(stream, norm_gains[1])
    qkv_two = project(roll_in(normed_two), w_qkv[1])
    heads_two = attention_grid(qkv_two, pos_bias[1], keep_two, region_two)
    branch_two = roll_out(project(heads_two, w_proj[1]))
    output = stream + branch_two.astype(jnp.float32)
    cot_rolled = roll_in(cotangent)
    d_heads_two = project(cot_rolled, w_proj[1].T)
    d_qkv_two = attention_grid_back(d_heads_two, qkv_two, pos_bias[1], keep_two, region_two)
    d_normed_two = roll_out(project(d_qkv_two, w_qkv[1].T))
    d_branch_two, gain_two = norm_back(d_normed_two, unit_two, inv_two, norm_gains[1])
    d_stream = (cotangent.astype(jnp.float32) + d_branch_two).astype(jnp.bfloat16)
    d_heads_one = project(d_stream, w_proj[0].T)
    d_qkv_one = attention_grid_back(d_heads_one, qkv_one, pos_bias[0], keep_one, region_one)
    d_normed_one = project(d_qkv_one, w_qkv[0].T)
    d_branch_one, gain_one = norm_back(d_normed_one, unit_one, inv_one, norm_gains[0])
    grad_tokens = (d_stream.astype(jnp.float32) + d_branch_one).astype(jnp.bfloat16)
    scale_out = float(TOKENS) ** (-0.5)
    proj_one = outer_sum(heads_one, d_stream)
    proj_two = outer_sum(heads_two, cot_rolled)
    grad_proj = (jnp.stack([proj_one, proj_two]) * scale_out).astype(jnp.bfloat16)
    grad_gains = jnp.stack([gain_one, gain_two]) * scale_out
    return (output, grad_tokens, grad_proj, grad_gains)
```

```python
import functools

import jax
import jax.numpy as jnp
import numpy as np
from jax import lax
from jax.experimental import pallas as pl
from jax.experimental.pallas import tpu as pltpu
from jax.sharding import PartitionSpec as P

D = 512
HEAD_DIM = 32
HEADS = 8
INNER = HEADS * HEAD_DIM
WIN_LAT = 6
WIN_LON = 12
HALF_LAT = WIN_LAT // 2
HALF_LON = WIN_LON // 2
WIN = WIN_LAT * WIN_LON
SPAN_LON = 2 * WIN_LON - 1
REACH = WIN_LAT * SPAN_LON
QPAD = 128
STACK = WIN * HEADS
GAIN_ROWS = 8

NORM_EPS = 1e-05
SCALE = HEAD_DIM ** (-0.5)
SHUT = -1e30

F32 = jnp.float32
BF16 = jnp.bfloat16


def dot_nn(left, right):
    return lax.dot_general(left, right, (((1,), (0,)), ((), ())), preferred_element_type=F32)


def dot_nt(left, right):
    return lax.dot_general(left, right, (((1,), (1,)), ((), ())), preferred_element_type=F32)


def dot_tn(left, right):
    return lax.dot_general(left, right, (((0,), (0,)), ((), ())), preferred_element_type=F32)


def window_matrices(cols):
    cells, count = WIN_LAT * cols, cols // WIN_LON
    order = np.zeros((count, QPAD, cells), np.float32)
    spread = np.zeros((count, WIN, HEADS, cells), np.float32)
    for w in range(count):
        for a in range(WIN_LAT):
            for e in range(WIN_LON):
                cell = a * cols + w * WIN_LON + e
                order[w, e * WIN_LAT + a, cell] = 1
                spread[w, e * WIN_LAT + a, :, cell] = 1
    return order.reshape(-1, cells), spread.reshape(-1, cells)


def reach_matrix():
    reach = np.zeros((REACH, WIN_LON, QPAD), np.float32)
    for e2 in range(WIN_LON):
        for a in range(WIN_LAT):
            for e in range(WIN_LON):
                reach[a * SPAN_LON + e - e2 + WIN_LON - 1, e2, e * WIN_LAT + a] = 1
    return reach.reshape(REACH, -1)


def roll_matrices(cols, direction):
    cells = WIN_LAT * cols
    own = np.zeros((cells, cells), np.float32)
    side = np.zeros((cells, WIN_LAT * HALF_LON), np.float32)
    far = np.zeros((cells, HALF_LAT * cols), np.float32)
    for i in range(WIN_LAT):
        for j in range(cols):
            row = i * cols + j
            from_i, from_j = i + direction * HALF_LAT, j + direction * HALF_LON
            if not 0 <= from_i < WIN_LAT:
                far[row, (from_i % WIN_LAT - (0 if direction > 0 else HALF_LAT)) * cols + j] = 1
            elif not 0 <= from_j < cols:
                side[row, from_i * HALF_LON + (from_j - cols if direction > 0 else from_j + HALF_LON)] = 1
            else:
                own[row, from_i * cols + from_j] = 1
    return own, side, far


def edge_matrix(cols, direction):
    edge = np.zeros((WIN_LAT, HALF_LON, WIN_LAT * cols), np.float32)
    for i in range(WIN_LAT):
        for j in range(HALF_LON):
            edge[i, j, i * cols + (j if direction > 0 else cols - HALF_LON + j)] = 1
    return edge.reshape(-1, WIN_LAT * cols)


def fixed(matrix):
    return jnp.asarray(matrix, BF16)


def norm_stats(values):
    row_mean = jnp.sum(values, axis=-1, keepdims=True) * (1.0 / D)
    centred = values - row_mean
    row_var = jnp.sum(centred * centred, axis=-1, keepdims=True) * (1.0 / D)
    inv_std = lax.rsqrt(row_var + NORM_EPS)
    return centred * inv_std, inv_std


def norm_back(d_float, unit_rows, inv_std, gain_row):
    d_unit = d_float * gain_row
    mean_grad = jnp.sum(d_unit, axis=-1, keepdims=True) * (1.0 / D)
    mean_proj = jnp.sum(d_unit * unit_rows, axis=-1, keepdims=True) * (1.0 / D)
    d_input = inv_std * (d_unit - mean_grad - unit_rows * mean_proj)
    return d_input, jnp.sum(d_float * unit_rows, axis=0, keepdims=True)


def masked_bias(table, reach, keep_of, split_rows):
    shifted = jnp.concatenate(
        [
            table[:, (WIN_LAT - 1 - a2) * SPAN_LON : (WIN_LAT - 1 - a2) * SPAN_LON + REACH]
            for a2 in range(WIN_LAT)
        ],
        axis=0,
    )
    high = shifted.astype(BF16)
    rest = shifted - high.astype(F32)
    middle = rest.astype(BF16)
    low = (rest - middle.astype(F32)).astype(BF16)
    spread = dot_nn(high, reach) + (dot_nn(middle, reach) + dot_nn(low, reach))
    place = lax.broadcasted_iota(jnp.int32, (HEADS, QPAD), 1)
    query_late = jnp.where(place % WIN_LAT >= HALF_LAT, 1, 0)
    tiles = []
    for a2 in range(WIN_LAT):
        key_late = 1 if a2 >= HALF_LAT else 0
        apart = jnp.where(query_late == key_late, 0, 1) * split_rows
        shut = apart + jnp.where(keep_of(a2) == 1, 0, 1)
        tiles.append(jnp.where(shut > 0, SHUT, 0.0).astype(F32))
    tile = jnp.concatenate(tiles, axis=0)
    blocks = [spread[:, QPAD * e2 : QPAD * (e2 + 1)] + tile for e2 in range(WIN_LON)]
    return jnp.concatenate(blocks, axis=0).reshape(WIN, HEADS, QPAD)


def lay_out(qkv, order, spread):
    count = order.shape[0] // QPAD
    queries = dot_nn(order, qkv[:, :INNER]).astype(BF16)
    stacked = dot_nn(spread, qkv[:, INNER:])
    head = lax.broadcasted_iota(jnp.int32, (HEADS, 2 * INNER), 0)
    lane = lax.broadcasted_iota(jnp.int32, (HEADS, 2 * INNER), 1)
    own = jnp.where((lane // HEAD_DIM) % HEADS == head, 1.0, 0.0).astype(F32)
    stacked = stacked.reshape(count * WIN, HEADS, 2 * INNER) * own[None]
    stacked = stacked.reshape(count * STACK, 2 * INNER).astype(BF16)
    return queries, stacked[:, :INNER], stacked[:, INNER:], own


def attend(queries, keys, values, bias, order_back):
    count = queries.shape[0] // QPAD
    all_probs, outs = [], []
    for w in range(count):
        rows = slice(w * STACK, (w + 1) * STACK)
        scores = dot_nt(keys[rows], queries[w * QPAD : (w + 1) * QPAD])
        scores = scores.reshape(WIN, HEADS, QPAD) * SCALE + bias
        exp_scores = jnp.exp(scores - jnp.max(scores, axis=0, keepdims=True))
        probs = exp_scores * (1.0 / jnp.sum(exp_scores, axis=0, keepdims=True))
        all_probs.append(probs)
        low = probs.reshape(STACK, QPAD).astype(BF16)
        outs.append(dot_tn(low, values[rows]).astype(BF16))
    heads = dot_nn(order_back, jnp.concatenate(outs, axis=0)).astype(BF16)
    return heads, all_probs


def attend_back(d_heads, all_probs, queries, keys, values, own, order, order_back, spread_back):
    d_out = dot_nn(order, d_heads).astype(BF16)
    d_queries, d_stack = [], []
    for w, probs in enumerate(all_probs):
        rows = slice(w * STACK, (w + 1) * STACK)
        here = slice(w * QPAD, (w + 1) * QPAD)
        d_probs = dot_nt(values[rows], d_out[here]).reshape(WIN, HEADS, QPAD)
        total = jnp.sum(d_probs * probs, axis=0, keepdims=True)
        d_low = (probs * (d_probs - total) * SCALE).reshape(STACK, QPAD).astype(BF16)
        low = probs.reshape(STACK, QPAD).astype(BF16)
        d_queries.append(dot_tn(d_low, keys[rows]).astype(BF16))
        d_keys = dot_nn(d_low, queries[here])
        d_values = dot_nn(low, d_out[here])
        both = jnp.concatenate([d_keys, d_values], axis=1).reshape(WIN, HEADS, 2 * INNER) * own[None]
        d_stack.append(both.reshape(STACK, 2 * INNER).astype(BF16))
    d_query_grid = dot_nn(order_back, jnp.concatenate(d_queries, axis=0)).astype(BF16)
    d_rest = dot_nn(spread_back, jnp.concatenate(d_stack, axis=0)).astype(BF16)
    return jnp.concatenate([d_query_grid, d_rest], axis=1)


def first_kernel(
    row_ref, keep_ref, tokens_ref, mask_ref, embed_ref, gains_ref, w_qkv_ref, w_proj_ref, table_ref, cot_ref,
    order_ref, order_back_ref, spread_ref, reach_ref, edge_ref,
    stream_ref, unit_one_ref, inv_one_ref, qkv_ref, heads_ref, probs_ref, normed_ref, strip_ref,
):
    rows, cols = mask_ref.shape
    mask = mask_ref[...].astype(F32)
    spread_mask = jnp.concatenate([jnp.broadcast_to(mask[r : r + 1], (cols, cols)) for r in range(rows)], axis=0)
    cell = lax.broadcasted_iota(jnp.int32, (rows * cols, cols), 0)
    lane = lax.broadcasted_iota(jnp.int32, (rows * cols, cols), 1)
    land = jnp.sum(jnp.where(cell % cols == lane, spread_mask, 0.0), axis=1, keepdims=True)
    embedded = tokens_ref[...].astype(F32) + jnp.where(land == 1.0, embed_ref[1:2], embed_ref[0:1])
    unit_one, inv_one = norm_stats(embedded)
    unit_one_ref[...] = unit_one
    inv_one_ref[...] = jnp.broadcast_to(inv_one, inv_one_ref.shape)
    normed_one = (unit_one * gains_ref[0:1]).astype(BF16)
    qkv = dot_nn(normed_one, w_qkv_ref[0]).astype(BF16)
    qkv_ref[...] = qkv
    bias = masked_bias(table_ref[0], reach_ref[...], lambda a2: keep_ref[row_ref[0] + a2], 0)
    queries, keys, values, own = lay_out(qkv, order_ref[...], spread_ref[...])
    heads, all_probs = attend(queries, keys, values, bias, order_back_ref[...])
    for w, probs in enumerate(all_probs):
        probs_ref[w] = probs
    heads_ref[...] = heads
    branch = dot_nn(heads, w_proj_ref[0]).astype(BF16)
    stream = embedded + branch.astype(F32)
    stream_ref[...] = stream
    unit_two, _ = norm_stats(stream)
    normed_two = (unit_two * gains_ref[1:2]).astype(BF16)
    normed_ref[...] = normed_two
    edge = edge_ref[...]
    strip_ref[:, :D] = dot_nn(edge, normed_two).astype(BF16)
    strip_ref[:, D:] = dot_nn(edge, cot_ref[...]).astype(BF16)


def second_kernel(
    row_ref, keep_ref, normed_ref, cot_ref, landed_ref, arrived_ref, w_qkv_ref, w_proj_ref, table_ref,
    order_ref, order_back_ref, spread_ref, spread_back_ref, reach_ref, own_ref, side_ref, far_ref, edge_ref,
    back_ref, strip_ref, proj_ref,
):
    lat_count = keep_ref.shape[0]
    far_part = dot_nn(side_ref[...], landed_ref[...]) + dot_nn(far_ref[...], arrived_ref[...])
    normed = (dot_nn(own_ref[...], normed_ref[...]) + far_part[:, :D]).astype(BF16)
    carried = (dot_nn(own_ref[...], cot_ref[...]) + far_part[:, D:]).astype(BF16)
    last_band = jnp.where(row_ref[0] + WIN_LAT >= lat_count, 1, 0)

    def keep_of(a2):
        place = row_ref[0] + (a2 + HALF_LAT)
        return keep_ref[jnp.where(place >= lat_count, place - lat_count, place)]

    bias = masked_bias(table_ref[0], reach_ref[...], keep_of, last_band)
    order, order_back = order_ref[...], order_back_ref[...]
    qkv = dot_nn(normed, w_qkv_ref[0]).astype(BF16)
    d_heads = dot_nt(carried, w_proj_ref[0]).astype(BF16)
    queries, keys, values, own = lay_out(qkv, order, spread_ref[...])
    heads, all_probs = attend(queries, keys, values, bias, order_back)
    branch = dot_nn(heads, w_proj_ref[0]).astype(BF16)
    proj_ref[...] = dot_tn(heads, carried).astype(BF16)
    d_qkv = attend_back(d_heads, all_probs, queries, keys, values, own, order, order_back, spread_back_ref[...])
    d_normed = dot_nt(d_qkv, w_qkv_ref[0]).astype(BF16)
    both = jnp.concatenate([branch, d_normed], axis=1)
    back_ref[...] = both
    strip_ref[...] = dot_nn(edge_ref[...], both).astype(BF16)


def third_kernel(
    stream_ref, unit_one_ref, inv_one_ref, qkv_ref, heads_ref, probs_ref, cot_ref, back_ref, landed_ref, arrived_ref,
    gains_ref, w_qkv_ref, w_proj_ref, proj_two_ref,
    order_ref, order_back_ref, spread_ref, spread_back_ref, own_ref, side_ref, far_ref,
    output_ref, grad_ref, sums_ref,
):
    unrolled = (
        dot_nn(own_ref[...], back_ref[...])
        + dot_nn(side_ref[...], landed_ref[...])
        + dot_nn(far_ref[...], arrived_ref[...])
    )
    stream = stream_ref[...]
    output_ref[...] = stream + unrolled[:, :D]
    unit_two, inv_two = norm_stats(stream)
    d_branch, gain_two = norm_back(unrolled[:, D:], unit_two, inv_two, gains_ref[1:2])
    d_stream = (cot_ref[...].astype(F32) + d_branch).astype(BF16)
    proj_one = dot_tn(heads_ref[...], d_stream)
    d_heads = dot_nt(d_stream, w_proj_ref[0]).astype(BF16)
    order = order_ref[...]
    queries, keys, values, own = lay_out(qkv_ref[...], order, spread_ref[...])
    all_probs = [probs_ref[w] for w in range(probs_ref.shape[0])]
    d_qkv = attend_back(
        d_heads, all_probs, queries, keys, values, own, order, order_back_ref[...], spread_back_ref[...]
    )
    d_normed = dot_nt(d_qkv, w_qkv_ref[0]).astype(BF16)
    d_branch, gain_one = norm_back(d_normed.astype(F32), unit_one_ref[...], inv_one_ref[:, 0:1], gains_ref[0:1])
    grad_ref[...] = (d_stream.astype(F32) + d_branch).astype(BF16)
    shards, share = sums_ref.shape[0], sums_ref.shape[1]
    half = shards // 2
    sums_ref[:half, :, :D] = proj_one.reshape(half, share, D).astype(BF16)
    sums_ref[half:, :, :D] = proj_two_ref[...].astype(F32).reshape(half, share, D).astype(BF16)
    gain = jnp.concatenate(
        [row[:, 128 * j : 128 * (j + 1)] for row in (gain_one, gain_two) for j in range(D // 128)], axis=0
    )
    pair = gain_pair(gain, share)
    for s in range(shards):
        sums_ref[s, :, D:] = pair


def gain_pair(gain, share):
    high = gain.astype(BF16).astype(F32)
    parts = [high, gain - high]
    if share > 2 * GAIN_ROWS:
        parts.append(jnp.zeros((share - 2 * GAIN_ROWS, 128), F32))
    return jnp.concatenate(parts, axis=0).astype(BF16)


def added(parts_ref):
    total = parts_ref[0].astype(F32)
    for s in range(1, parts_ref.shape[0]):
        total = total + parts_ref[s].astype(F32)
    gain = total[:GAIN_ROWS, D:] + total[GAIN_ROWS : 2 * GAIN_ROWS, D:]
    return total[:, :D], gain


def lon_sum_kernel(parts_ref, out_ref):
    proj, gain = added(parts_ref)
    low = proj.astype(BF16)
    pair = gain_pair(gain, parts_ref.shape[1])
    for s in range(out_ref.shape[0]):
        out_ref[s, :, :D] = low
        out_ref[s, :, D:] = pair


def lat_sum_kernel(scale, parts_ref, proj_ref, gains_ref):
    proj, gain = added(parts_ref)
    low = (proj * scale).astype(BF16)
    for s in range(proj_ref.shape[0]):
        proj_ref[s] = low
    gain = gain * scale
    per_row = D // 128
    for r in range(GAIN_ROWS):
        gains_ref[r // per_row : r // per_row + 1, 128 * (r % per_row) : 128 * (r % per_row + 1)] = gain[r : r + 1]


def call(kernel, outs, operands):
    specs, arrays = [], []
    for operand in operands:
        if not isinstance(operand, tuple):
            specs.append(pl.BlockSpec(memory_space=pltpu.VMEM))
            arrays.append(operand)
        elif operand[0] == "scalars":
            specs.append(pl.BlockSpec(memory_space=pltpu.SMEM))
            arrays.append(operand[1])
        else:
            layer, array = operand
            rest = tuple(array.shape[1:])
            specs.append(pl.BlockSpec((1,) + rest, functools.partial(lambda b, i: (b,) + (0,) * 2, layer)))
            arrays.append(array)
    whole = [
        spec if spec.block_shape is not None or spec.memory_space == pltpu.SMEM
        else pl.BlockSpec(array.shape, functools.partial(lambda n, i: (0,) * n, array.ndim))
        for spec, array in zip(specs, arrays)
    ]
    out_specs = [pl.BlockSpec(o.shape, functools.partial(lambda n, i: (0,) * n, len(o.shape))) for o in outs]
    return pl.pallas_call(
        kernel,
        grid=(1,),
        in_specs=whole,
        out_specs=out_specs,
        out_shape=outs,
        compiler_params=pltpu.CompilerParams(vmem_limit_bytes=50 * 1024 * 1024),
    )(*arrays)


def passed_along(array, axis, by):
    length = lax.axis_size(axis)
    return lax.ppermute(array, axis, [(i, (i + by) % length) for i in range(length)])


def shape(*dims, dtype=BF16):
    return jax.ShapeDtypeStruct(dims, dtype)


def local(tokens, land_mask, keep_rows, land_embed, norm_gains, w_qkv, w_proj, rel_bias, cotangent):
    rows, cols = tokens.shape[0], tokens.shape[1]
    cells, count = rows * cols, cols // WIN_LON
    lon_size, lat_size = lax.axis_size("lon"), lax.axis_size("lat")
    scale_out = float(rows * lat_size * cols * lon_size) ** (-0.5)
    share = 2 * INNER // lon_size
    row_first = (lax.axis_index("lat") * rows).astype(jnp.int32).reshape(1)
    order, spread = window_matrices(cols)
    order, order_back, spread, spread_back = (fixed(m) for m in (order, order.T, spread, spread.T))
    reach = fixed(reach_matrix())
    cot_flat = cotangent.reshape(cells, D)
    rows_in, keep_in = ("scalars", row_first), ("scalars", keep_rows)

    stream, unit_one, inv_one, qkv_one, heads_one, probs_one, normed_two, strip = call(
        first_kernel,
        [
            shape(cells, D, dtype=F32), shape(cells, D, dtype=F32), shape(cells, 128, dtype=F32),
            shape(cells, 3 * INNER), shape(cells, INNER), shape(count, WIN, HEADS, QPAD, dtype=F32),
            shape(cells, D), shape(rows * HALF_LON, 2 * D),
        ],
        [
            rows_in, keep_in, tokens.reshape(cells, D), land_mask, land_embed, norm_gains, (0, w_qkv), (0, w_proj),
            (0, rel_bias), cot_flat, order, order_back, spread, reach, fixed(edge_matrix(cols, 1)),
        ],
    )

    landed = passed_along(strip, "lon", -1)
    inside = slice(HALF_LON, None)
    own_edge = jnp.concatenate(
        [normed_two.reshape(rows, cols, D)[:HALF_LAT, inside], cotangent[:HALF_LAT, inside]], axis=2
    )
    edge_rows = jnp.concatenate([own_edge, landed.reshape(rows, HALF_LON, 2 * D)[:HALF_LAT]], axis=1)
    arrived = passed_along(edge_rows, "lat", -1).reshape(HALF_LAT * cols, 2 * D)

    back, strip, proj_two = call(
        second_kernel,
        [shape(cells, 2 * D), shape(rows * HALF_LON, 2 * D), shape(INNER, D)],
        [
            rows_in, keep_in, normed_two, cot_flat, landed, arrived, (1, w_qkv), (1, w_proj), (1, rel_bias),
            order, order_back, spread, spread_back, reach, *(fixed(m) for m in roll_matrices(cols, 1)),
            fixed(edge_matrix(cols, -1)),
        ],
    )

    landed = passed_along(strip, "lon", 1)
    own_edge = back.reshape(rows, cols, 2 * D)[HALF_LAT:, : cols - HALF_LON]
    edge_rows = jnp.concatenate([landed.reshape(rows, HALF_LON, 2 * D)[HALF_LAT:], own_edge], axis=1)
    arrived = passed_along(edge_rows, "lat", 1).reshape(HALF_LAT * cols, 2 * D)

    output, grad_tokens, sums = call(
        third_kernel,
        [shape(cells, D, dtype=F32), shape(cells, D), shape(lon_size, share, D + 128)],
        [
            stream, unit_one, inv_one, qkv_one, heads_one, probs_one, cot_flat, back, landed, arrived, norm_gains,
            (0, w_qkv), (0, w_proj), proj_two, order, order_back, spread, spread_back,
            *(fixed(m) for m in roll_matrices(cols, -1)),
        ],
    )

    parts = lax.all_to_all(sums, "lon", 0, 0, tiled=True)
    (lon_sums,) = call(lon_sum_kernel, [shape(lat_size, share, D + 128)], [parts])
    parts = lax.all_to_all(lon_sums, "lat", 0, 0, tiled=True)
    proj, grad_gains = call(
        functools.partial(lat_sum_kernel, scale_out), [shape(lon_size, share, D), shape(2, D, dtype=F32)], [parts]
    )
    grad_proj = lax.all_to_all(proj, "lon", 0, 0, tiled=True).reshape(2, INNER, D)
    return output.reshape(rows, cols, D), grad_tokens.reshape(rows, cols, D), grad_proj, grad_gains


def solution(mesh):
    in_specs = (
        P("lat", "lon", None),
        P("lat", "lon"),
        P(),
        P(),
        P(),
        P(),
        P(),
        P(),
        P("lat", "lon", None),
    )
    out_specs = (P("lat", "lon", None), P("lat", "lon", None), P(), P())
    return jax.shard_map(local, mesh=mesh, in_specs=in_specs, out_specs=out_specs, check_vma=False)
```

```python
import functools

import jax
import jax.numpy as jnp
import numpy as np
from jax import lax
from jax.experimental import pallas as pl
from jax.experimental.pallas import tpu as pltpu
from jax.sharding import Mesh
from jax.sharding import PartitionSpec as P

D = 512
HEAD_DIM = 32
HEADS = 8
INNER = HEADS * HEAD_DIM
WIN_LAT = 6
WIN_LON = 12
HALF_LAT = WIN_LAT // 2
HALF_LON = WIN_LON // 2
WIN = WIN_LAT * WIN_LON
SPAN_LON = 2 * WIN_LON - 1
REACH = WIN_LAT * SPAN_LON
QPAD = 128
STACK = WIN * HEADS
GAIN_ROWS = 8

NORM_EPS = 1e-05
SCALE = HEAD_DIM ** (-0.5)
SHUT = -1e30

F32 = jnp.float32
BF16 = jnp.bfloat16


def dot_nn(left, right):
    return lax.dot_general(left, right, (((1,), (0,)), ((), ())), preferred_element_type=F32)


def dot_nt(left, right):
    return lax.dot_general(left, right, (((1,), (1,)), ((), ())), preferred_element_type=F32)


def dot_tn(left, right):
    return lax.dot_general(left, right, (((0,), (0,)), ((), ())), preferred_element_type=F32)


def window_matrices(cols):
    cells, count = WIN_LAT * cols, cols // WIN_LON
    order = np.zeros((count, QPAD, cells), np.float32)
    spread = np.zeros((count, WIN, HEADS, cells), np.float32)
    for w in range(count):
        for a in range(WIN_LAT):
            for e in range(WIN_LON):
                cell = a * cols + w * WIN_LON + e
                order[w, e * WIN_LAT + a, cell] = 1
                spread[w, e * WIN_LAT + a, :, cell] = 1
    return order.reshape(-1, cells), spread.reshape(-1, cells)


def reach_matrix():
    reach = np.zeros((REACH, WIN_LON, QPAD), np.float32)
    for e2 in range(WIN_LON):
        for a in range(WIN_LAT):
            for e in range(WIN_LON):
                reach[a * SPAN_LON + e - e2 + WIN_LON - 1, e2, e * WIN_LAT + a] = 1
    return reach.reshape(REACH, -1)


def roll_matrices(cols, direction):
    cells = WIN_LAT * cols
    own = np.zeros((cells, cells), np.float32)
    side = np.zeros((cells, WIN_LAT * HALF_LON), np.float32)
    far = np.zeros((cells, HALF_LAT * cols), np.float32)
    for i in range(WIN_LAT):
        for j in range(cols):
            row = i * cols + j
            from_i, from_j = i + direction * HALF_LAT, j + direction * HALF_LON
            if not 0 <= from_i < WIN_LAT:
                far[row, (from_i % WIN_LAT - (0 if direction > 0 else HALF_LAT)) * cols + j] = 1
            elif not 0 <= from_j < cols:
                side[row, from_i * HALF_LON + (from_j - cols if direction > 0 else from_j + HALF_LON)] = 1
            else:
                own[row, from_i * cols + from_j] = 1
    return own, side, far


def edge_matrix(cols, direction):
    edge = np.zeros((WIN_LAT, HALF_LON, WIN_LAT * cols), np.float32)
    for i in range(WIN_LAT):
        for j in range(HALF_LON):
            edge[i, j, i * cols + (j if direction > 0 else cols - HALF_LON + j)] = 1
    return edge.reshape(-1, WIN_LAT * cols)


def fixed(matrix):
    return jnp.asarray(matrix, BF16)


def norm_stats(values):
    row_mean = jnp.sum(values, axis=-1, keepdims=True) * (1.0 / D)
    centred = values - row_mean
    row_var = jnp.sum(centred * centred, axis=-1, keepdims=True) * (1.0 / D)
    inv_std = lax.rsqrt(row_var + NORM_EPS)
    return centred * inv_std, inv_std


def norm_back(d_float, unit_rows, inv_std, gain_row):
    d_unit = d_float * gain_row
    mean_grad = jnp.sum(d_unit, axis=-1, keepdims=True) * (1.0 / D)
    mean_proj = jnp.sum(d_unit * unit_rows, axis=-1, keepdims=True) * (1.0 / D)
    d_input = inv_std * (d_unit - mean_grad - unit_rows * mean_proj)
    return d_input, jnp.sum(d_float * unit_rows, axis=0, keepdims=True)


def masked_bias(table, reach, keep_of, split_rows):
    shifted = jnp.concatenate(
        [
            table[:, (WIN_LAT - 1 - a2) * SPAN_LON : (WIN_LAT - 1 - a2) * SPAN_LON + REACH]
            for a2 in range(WIN_LAT)
        ],
        axis=0,
    )
    high = shifted.astype(BF16)
    rest = shifted - high.astype(F32)
    middle = rest.astype(BF16)
    low = (rest - middle.astype(F32)).astype(BF16)
    spread = dot_nn(high, reach) + (dot_nn(middle, reach) + dot_nn(low, reach))
    place = lax.broadcasted_iota(jnp.int32, (HEADS, QPAD), 1)
    query_late = jnp.where(place % WIN_LAT >= HALF_LAT, 1, 0)
    tiles = []
    for a2 in range(WIN_LAT):
        key_late = 1 if a2 >= HALF_LAT else 0
        apart = jnp.where(query_late == key_late, 0, 1) * split_rows
        shut = apart + jnp.where(keep_of(a2) == 1, 0, 1)
        tiles.append(jnp.where(shut > 0, SHUT, 0.0).astype(F32))
    tile = jnp.concatenate(tiles, axis=0)
    blocks = [spread[:, QPAD * e2 : QPAD * (e2 + 1)] + tile for e2 in range(WIN_LON)]
    return jnp.concatenate(blocks, axis=0).reshape(WIN, HEADS, QPAD)


def lay_out(qkv, order, spread):
    count = order.shape[0] // QPAD
    queries = dot_nn(order, qkv[:, :INNER]).astype(BF16)
    stacked = dot_nn(spread, qkv[:, INNER:])
    head = lax.broadcasted_iota(jnp.int32, (HEADS, 2 * INNER), 0)
    lane = lax.broadcasted_iota(jnp.int32, (HEADS, 2 * INNER), 1)
    own = jnp.where((lane // HEAD_DIM) % HEADS == head, 1.0, 0.0).astype(F32)
    stacked = stacked.reshape(count * WIN, HEADS, 2 * INNER) * own[None]
    stacked = stacked.reshape(count * STACK, 2 * INNER).astype(BF16)
    return queries, stacked[:, :INNER], stacked[:, INNER:], own


def attend(queries, keys, values, bias, order_back):
    count = queries.shape[0] // QPAD
    all_probs, outs = [], []
    for w in range(count):
        rows = slice(w * STACK, (w + 1) * STACK)
        scores = dot_nt(keys[rows], queries[w * QPAD : (w + 1) * QPAD])
        scores = scores.reshape(WIN, HEADS, QPAD) * SCALE + bias
        exp_scores = jnp.exp(scores - jnp.max(scores, axis=0, keepdims=True))
        probs = exp_scores * (1.0 / jnp.sum(exp_scores, axis=0, keepdims=True))
        all_probs.append(probs)
        low = probs.reshape(STACK, QPAD).astype(BF16)
        outs.append(dot_tn(low, values[rows]).astype(BF16))
    heads = dot_nn(order_back, jnp.concatenate(outs, axis=0)).astype(BF16)
    return heads, all_probs


def attend_back(d_heads, all_probs, queries, keys, values, own, order, order_back, spread_back):
    d_out = dot_nn(order, d_heads).astype(BF16)
    d_queries, d_stack = [], []
    for w, probs in enumerate(all_probs):
        rows = slice(w * STACK, (w + 1) * STACK)
        here = slice(w * QPAD, (w + 1) * QPAD)
        d_probs = dot_nt(values[rows], d_out[here]).reshape(WIN, HEADS, QPAD)
        total = jnp.sum(d_probs * probs, axis=0, keepdims=True)
        d_low = (probs * (d_probs - total) * SCALE).reshape(STACK, QPAD).astype(BF16)
        low = probs.reshape(STACK, QPAD).astype(BF16)
        d_queries.append(dot_tn(d_low, keys[rows]).astype(BF16))
        d_keys = dot_nn(d_low, queries[here])
        d_values = dot_nn(low, d_out[here])
        both = jnp.concatenate([d_keys, d_values], axis=1).reshape(WIN, HEADS, 2 * INNER) * own[None]
        d_stack.append(both.reshape(STACK, 2 * INNER).astype(BF16))
    d_query_grid = dot_nn(order_back, jnp.concatenate(d_queries, axis=0)).astype(BF16)
    d_rest = dot_nn(spread_back, jnp.concatenate(d_stack, axis=0)).astype(BF16)
    return jnp.concatenate([d_query_grid, d_rest], axis=1)


def first_kernel(
    row_ref, keep_ref, tokens_ref, mask_ref, embed_ref, gains_ref, w_qkv_ref, w_proj_ref, table_ref, cot_ref,
    order_ref, order_back_ref, spread_ref, reach_ref, edge_ref,
    wide_ref, saved_ref, probs_ref, rolling_ref, strip_ref,
):
    rows, cols = mask_ref.shape
    mask = mask_ref[...].astype(F32)
    spread_mask = jnp.concatenate([jnp.broadcast_to(mask[r : r + 1], (cols, cols)) for r in range(rows)], axis=0)
    cell = lax.broadcasted_iota(jnp.int32, (rows * cols, cols), 0)
    lane = lax.broadcasted_iota(jnp.int32, (rows * cols, cols), 1)
    land = jnp.sum(jnp.where(cell % cols == lane, spread_mask, 0.0), axis=1, keepdims=True)
    embedded = tokens_ref[...].astype(F32) + jnp.where(land == 1.0, embed_ref[1:2], embed_ref[0:1])
    wide_ref[:, :D] = embedded
    unit_one, _ = norm_stats(embedded)
    normed_one = (unit_one * gains_ref[0:1]).astype(BF16)
    qkv = dot_nn(normed_one, w_qkv_ref[0]).astype(BF16)
    saved_ref[:, : 3 * INNER] = qkv
    bias = masked_bias(table_ref[0], reach_ref[...], lambda a2: keep_ref[row_ref[0] + a2], 0)
    queries, keys, values, own = lay_out(qkv, order_ref[...], spread_ref[...])
    heads, all_probs = attend(queries, keys, values, bias, order_back_ref[...])
    for w, probs in enumerate(all_probs):
        probs_ref[w] = probs
    saved_ref[:, 3 * INNER :] = heads
    branch = dot_nn(heads, w_proj_ref[0]).astype(BF16)
    stream = embedded + branch.astype(F32)
    wide_ref[:, D:] = stream
    unit_two, _ = norm_stats(stream)
    normed_two = (unit_two * gains_ref[1:2]).astype(BF16)
    d_heads_two = dot_nt(cot_ref[...], w_proj_ref[1]).astype(BF16)
    rolling = jnp.concatenate([normed_two, d_heads_two], axis=1)
    rolling_ref[...] = rolling
    strip_ref[...] = dot_nn(edge_ref[...], rolling).astype(BF16)


def second_kernel(
    row_ref, keep_ref, rolling_ref, landed_ref, arrived_ref, w_qkv_ref, table_ref,
    order_ref, order_back_ref, spread_ref, spread_back_ref, reach_ref, own_ref, side_ref, far_ref, edge_ref,
    back_ref, strip_ref,
):
    lat_count = keep_ref.shape[0]
    rolled = (
        dot_nn(own_ref[...], rolling_ref[...])
        + dot_nn(side_ref[...], landed_ref[...])
        + dot_nn(far_ref[...], arrived_ref[...])
    ).astype(BF16)
    normed, d_heads = rolled[:, :D], rolled[:, D:]
    last_band = jnp.where(row_ref[0] + WIN_LAT >= lat_count, 1, 0)

    def keep_of(a2):
        place = row_ref[0] + (a2 + HALF_LAT)
        return keep_ref[jnp.where(place >= lat_count, place - lat_count, place)]

    bias = masked_bias(table_ref[0], reach_ref[...], keep_of, last_band)
    order, order_back = order_ref[...], order_back_ref[...]
    qkv = dot_nn(normed, w_qkv_ref[0]).astype(BF16)
    queries, keys, values, own = lay_out(qkv, order, spread_ref[...])
    heads, all_probs = attend(queries, keys, values, bias, order_back)
    d_qkv = attend_back(d_heads, all_probs, queries, keys, values, own, order, order_back, spread_back_ref[...])
    d_normed = dot_nt(d_qkv, w_qkv_ref[0]).astype(BF16)
    both = jnp.concatenate([d_normed, heads], axis=1)
    back_ref[...] = both
    strip_ref[...] = dot_nn(edge_ref[...], both).astype(BF16)


def third_kernel(
    core_ref, wide_ref, saved_ref, probs_ref, cot_ref, back_ref, landed_ref, arrived_ref, gains_ref, w_qkv_ref, w_proj_ref,
    order_ref, order_back_ref, spread_ref, spread_back_ref, own_ref, side_ref, far_ref,
    output_ref, grad_ref, kept_ref, sent_ref,
):
    unrolled = (
        dot_nn(own_ref[...], back_ref[...])
        + dot_nn(side_ref[...], landed_ref[...])
        + dot_nn(far_ref[...], arrived_ref[...])
    )
    stream = wide_ref[:, D:]
    unit_two, inv_two = norm_stats(stream)
    d_branch, gain_two = norm_back(unrolled[:, :D], unit_two, inv_two, gains_ref[1:2])
    cotangent = cot_ref[...]
    d_stream = (cotangent.astype(F32) + d_branch).astype(BF16)
    qkv, heads_one = saved_ref[:, : 3 * INNER], saved_ref[:, 3 * INNER :]
    heads_two = unrolled[:, D:].astype(BF16)
    branch_two = dot_nn(heads_two, w_proj_ref[1]).astype(BF16)
    output_ref[...] = stream + branch_two.astype(F32)
    proj_one = dot_tn(heads_one, d_stream)
    proj_two = dot_tn(heads_two, cotangent)
    upper = core_ref[0] == 1
    kept_ref[:INNER] = jnp.where(upper, proj_two, proj_one).astype(BF16)
    sent_ref[:INNER] = jnp.where(upper, proj_one, proj_two).astype(BF16)
    d_heads = dot_nt(d_stream, w_proj_ref[0]).astype(BF16)
    order = order_ref[...]
    queries, keys, values, own = lay_out(qkv, order, spread_ref[...])
    all_probs = [probs_ref[w] for w in range(probs_ref.shape[0])]
    d_qkv = attend_back(
        d_heads, all_probs, queries, keys, values, own, order, order_back_ref[...], spread_back_ref[...]
    )
    d_normed = dot_nt(d_qkv, w_qkv_ref[0]).astype(BF16)
    unit_one, inv_one = norm_stats(wide_ref[:, :D])
    d_branch, gain_one = norm_back(d_normed.astype(F32), unit_one, inv_one, gains_ref[0:1])
    grad_ref[...] = (d_stream.astype(F32) + d_branch).astype(BF16)
    gain = jnp.concatenate(
        [row[:, 128 * j : 128 * (j + 1)] for row in (gain_one, gain_two) for j in range(D // 128)], axis=0
    )
    pair = jnp.concatenate([gain_pair(gain), jnp.zeros((2 * GAIN_ROWS, D - 128), BF16)], axis=1)
    kept_ref[INNER:] = pair
    sent_ref[INNER:] = pair


def gain_pair(gain):
    high = gain.astype(BF16).astype(F32)
    return jnp.concatenate([high, gain - high], axis=0).astype(BF16)


def pair_sum(pair):
    return pair[:GAIN_ROWS] + pair[GAIN_ROWS : 2 * GAIN_ROWS]


def core_sum_kernel(kept_ref, landed_ref, out_ref):
    total = kept_ref[...].astype(F32) + landed_ref[...].astype(F32)
    low = total[:INNER].astype(BF16)
    pair = gain_pair(pair_sum(total[INNER:, :128]))
    pieces, tall = out_ref.shape[0], out_ref.shape[1]
    for s in range(pieces):
        row, col = tall * (s // 2), D // 2 * (s % 2)
        out_ref[s, :, : D // 2] = low[row : row + tall, col : col + D // 2]
        out_ref[s, : 2 * GAIN_ROWS, D // 2 :] = pair
        if tall > 2 * GAIN_ROWS:
            out_ref[s, 2 * GAIN_ROWS :, D // 2 :] = jnp.zeros((tall - 2 * GAIN_ROWS, 128), BF16)


def added(parts_ref):
    total = parts_ref[0].astype(F32)
    for s in range(1, parts_ref.shape[0]):
        total = total + parts_ref[s].astype(F32)
    return total[:, : D // 2], pair_sum(total[:, D // 2 :])


def plane_sum_kernel(parts_ref, out_ref):
    proj, gain = added(parts_ref)
    low, pair = proj.astype(BF16), gain_pair(gain)
    tall = out_ref.shape[1]
    for s in range(out_ref.shape[0]):
        out_ref[s, :, : D // 2] = low
        out_ref[s, : 2 * GAIN_ROWS, D // 2 :] = pair
        if tall > 2 * GAIN_ROWS:
            out_ref[s, 2 * GAIN_ROWS :, D // 2 :] = jnp.zeros((tall - 2 * GAIN_ROWS, 128), BF16)


def depth_sum_kernel(scale, parts_ref, proj_ref, gains_ref):
    proj, gain = added(parts_ref)
    low = (proj * scale).astype(BF16)
    for s in range(proj_ref.shape[0]):
        proj_ref[s] = low
    gain = gain * scale
    per_row = D // 128
    for r in range(GAIN_ROWS):
        gains_ref[r // per_row : r // per_row + 1, 128 * (r % per_row) : 128 * (r % per_row + 1)] = gain[r : r + 1]


def join_kernel(core_ref, mine_ref, other_ref, out_ref):
    pieces, tall = mine_ref.shape[0], mine_ref.shape[1]
    upper = core_ref[0] == 1
    for s in range(pieces):
        row, col = tall * (s // 2), D // 2 * (s % 2)
        mine, other = mine_ref[s], other_ref[s]
        out_ref[0, row : row + tall, col : col + D // 2] = jnp.where(upper, other, mine)
        out_ref[1, row : row + tall, col : col + D // 2] = jnp.where(upper, mine, other)


def scalars(array):
    return array, pl.BlockSpec(memory_space=pltpu.SMEM)


def whole(array):
    return array, pl.BlockSpec(array.shape, functools.partial(lambda n, i: (0,) * n, array.ndim))


def in_hbm(array):
    return whole(pltpu.with_memory_space_constraint(array, pltpu.HBM))


def layer(array, index):
    spec = pl.BlockSpec((1,) + array.shape[1:], lambda i: (index,) + (0,) * (array.ndim - 1))
    return pltpu.with_memory_space_constraint(array, pltpu.HBM), spec


def hbm(*dims, dtype=BF16):
    return pltpu.HBM(dims, dtype)


def either(*dims, dtype=BF16):
    return jax.ShapeDtypeStruct(dims, dtype)


def call(kernel, outs, operands):
    arrays, specs = zip(*operands)
    out_specs = [pl.BlockSpec(o.shape, functools.partial(lambda n, i: (0,) * n, len(o.shape))) for o in outs]
    return pl.pallas_call(
        kernel,
        grid=(1,),
        in_specs=specs,
        out_specs=out_specs,
        out_shape=outs,
        compiler_params=pltpu.CompilerParams(vmem_limit_bytes=50 * 1024 * 1024),
    )(*arrays)


LON = ("z_lo", "x", "core")
LAT = ("z_hi", "y")
PLANE = ("x", "y")
DEPTH = ("z_lo", "z_hi")


def passed_along(array, axes, by):
    length = lax.axis_size(axes)
    return lax.ppermute(array, axes, [(i, (i + by) % length) for i in range(length)])


def local(tokens, land_mask, keep_rows, land_embed, norm_gains, w_qkv, w_proj, rel_bias, cotangent):
    rows, cols = tokens.shape[0], tokens.shape[1]
    cells, count = rows * cols, cols // WIN_LON
    half, wide = rows * HALF_LON, D + INNER
    scale_out = float(rows * lax.axis_size(LAT) * cols * lax.axis_size(LON)) ** (-0.5)
    row_first = scalars((lax.axis_index(LAT) * rows).astype(jnp.int32).reshape(1))
    core = scalars(lax.axis_index("core").astype(jnp.int32).reshape(1))
    keep_in = scalars(keep_rows)
    order, spread = window_matrices(cols)
    order, order_back, spread, spread_back = (in_hbm(fixed(m)) for m in (order, order.T, spread, spread.T))
    reach = in_hbm(fixed(reach_matrix()))
    cot_flat = in_hbm(cotangent.reshape(cells, D))

    wide_one, saved, probs, rolling, strip = call(
        first_kernel,
        [
            hbm(cells, 2 * D, dtype=F32), hbm(cells, 4 * INNER), hbm(count, WIN, HEADS, QPAD, dtype=F32),
            either(cells, wide), either(half, wide),
        ],
        [
            row_first, keep_in, in_hbm(tokens.reshape(cells, D)), in_hbm(land_mask), in_hbm(land_embed),
            in_hbm(norm_gains), layer(w_qkv, 0), in_hbm(w_proj), layer(rel_bias, 0), cot_flat,
            order, order_back, spread, reach, in_hbm(fixed(edge_matrix(cols, 1))),
        ],
    )

    landed = passed_along(strip, LON, -1)
    own_edge = rolling.reshape(rows, cols, wide)[:HALF_LAT, HALF_LON:]
    edge_rows = jnp.concatenate([own_edge, landed.reshape(rows, HALF_LON, wide)[:HALF_LAT]], axis=1)
    arrived = passed_along(edge_rows, LAT, -1).reshape(HALF_LAT * cols, wide)

    back, strip = call(
        second_kernel,
        [either(cells, wide), either(half, wide)],
        [
            row_first, keep_in, whole(rolling), whole(landed), whole(arrived), layer(w_qkv, 1), layer(rel_bias, 1),
            order, order_back, spread, spread_back, reach, *(in_hbm(fixed(m)) for m in roll_matrices(cols, 1)),
            in_hbm(fixed(edge_matrix(cols, -1))),
        ],
    )

    landed = passed_along(strip, LON, 1)
    own_edge = back.reshape(rows, cols, wide)[HALF_LAT:, : cols - HALF_LON]
    edge_rows = jnp.concatenate([landed.reshape(rows, HALF_LON, wide)[HALF_LAT:], own_edge], axis=1)
    arrived = passed_along(edge_rows, LAT, 1).reshape(HALF_LAT * cols, wide)

    output, grad_tokens, kept, sent = call(
        third_kernel,
        [hbm(cells, D, dtype=F32), hbm(cells, D), either(INNER + 2 * GAIN_ROWS, D), either(INNER + 2 * GAIN_ROWS, D)],
        [
            core, in_hbm(wide_one), in_hbm(saved), in_hbm(probs), cot_flat, whole(back), whole(landed), whole(arrived),
            in_hbm(norm_gains), layer(w_qkv, 0), in_hbm(w_proj), order, order_back, spread, spread_back,
            *(in_hbm(fixed(m)) for m in roll_matrices(cols, -1)),
        ],
    )

    planes, depths, cores = lax.axis_size(PLANE), lax.axis_size(DEPTH), lax.axis_size("core")
    tall = 2 * INNER // planes
    swap = [(i, (i + 1) % cores) for i in range(cores)]
    landed = lax.ppermute(sent, "core", swap)
    (pieces,) = call(core_sum_kernel, [either(planes, tall, D // 2 + 128)], [whole(kept), whole(landed)])
    parts = lax.all_to_all(pieces, PLANE, 0, 0, tiled=True)
    (pieces,) = call(plane_sum_kernel, [either(depths, tall, D // 2 + 128)], [whole(parts)])
    parts = lax.all_to_all(pieces, DEPTH, 0, 0, tiled=True)
    pieces, grad_gains = call(
        functools.partial(depth_sum_kernel, scale_out),
        [either(planes, tall, D // 2), either(2, D, dtype=F32)],
        [whole(parts)],
    )
    mine = lax.all_to_all(pieces, PLANE, 0, 0, tiled=True)
    other = lax.ppermute(mine, "core", swap)
    (grad_proj,) = call(join_kernel, [either(2, INNER, D)], [core, whole(mine), whole(other)])
    return output.reshape(rows, cols, D), grad_tokens.reshape(rows, cols, D), grad_proj, grad_gains


def chip_axes(lon, lat):
    x = min(4, lon // 2)
    y = min(8, lat)
    return (lon // (2 * x), x, 2, lat // y, y)


def solution(mesh):
    sizes = chip_axes(mesh.shape["lon"], mesh.shape["lat"])
    fine = Mesh(mesh.devices.reshape(sizes), LON + LAT)
    grid = P(LAT, LON, None)
    in_specs = (grid, P(LAT, LON), P(), P(), P(), P(), P(), P(), grid)
    out_specs = (grid, grid, P(), P())
    return jax.shard_map(local, mesh=fine, in_specs=in_specs, out_specs=out_specs, check_vma=False)
```

```python
import functools

import jax
import jax.numpy as jnp
import numpy as np
from jax import lax
from jax.experimental import pallas as pl
from jax.experimental.pallas import tpu as pltpu
from jax.sharding import Mesh
from jax.sharding import PartitionSpec as P

D = 512
HEAD_DIM = 32
HEADS = 8
INNER = HEADS * HEAD_DIM
WIN_LAT = 6
WIN_LON = 12
HALF_LAT = WIN_LAT // 2
HALF_LON = WIN_LON // 2
WIN = WIN_LAT * WIN_LON
SPAN_LON = 2 * WIN_LON - 1
REACH = WIN_LAT * SPAN_LON
PLACES = 80
SIDE = 48
GROUP = 4
GROUPS = HEADS // GROUP
SHEET = GROUP * HEAD_DIM
TILES = WIN * GROUP // 8
LOG2E = 1.4426950408889634
STACK = WIN * GROUP
GAIN_ROWS = 8

NORM_EPS = 1e-05
SCALE = HEAD_DIM ** (-0.5)
SHUT = -1e30

F32 = jnp.float32
BF16 = jnp.bfloat16


def dot_nn(left, right):
    return lax.dot_general(left, right, (((1,), (0,)), ((), ())), preferred_element_type=F32)


def dot_nt(left, right):
    return lax.dot_general(left, right, (((1,), (1,)), ((), ())), preferred_element_type=F32)


def dot_tn(left, right):
    return lax.dot_general(left, right, (((0,), (0,)), ((), ())), preferred_element_type=F32)


def spread_matrix():
    spread = np.zeros((WIN, GROUP, PLACES), np.float32)
    for key in range(WIN):
        spread[key, :, key] = 1
    return spread.reshape(STACK, PLACES)


def reach_matrix():
    reach = np.zeros((REACH, WIN_LON, 128), np.float32)
    for e2 in range(WIN_LON):
        for a in range(WIN_LAT):
            for e in range(WIN_LON):
                reach[a * SPAN_LON + e - e2 + WIN_LON - 1, e2, e * WIN_LAT + a] = 1
    return reach.reshape(REACH, -1)


def own_windows(cols):
    order = np.zeros((cols // WIN_LON, PLACES, WIN_LAT * cols), np.float32)
    for w in range(cols // WIN_LON):
        for a in range(WIN_LAT):
            for e in range(WIN_LON):
                order[w, e * WIN_LAT + a, a * cols + w * WIN_LON + e] = 1
    return order.reshape(-1, WIN_LAT * cols)


def side_rows(cols, first):
    strip = np.zeros((SIDE, WIN_LAT * cols), np.float32)
    for i in range(WIN_LAT):
        for j in range(HALF_LON):
            strip[side_place(i, j), i * cols + first + j] = 1
    return strip


def side_place(i, j):
    return i // HALF_LAT * (SIDE // 2) + i % HALF_LAT * HALF_LON + j


def band_rows(cols):
    return -(-HALF_LAT * cols // 16) * 16


def near_place(i, j, cols):
    cells, band = WIN_LAT * cols, band_rows(cols)
    strip = band + SIDE
    left, own, right, below = strip, strip + SIDE, strip + SIDE + cells, strip + 2 * SIDE + cells
    inside = 0 <= j < cols
    corner = (j + HALF_LON) if j < 0 else (SIDE // 2 + j - cols)
    if i < 0:
        return (i + WIN_LAT) * cols + j - (cells - band) if inside else band + (i + HALF_LAT) * HALF_LON + corner
    if i >= WIN_LAT:
        row = i - WIN_LAT
        return below + (row * cols + j if inside else band + row * HALF_LON + corner)
    if inside:
        return own + i * cols + j
    return left + side_place(i, j + HALF_LON) if j < 0 else right + side_place(i, j - cols)


def near_windows(cols):
    cells, across = WIN_LAT * cols, cols // WIN_LON + 1
    near = 2 * (band_rows(cols) + 2 * SIDE) + cells
    order = np.zeros((2, across, PLACES, near), np.float32)
    back = np.zeros((cells, 2, across, PLACES), np.float32)
    for u in range(2):
        for v in range(across):
            for a in range(WIN_LAT):
                for e in range(WIN_LON):
                    i, j = u * WIN_LAT + a - HALF_LAT, v * WIN_LON + e - HALF_LON
                    place = e * WIN_LAT + a
                    order[u, v, place, near_place(i, j, cols)] = 1
                    if 0 <= i < WIN_LAT and 0 <= j < cols:
                        back[i * cols + j, u, v, place] = 1
    return order.reshape(-1, near), back.reshape(cells, -1)


def fixed(matrix):
    return jnp.asarray(matrix, BF16)


def norm_stats(values):
    row_mean = jnp.sum(values, axis=-1, keepdims=True) * (1.0 / D)
    centred = values - row_mean
    row_var = jnp.sum(centred * centred, axis=-1, keepdims=True) * (1.0 / D)
    inv_std = lax.rsqrt(row_var + NORM_EPS)
    return centred * inv_std, inv_std


def norm_back(d_float, unit_rows, inv_std, gain_row):
    d_unit = d_float * gain_row
    mean_grad = jnp.sum(d_unit, axis=-1, keepdims=True) * (1.0 / D)
    mean_proj = jnp.sum(d_unit * unit_rows, axis=-1, keepdims=True) * (1.0 / D)
    d_input = inv_std * (d_unit - mean_grad - unit_rows * mean_proj)
    return d_input, jnp.sum(d_float * unit_rows, axis=0, keepdims=True)


def position_bias(table, reach):
    table = table * LOG2E
    shifted = jnp.concatenate(
        [
            table[g * GROUP : (g + 1) * GROUP, (WIN_LAT - 1 - a2) * SPAN_LON : (WIN_LAT - 1 - a2) * SPAN_LON + REACH]
            for g in range(GROUPS)
            for a2 in range(WIN_LAT)
        ],
        axis=0,
    )
    high = shifted.astype(BF16)
    rest = shifted - high.astype(F32)
    middle = rest.astype(BF16)
    low = (rest - middle.astype(F32)).astype(BF16)
    spread = dot_nn(high, reach) + (dot_nn(middle, reach) + dot_nn(low, reach))
    return [spread[:, 128 * e2 : 128 * e2 + PLACES] for e2 in range(WIN_LON)]


def masked(blocks, keep_of, split_rows):
    rows = WIN_LAT * GROUP
    place = lax.broadcasted_iota(jnp.int32, (rows, PLACES), 1)
    key_row = lax.broadcasted_iota(jnp.int32, (rows, PLACES), 0) // GROUP
    query_late = jnp.where(place % WIN_LAT >= HALF_LAT, 1, 0)
    key_late = jnp.where(key_row >= HALF_LAT, 1, 0)
    shut = jnp.where(query_late == key_late, 0, 1) * split_rows
    for a2 in range(WIN_LAT):
        shut = shut + jnp.where(key_row == a2, 1, 0) * jnp.where(keep_of(a2) == 1, 0, 1)
    tile = jnp.where(shut > 0, SHUT, 0.0).astype(F32)
    return [
        jnp.concatenate([block[g * rows : (g + 1) * rows] + tile for block in blocks], axis=0).reshape(TILES, 8, PLACES)
        for g in range(GROUPS)
    ]


def own_head():
    head = lax.broadcasted_iota(jnp.int32, (8, 2 * INNER), 0) % GROUP
    lane = lax.broadcasted_iota(jnp.int32, (8, 2 * INNER), 1)
    return jnp.where((lane // HEAD_DIM) % GROUP == head, 1.0, 0.0).astype(F32)[None]


def sheet(array, g):
    return array[:, g * SHEET : (g + 1) * SHEET]


def own_parts(stacked, own):
    return (stacked.reshape(TILES, 8, 2 * INNER) * own).reshape(STACK, 2 * INNER).astype(BF16)


def stack_up(key_values, spread, own):
    stacks = [own_parts(stacked, own) for stacked in [dot_nn(spread, each) for each in key_values]]
    return [(stack[:, :INNER], stack[:, INNER:]) for stack in stacks]


def over_keys(combine, tiles):
    return combine(tiles, jnp.concatenate([tiles[GROUP:], tiles[:GROUP]], axis=0))


def attend(queries, stacks, biases):
    both = [(w, g) for w in range(len(queries)) for g in range(GROUPS)]
    scores = [dot_nt(sheet(stacks[w][0], g), sheet(queries[w], g)) for w, g in both]
    scores = [
        one.reshape(TILES, 8, PLACES) * (SCALE * LOG2E) + biases[w][g] for one, (w, g) in zip(scores, both)
    ]
    tops = [over_keys(jnp.maximum, jnp.max(one, axis=0)) for one in scores]
    exps = [jnp.exp2(one - top) for one, top in zip(scores, tops)]
    shares = [1.0 / over_keys(jnp.add, jnp.sum(one, axis=0)) for one in exps]
    probs = [one * share for one, share in zip(exps, shares)]
    lows = [one.reshape(STACK, PLACES).astype(BF16) for one in probs]
    outs = [dot_tn(low, sheet(stacks[w][1], g)).astype(BF16) for low, (w, g) in zip(lows, both)]
    per_window = [slice(w * GROUPS, (w + 1) * GROUPS) for w in range(len(queries))]
    return [probs[here] for here in per_window], [jnp.concatenate(outs[here], axis=1) for here in per_window]


def attend_back(d_outs, probs, queries, stacks, spread_back, own):
    both = [(w, g) for w in range(len(queries)) for g in range(GROUPS)]
    d_probs = [dot_nt(sheet(stacks[w][1], g), sheet(d_outs[w], g)) for w, g in both]
    d_probs = [one.reshape(TILES, 8, PLACES) for one in d_probs]
    totals = [over_keys(jnp.add, jnp.sum(one * probs[w][g], axis=0)) for one, (w, g) in zip(d_probs, both)]
    d_lows = [
        (probs[w][g] * (one - total) * SCALE).reshape(STACK, PLACES).astype(BF16)
        for one, total, (w, g) in zip(d_probs, totals, both)
    ]
    lows = [probs[w][g].reshape(STACK, PLACES).astype(BF16) for w, g in both]
    d_values = [dot_nn(low, sheet(d_outs[w], g)) for low, (w, g) in zip(lows, both)]
    d_keys = [dot_nn(d_low, sheet(queries[w], g)) for d_low, (w, g) in zip(d_lows, both)]
    d_queries = [dot_tn(d_low, sheet(stacks[w][0], g)).astype(BF16) for d_low, (w, g) in zip(d_lows, both)]
    per_window = [slice(w * GROUPS, (w + 1) * GROUPS) for w in range(len(queries))]
    d_stacks = [own_parts(jnp.concatenate(d_keys[here] + d_values[here], axis=1), own) for here in per_window]
    d_rest = [dot_nn(spread_back, d_stack).astype(BF16) for d_stack in d_stacks]
    return [jnp.concatenate(d_queries[here] + [rest], axis=1) for here, rest in zip(per_window, d_rest)]


def window_rows(array, w):
    return array[w * PLACES : (w + 1) * PLACES]


def first_kernel(
    row_ref, keep_ref, tokens_ref, mask_ref, embed_ref, gains_ref, w_qkv_ref, w_proj_ref, table_ref, cot_ref,
    order_ref, order_back_ref, spread_ref, reach_ref, left_ref, right_ref,
    wide_ref, qkv_ref, heads_ref, probs_ref, rolling_ref, to_left_ref, to_right_ref,
):
    rows, cols = mask_ref.shape
    mask = mask_ref[...].astype(F32)
    spread_mask = jnp.concatenate([jnp.broadcast_to(mask[r : r + 1], (cols, cols)) for r in range(rows)], axis=0)
    cell = lax.broadcasted_iota(jnp.int32, (rows * cols, cols), 0)
    lane = lax.broadcasted_iota(jnp.int32, (rows * cols, cols), 1)
    land = jnp.sum(jnp.where(cell % cols == lane, spread_mask, 0.0), axis=1, keepdims=True)
    embedded = tokens_ref[...].astype(F32) + jnp.where(land == 1.0, embed_ref[1:2], embed_ref[0:1])
    wide_ref[:, :D] = embedded
    unit_one, _ = norm_stats(embedded)
    normed_one = (unit_one * gains_ref[0:1]).astype(BF16)
    ordered = dot_nn(order_ref[...], normed_one).astype(BF16)
    qkv = dot_nn(ordered, w_qkv_ref[0]).astype(BF16)
    qkv_ref[...] = qkv
    bias = masked(position_bias(table_ref[0], reach_ref[...]), lambda a2: keep_ref[row_ref[0] + a2], 0)
    spread, own = spread_ref[...], own_head()
    windows = [window_rows(qkv, w) for w in range(cols // WIN_LON)]
    stacks = stack_up([here[:, INNER:] for here in windows], spread, own)
    all_probs, outs = attend([here[:, :INNER] for here in windows], stacks, [bias] * len(windows))
    for w, probs in enumerate(all_probs):
        for g in range(GROUPS):
            probs_ref[w, g] = probs[g]
    heads = dot_nn(order_back_ref[...], jnp.concatenate(outs, axis=0)).astype(BF16)
    heads_ref[...] = heads
    branch = dot_nn(heads, w_proj_ref[0]).astype(BF16)
    stream = embedded + branch.astype(F32)
    wide_ref[:, D:] = stream
    unit_two, _ = norm_stats(stream)
    normed_two = (unit_two * gains_ref[1:2]).astype(BF16)
    d_heads_two = dot_nt(cot_ref[...], w_proj_ref[1]).astype(BF16)
    rolling = jnp.concatenate([normed_two, d_heads_two], axis=1)
    rolling_ref[...] = rolling
    to_left_ref[...] = dot_nn(left_ref[...], rolling).astype(BF16)
    to_right_ref[...] = dot_nn(right_ref[...], rolling).astype(BF16)


def second_kernel(
    core_ref, row_ref, keep_ref, above_ref, left_ref, rolling_ref, right_ref, below_ref,
    wide_ref, qkv_ref, heads_ref, probs_ref, cot_ref, gains_ref, w_qkv_ref, w_proj_ref, table_ref,
    order_ref, order_back_ref, near_order_ref, near_back_ref, spread_ref, spread_back_ref, reach_ref,
    output_ref, grad_ref, kept_ref, sent_ref,
):
    lat_count = keep_ref.shape[0]
    row_first = row_ref[0]
    spread, spread_back, own = spread_ref[...], spread_back_ref[...], own_head()
    near = jnp.concatenate(
        [above_ref[...], left_ref[...], rolling_ref[...], right_ref[...], below_ref[...]], axis=0
    )
    ordered = dot_nn(near_order_ref[...], near).astype(BF16)
    qkv_two = dot_nn(ordered[:, :D], w_qkv_ref[1]).astype(BF16)
    blocks = position_bias(table_ref[0], reach_ref[...])
    across = near_order_ref.shape[0] // PLACES // 2
    biases = []
    for u in range(2):

        def keep_of(a2, u=u):
            place = row_first + (u * WIN_LAT - HALF_LAT + a2)
            place = jnp.where(place < 0, place + lat_count, place)
            return keep_ref[jnp.where(place >= lat_count, place - lat_count, place)]

        last_band = jnp.where((row_first + u * WIN_LAT) % lat_count == 0, 1, 0)
        biases += [masked(blocks, keep_of, last_band)] * across
    windows = [window_rows(qkv_two, w) for w in range(2 * across)]
    d_outs = [window_rows(ordered, w)[:, D:] for w in range(2 * across)]
    queries = [here[:, :INNER] for here in windows]
    stacks = stack_up([here[:, INNER:] for here in windows], spread, own)
    all_probs, outs = attend(queries, stacks, biases)
    d_windows = attend_back(d_outs, all_probs, queries, stacks, spread_back, own)
    rows_two = jnp.concatenate([jnp.concatenate(d_windows, axis=0), jnp.concatenate(outs, axis=0)], axis=1)
    unrolled = dot_nn(near_back_ref[...], rows_two).astype(BF16)
    heads_two = unrolled[:, 3 * INNER :]
    d_normed_two = dot_nt(unrolled[:, : 3 * INNER], w_qkv_ref[1]).astype(BF16)

    stream = wide_ref[:, D:]
    unit_two, inv_two = norm_stats(stream)
    d_branch, gain_two = norm_back(d_normed_two.astype(F32), unit_two, inv_two, gains_ref[1:2])
    cotangent = cot_ref[...]
    d_stream = (cotangent.astype(F32) + d_branch).astype(BF16)
    branch_two = dot_nn(heads_two, w_proj_ref[1]).astype(BF16)
    output_ref[...] = stream + branch_two.astype(F32)
    proj_one = dot_tn(heads_ref[...], d_stream)
    proj_two = dot_tn(heads_two, cotangent)
    upper = core_ref[0] == 1
    kept_ref[:INNER] = jnp.where(upper, proj_two, proj_one).astype(BF16)
    sent_ref[:INNER] = jnp.where(upper, proj_one, proj_two).astype(BF16)

    d_heads = dot_nt(d_stream, w_proj_ref[0]).astype(BF16)
    d_outs = dot_nn(order_ref[...], d_heads).astype(BF16)
    qkv_one = qkv_ref[...]
    windows = [window_rows(qkv_one, w) for w in range(probs_ref.shape[0])]
    d_outs = [window_rows(d_outs, w) for w in range(probs_ref.shape[0])]
    stacks = stack_up([here[:, INNER:] for here in windows], spread, own)
    all_probs = [[probs_ref[w, g] for g in range(GROUPS)] for w in range(probs_ref.shape[0])]
    d_windows = attend_back(d_outs, all_probs, [here[:, :INNER] for here in windows], stacks, spread_back, own)
    d_qkv = dot_nn(order_back_ref[...], jnp.concatenate(d_windows, axis=0)).astype(BF16)
    d_normed = dot_nt(d_qkv, w_qkv_ref[0]).astype(BF16)
    unit_one, inv_one = norm_stats(wide_ref[:, :D])
    d_branch, gain_one = norm_back(d_normed.astype(F32), unit_one, inv_one, gains_ref[0:1])
    grad_ref[...] = (d_stream.astype(F32) + d_branch).astype(BF16)
    gain = jnp.concatenate(
        [row[:, 128 * j : 128 * (j + 1)] for row in (gain_one, gain_two) for j in range(D // 128)], axis=0
    )
    pair = jnp.concatenate([gain_pair(gain), jnp.zeros((2 * GAIN_ROWS, D - 128), BF16)], axis=1)
    kept_ref[INNER:] = pair
    sent_ref[INNER:] = pair


def gain_pair(gain):
    high = gain.astype(BF16).astype(F32)
    return jnp.concatenate([high, gain - high], axis=0).astype(BF16)


def pair_sum(pair):
    return pair[:GAIN_ROWS] + pair[GAIN_ROWS : 2 * GAIN_ROWS]


def core_sum_kernel(kept_ref, landed_ref, out_ref):
    total = kept_ref[...].astype(F32) + landed_ref[...].astype(F32)
    low = total[:INNER].astype(BF16)
    pair = gain_pair(pair_sum(total[INNER:, :128]))
    pieces, tall = out_ref.shape[0], out_ref.shape[1]
    for s in range(pieces):
        row, col = tall * (s // 2), D // 2 * (s % 2)
        out_ref[s, :, : D // 2] = low[row : row + tall, col : col + D // 2]
        out_ref[s, : 2 * GAIN_ROWS, D // 2 :] = pair
        if tall > 2 * GAIN_ROWS:
            out_ref[s, 2 * GAIN_ROWS :, D // 2 :] = jnp.zeros((tall - 2 * GAIN_ROWS, 128), BF16)


def added(parts_ref):
    total = parts_ref[0].astype(F32)
    for s in range(1, parts_ref.shape[0]):
        total = total + parts_ref[s].astype(F32)
    return total[:, : D // 2], pair_sum(total[:, D // 2 :])


def plane_sum_kernel(parts_ref, out_ref):
    proj, gain = added(parts_ref)
    low, pair = proj.astype(BF16), gain_pair(gain)
    tall = out_ref.shape[1]
    for s in range(out_ref.shape[0]):
        out_ref[s, :, : D // 2] = low
        out_ref[s, : 2 * GAIN_ROWS, D // 2 :] = pair
        if tall > 2 * GAIN_ROWS:
            out_ref[s, 2 * GAIN_ROWS :, D // 2 :] = jnp.zeros((tall - 2 * GAIN_ROWS, 128), BF16)


def depth_sum_kernel(scale, parts_ref, proj_ref, gains_ref):
    proj, gain = added(parts_ref)
    low = (proj * scale).astype(BF16)
    for s in range(proj_ref.shape[0]):
        proj_ref[s] = low
    gain = gain * scale
    per_row = D // 128
    for r in range(GAIN_ROWS):
        gains_ref[r // per_row : r // per_row + 1, 128 * (r % per_row) : 128 * (r % per_row + 1)] = gain[r : r + 1]


def join_kernel(core_ref, mine_ref, other_ref, out_ref):
    pieces, tall = mine_ref.shape[0], mine_ref.shape[1]
    upper = core_ref[0] == 1
    for s in range(pieces):
        row, col = tall * (s // 2), D // 2 * (s % 2)
        mine, other = mine_ref[s], other_ref[s]
        out_ref[0, row : row + tall, col : col + D // 2] = jnp.where(upper, other, mine)
        out_ref[1, row : row + tall, col : col + D // 2] = jnp.where(upper, mine, other)


def scalars(array):
    return array, pl.BlockSpec(memory_space=pltpu.SMEM)


def whole(array):
    return array, pl.BlockSpec(array.shape, functools.partial(lambda n, i: (0,) * n, array.ndim))


def in_hbm(array):
    return whole(pltpu.with_memory_space_constraint(array, pltpu.HBM))


def layer(array, index):
    spec = pl.BlockSpec((1,) + array.shape[1:], lambda i: (index,) + (0,) * (array.ndim - 1))
    return pltpu.with_memory_space_constraint(array, pltpu.HBM), spec


def hbm(*dims, dtype=BF16):
    return pltpu.HBM(dims, dtype)


def either(*dims, dtype=BF16):
    return jax.ShapeDtypeStruct(dims, dtype)


def call(kernel, outs, operands):
    arrays, specs = zip(*operands)
    out_specs = [pl.BlockSpec(o.shape, functools.partial(lambda n, i: (0,) * n, len(o.shape))) for o in outs]
    return pl.pallas_call(
        kernel,
        grid=(1,),
        in_specs=specs,
        out_specs=out_specs,
        out_shape=outs,
        compiler_params=pltpu.CompilerParams(vmem_limit_bytes=50 * 1024 * 1024),
    )(*arrays)


LON = ("z_lo", "x", "core")
LAT = ("z_hi", "y")
PLANE = ("x", "y")
DEPTH = ("z_lo", "z_hi")


def passed_along(array, axes, by):
    length = lax.axis_size(axes)
    return lax.ppermute(array, axes, [(i, (i + by) % length) for i in range(length)])


def local(tokens, land_mask, keep_rows, land_embed, norm_gains, w_qkv, w_proj, rel_bias, cotangent):
    rows, cols = tokens.shape[0], tokens.shape[1]
    cells, count = rows * cols, cols // WIN_LON
    band, wide = band_rows(cols), D + INNER
    scale_out = float(rows * lax.axis_size(LAT) * cols * lax.axis_size(LON)) ** (-0.5)
    row_first = scalars((lax.axis_index(LAT) * rows).astype(jnp.int32).reshape(1))
    core = scalars(lax.axis_index("core").astype(jnp.int32).reshape(1))
    keep_in = scalars(keep_rows)
    order = own_windows(cols)
    order, order_back = in_hbm(fixed(order)), in_hbm(fixed(order.T))
    near_order, near_back = (in_hbm(fixed(m)) for m in near_windows(cols))
    spread = spread_matrix()
    spread, spread_back = in_hbm(fixed(spread)), in_hbm(fixed(spread.T))
    reach = in_hbm(fixed(reach_matrix()))
    cot_flat = in_hbm(cotangent.reshape(cells, D))

    wide_one, qkv_one, heads_one, probs_one, rolling, to_left, to_right = call(
        first_kernel,
        [
            hbm(cells, 2 * D, dtype=F32), hbm(count * PLACES, 3 * INNER), hbm(cells, INNER),
            hbm(count, GROUPS, TILES, 8, PLACES, dtype=F32), either(cells, wide), either(SIDE, wide), either(SIDE, wide),
        ],
        [
            row_first, keep_in, in_hbm(tokens.reshape(cells, D)), in_hbm(land_mask), in_hbm(land_embed),
            in_hbm(norm_gains), layer(w_qkv, 0), in_hbm(w_proj), layer(rel_bias, 0), cot_flat,
            order, order_back, spread, reach,
            in_hbm(fixed(side_rows(cols, 0))), in_hbm(fixed(side_rows(cols, cols - HALF_LON))),
        ],
    )

    right = passed_along(to_left, LON, -1)
    left = passed_along(to_right, LON, 1)
    to_above = jnp.concatenate([rolling[:band], left[: SIDE // 2], right[: SIDE // 2]], axis=0)
    to_below = jnp.concatenate([rolling[cells - band :], left[SIDE // 2 :], right[SIDE // 2 :]], axis=0)
    below = passed_along(to_above, LAT, -1)
    above = passed_along(to_below, LAT, 1)

    output, grad_tokens, kept, sent = call(
        second_kernel,
        [hbm(cells, D, dtype=F32), hbm(cells, D), either(INNER + 2 * GAIN_ROWS, D), either(INNER + 2 * GAIN_ROWS, D)],
        [
            core, row_first, keep_in, whole(above), whole(left), whole(rolling), whole(right), whole(below),
            in_hbm(wide_one), in_hbm(qkv_one), in_hbm(heads_one), in_hbm(probs_one), cot_flat,
            in_hbm(norm_gains), in_hbm(w_qkv), in_hbm(w_proj), layer(rel_bias, 1),
            order, order_back, near_order, near_back, spread, spread_back, reach,
        ],
    )

    planes, depths, cores = lax.axis_size(PLANE), lax.axis_size(DEPTH), lax.axis_size("core")
    tall = 2 * INNER // planes
    swap = [(i, (i + 1) % cores) for i in range(cores)]
    landed = lax.ppermute(sent, "core", swap)
    (pieces,) = call(core_sum_kernel, [either(planes, tall, D // 2 + 128)], [whole(kept), whole(landed)])
    parts = lax.all_to_all(pieces, PLANE, 0, 0, tiled=True)
    (pieces,) = call(plane_sum_kernel, [either(depths, tall, D // 2 + 128)], [whole(parts)])
    parts = lax.all_to_all(pieces, DEPTH, 0, 0, tiled=True)
    pieces, grad_gains = call(
        functools.partial(depth_sum_kernel, scale_out),
        [either(planes, tall, D // 2), either(2, D, dtype=F32)],
        [whole(parts)],
    )
    mine = lax.all_to_all(pieces, PLANE, 0, 0, tiled=True)
    other = lax.ppermute(mine, "core", swap)
    (grad_proj,) = call(join_kernel, [either(2, INNER, D)], [core, whole(mine), whole(other)])
    return output.reshape(rows, cols, D), grad_tokens.reshape(rows, cols, D), grad_proj, grad_gains


def chip_axes(lon, lat):
    x = min(4, lon // 2)
    y = min(8, lat)
    return (lon // (2 * x), x, 2, lat // y, y)


def solution(mesh):
    sizes = chip_axes(mesh.shape["lon"], mesh.shape["lat"])
    fine = Mesh(mesh.devices.reshape(sizes), LON + LAT)
    grid = P(LAT, LON, None)
    in_specs = (grid, P(LAT, LON), P(), P(), P(), P(), P(), P(), grid)
    out_specs = (grid, grid, P(), P())
    return jax.shard_map(local, mesh=fine, in_specs=in_specs, out_specs=out_specs, check_vma=False)
```

```python
import functools

import jax
import jax.numpy as jnp
import numpy as np
from jax import lax
from jax.experimental import pallas as pl
from jax.experimental.pallas import tpu as pltpu
from jax.sharding import Mesh
from jax.sharding import PartitionSpec as P

D = 512
HEAD_DIM = 32
HEADS = 8
INNER = HEADS * HEAD_DIM
WIN_LAT = 6
WIN_LON = 12
HALF_LAT = WIN_LAT // 2
HALF_LON = WIN_LON // 2
WIN = WIN_LAT * WIN_LON
SPAN_LON = 2 * WIN_LON - 1
REACH = WIN_LAT * SPAN_LON
PLACES = 80
SIDE = 80
GROUP = 4
GROUPS = HEADS // GROUP
SHEET = GROUP * HEAD_DIM
TILES = WIN * GROUP // 8
LOG2E = 1.4426950408889634
STACK = WIN * GROUP
GAIN_ROWS = 8

NORM_EPS = 1e-05
SCALE = HEAD_DIM ** (-0.5)
SHUT = -1e30

F32 = jnp.float32
BF16 = jnp.bfloat16


def dot_nn(left, right):
    return lax.dot_general(left, right, (((1,), (0,)), ((), ())), preferred_element_type=F32)


def dot_nt(left, right):
    return lax.dot_general(left, right, (((1,), (1,)), ((), ())), preferred_element_type=F32)


def dot_tn(left, right):
    return lax.dot_general(left, right, (((0,), (0,)), ((), ())), preferred_element_type=F32)


def spread_matrix():
    spread = np.zeros((WIN, GROUP, PLACES), np.float32)
    for key in range(WIN):
        spread[key, :, key] = 1
    return spread.reshape(STACK, PLACES)


def reach_matrix():
    reach = np.zeros((REACH, WIN_LON, 128), np.float32)
    for e2 in range(WIN_LON):
        for a in range(WIN_LAT):
            for e in range(WIN_LON):
                reach[a * SPAN_LON + e - e2 + WIN_LON - 1, e2, e * WIN_LAT + a] = 1
    return reach.reshape(REACH, -1)


def own_windows(cols):
    order = np.zeros((cols // WIN_LON, PLACES, WIN_LAT * cols), np.float32)
    for w in range(cols // WIN_LON):
        for a in range(WIN_LAT):
            for e in range(WIN_LON):
                order[w, e * WIN_LAT + a, a * cols + w * WIN_LON + e] = 1
    return order.reshape(-1, WIN_LAT * cols)


def band_rows(cols):
    return -(-HALF_LAT * cols // 16) * 16


def near_place(i, j, cols):
    band = band_rows(cols)
    if 0 <= j < cols:
        return band - HALF_LAT * cols + (i + HALF_LAT) * cols + j
    first = 2 * band + WIN_LAT * cols + (0 if j < 0 else SIDE)
    return first + (i + HALF_LAT) * HALF_LON + (j + HALF_LON if j < 0 else j - cols)


def near_windows(cols):
    cells, across = WIN_LAT * cols, cols // WIN_LON + 1
    near = 2 * (band_rows(cols) + SIDE) + cells
    order = np.zeros((2, across, PLACES, near), np.float32)
    back = np.zeros((cells, 2, across, PLACES), np.float32)
    for u in range(2):
        for v in range(across):
            for a in range(WIN_LAT):
                for e in range(WIN_LON):
                    i, j = u * WIN_LAT + a - HALF_LAT, v * WIN_LON + e - HALF_LON
                    place = e * WIN_LAT + a
                    order[u, v, place, near_place(i, j, cols)] = 1
                    if 0 <= i < WIN_LAT and 0 <= j < cols:
                        back[i * cols + j, u, v, place] = 1
    return order.reshape(-1, near), back.reshape(cells, -1)


def fixed(matrix):
    return jnp.asarray(matrix, BF16)


def norm_stats(values):
    row_mean = jnp.sum(values, axis=-1, keepdims=True) * (1.0 / D)
    centred = values - row_mean
    row_var = jnp.sum(centred * centred, axis=-1, keepdims=True) * (1.0 / D)
    inv_std = lax.rsqrt(row_var + NORM_EPS)
    return centred * inv_std, inv_std


def norm_back(d_float, unit_rows, inv_std, gain_row):
    d_unit = d_float * gain_row
    mean_grad = jnp.sum(d_unit, axis=-1, keepdims=True) * (1.0 / D)
    mean_proj = jnp.sum(d_unit * unit_rows, axis=-1, keepdims=True) * (1.0 / D)
    d_input = inv_std * (d_unit - mean_grad - unit_rows * mean_proj)
    return d_input, jnp.sum(d_float * unit_rows, axis=0, keepdims=True)


def position_bias(table, reach):
    table = table * LOG2E
    shifted = jnp.concatenate(
        [
            table[g * GROUP : (g + 1) * GROUP, (WIN_LAT - 1 - a2) * SPAN_LON : (WIN_LAT - 1 - a2) * SPAN_LON + REACH]
            for g in range(GROUPS)
            for a2 in range(WIN_LAT)
        ],
        axis=0,
    )
    high = shifted.astype(BF16)
    rest = shifted - high.astype(F32)
    middle = rest.astype(BF16)
    low = (rest - middle.astype(F32)).astype(BF16)
    spread = dot_nn(high, reach) + (dot_nn(middle, reach) + dot_nn(low, reach))
    return [spread[:, 128 * e2 : 128 * e2 + PLACES] for e2 in range(WIN_LON)]


def masked(blocks, keep_of, split_rows):
    rows = WIN_LAT * GROUP
    place = lax.broadcasted_iota(jnp.int32, (rows, PLACES), 1)
    key_row = lax.broadcasted_iota(jnp.int32, (rows, PLACES), 0) // GROUP
    query_late = jnp.where(place % WIN_LAT >= HALF_LAT, 1, 0)
    key_late = jnp.where(key_row >= HALF_LAT, 1, 0)
    shut = jnp.where(query_late == key_late, 0, 1) * split_rows
    for a2 in range(WIN_LAT):
        shut = shut + jnp.where(key_row == a2, 1, 0) * jnp.where(keep_of(a2) == 1, 0, 1)
    tile = jnp.where(shut > 0, SHUT, 0.0).astype(F32)
    return [
        jnp.concatenate([block[g * rows : (g + 1) * rows] + tile for block in blocks], axis=0).reshape(TILES, 8, PLACES)
        for g in range(GROUPS)
    ]


def own_head():
    head = lax.broadcasted_iota(jnp.int32, (8, 2 * INNER), 0) % GROUP
    lane = lax.broadcasted_iota(jnp.int32, (8, 2 * INNER), 1)
    return jnp.where((lane // HEAD_DIM) % GROUP == head, 1.0, 0.0).astype(F32)[None]


def sheet(array, g):
    return array[:, g * SHEET : (g + 1) * SHEET]


def own_parts(stacked, own):
    return (stacked.reshape(TILES, 8, 2 * INNER) * own).reshape(STACK, 2 * INNER).astype(BF16)


def stack_up(key_values, spread, own):
    stacks = [own_parts(stacked, own) for stacked in [dot_nn(spread, each) for each in key_values]]
    return [(stack[:, :INNER], stack[:, INNER:]) for stack in stacks]


def over_keys(combine, tiles):
    return combine(tiles, jnp.concatenate([tiles[GROUP:], tiles[:GROUP]], axis=0))


def attend(queries, stacks, biases):
    both = [(w, g) for w in range(len(queries)) for g in range(GROUPS)]
    scores = [dot_nt(sheet(stacks[w][0], g), sheet(queries[w], g)) for w, g in both]
    scores = [
        one.reshape(TILES, 8, PLACES) * (SCALE * LOG2E) + biases[w][g] for one, (w, g) in zip(scores, both)
    ]
    tops = [over_keys(jnp.maximum, jnp.max(one, axis=0)) for one in scores]
    exps = [jnp.exp2(one - top) for one, top in zip(scores, tops)]
    shares = [1.0 / over_keys(jnp.add, jnp.sum(one, axis=0)) for one in exps]
    probs = [one * share for one, share in zip(exps, shares)]
    lows = [one.reshape(STACK, PLACES).astype(BF16) for one in probs]
    outs = [dot_tn(low, sheet(stacks[w][1], g)).astype(BF16) for low, (w, g) in zip(lows, both)]
    per_window = [slice(w * GROUPS, (w + 1) * GROUPS) for w in range(len(queries))]
    return [probs[here] for here in per_window], [jnp.concatenate(outs[here], axis=1) for here in per_window]


def attend_back(d_outs, probs, queries, stacks, spread_back, own):
    both = [(w, g) for w in range(len(queries)) for g in range(GROUPS)]
    d_probs = [dot_nt(sheet(stacks[w][1], g), sheet(d_outs[w], g)) for w, g in both]
    d_probs = [one.reshape(TILES, 8, PLACES) for one in d_probs]
    totals = [over_keys(jnp.add, jnp.sum(one * probs[w][g], axis=0)) for one, (w, g) in zip(d_probs, both)]
    d_lows = [
        (probs[w][g] * (one - total) * SCALE).reshape(STACK, PLACES).astype(BF16)
        for one, total, (w, g) in zip(d_probs, totals, both)
    ]
    lows = [probs[w][g].reshape(STACK, PLACES).astype(BF16) for w, g in both]
    d_values = [dot_nn(low, sheet(d_outs[w], g)) for low, (w, g) in zip(lows, both)]
    d_keys = [dot_nn(d_low, sheet(queries[w], g)) for d_low, (w, g) in zip(d_lows, both)]
    d_queries = [dot_tn(d_low, sheet(stacks[w][0], g)).astype(BF16) for d_low, (w, g) in zip(d_lows, both)]
    per_window = [slice(w * GROUPS, (w + 1) * GROUPS) for w in range(len(queries))]
    d_stacks = [own_parts(jnp.concatenate(d_keys[here] + d_values[here], axis=1), own) for here in per_window]
    d_rest = [dot_nn(spread_back, d_stack).astype(BF16) for d_stack in d_stacks]
    return [jnp.concatenate(d_queries[here] + [rest], axis=1) for here, rest in zip(per_window, d_rest)]


def window_rows(array, w):
    return array[w * PLACES : (w + 1) * PLACES]


def first_kernel(
    odd_ref, row_ref, keep_ref, tokens_ref, mask_ref, embed_ref, gains_ref, w_qkv_ref, w_proj_ref, table_ref, cot_ref,
    order_ref, order_back_ref, spread_ref, reach_ref,
    wide_ref, qkv_ref, heads_ref, probs_ref, rolling_ref, one_ref, two_ref,
):
    rows, cols = mask_ref.shape
    mask = mask_ref[...].astype(F32)
    spread_mask = jnp.concatenate([jnp.broadcast_to(mask[r : r + 1], (cols, cols)) for r in range(rows)], axis=0)
    cell = lax.broadcasted_iota(jnp.int32, (rows * cols, cols), 0)
    lane = lax.broadcasted_iota(jnp.int32, (rows * cols, cols), 1)
    land = jnp.sum(jnp.where(cell % cols == lane, spread_mask, 0.0), axis=1, keepdims=True)
    embedded = tokens_ref[...].astype(F32) + jnp.where(land == 1.0, embed_ref[1:2], embed_ref[0:1])
    wide_ref[:, :D] = embedded
    unit_one, _ = norm_stats(embedded)
    normed_one = (unit_one * gains_ref[0:1]).astype(BF16)
    ordered = dot_nn(order_ref[...], normed_one).astype(BF16)
    qkv = dot_nn(ordered, w_qkv_ref[0]).astype(BF16)
    qkv_ref[...] = qkv
    bias = masked(position_bias(table_ref[0], reach_ref[...]), lambda a2: keep_ref[row_ref[0] + a2], 0)
    spread, own = spread_ref[...], own_head()
    windows = [window_rows(qkv, w) for w in range(cols // WIN_LON)]
    stacks = stack_up([here[:, INNER:] for here in windows], spread, own)
    all_probs, outs = attend([here[:, :INNER] for here in windows], stacks, [bias] * len(windows))
    for w, probs in enumerate(all_probs):
        for g in range(GROUPS):
            probs_ref[w, g] = probs[g]
    heads = dot_nn(order_back_ref[...], jnp.concatenate(outs, axis=0)).astype(BF16)
    heads_ref[...] = heads
    branch = dot_nn(heads, w_proj_ref[0]).astype(BF16)
    stream = embedded + branch.astype(F32)
    wide_ref[:, D:] = stream
    unit_two, _ = norm_stats(stream)
    normed_two = (unit_two * gains_ref[1:2]).astype(BF16)
    d_heads_two = dot_nt(cot_ref[...], w_proj_ref[1]).astype(BF16)
    rolling = jnp.concatenate([normed_two, d_heads_two], axis=1)
    rolling_ref[...] = rolling
    band = one_ref.shape[0]
    upper, lower = rolling[:band], rolling[rows * cols - band :]
    odd = odd_ref[0] == 1
    one_ref[...] = jnp.where(odd, lower, upper)
    two_ref[...] = jnp.where(odd, upper, lower)


def edge_kernel(cols, odd_ref, core_ref, one_ref, rolling_ref, two_ref, to_one_ref, to_two_ref):
    band, cells = one_ref.shape[0], rolling_ref.shape[0]
    tall = jnp.concatenate([one_ref[...], rolling_ref[...], two_ref[...]], axis=0)
    shape = (SIDE, tall.shape[0])
    row = lax.broadcasted_iota(jnp.int32, shape, 0)
    place = lax.broadcasted_iota(jnp.int32, shape, 1)
    i = row // HALF_LON
    far = odd_ref[0] * (band + cells)
    first = jnp.where(i < HALF_LAT, band - HALF_LAT * cols + far, band - HALF_LAT * cols)
    first = jnp.where(i >= HALF_LAT + WIN_LAT, first - far, first)
    source = first + i * cols + row % HALF_LON
    source = jnp.where(i < 2 * WIN_LAT, source, -1)
    shift = (cols - HALF_LON) * core_ref[0]
    for out_ref, column in ((to_one_ref, shift), (to_two_ref, cols - HALF_LON - shift)):
        pick = jnp.where(place == jnp.where(source < 0, -1, source + column), 1.0, 0.0).astype(BF16)
        out_ref[...] = dot_nn(pick, tall).astype(BF16)


def second_kernel(
    odd_ref, core_ref, row_ref, keep_ref, one_ref, rolling_ref, two_ref, side_one_ref, side_two_ref,
    wide_ref, qkv_ref, heads_ref, probs_ref, cot_ref, gains_ref, w_qkv_ref, w_proj_ref, table_ref,
    order_ref, order_back_ref, near_order_ref, near_back_ref, spread_ref, spread_back_ref, reach_ref,
    output_ref, grad_ref, kept_ref, sent_ref,
):
    lat_count = keep_ref.shape[0]
    row_first = row_ref[0]
    spread, spread_back, own = spread_ref[...], spread_back_ref[...], own_head()
    odd, upper = odd_ref[0] == 1, core_ref[0] == 1
    one, two, side_one, side_two = one_ref[...], two_ref[...], side_one_ref[...], side_two_ref[...]
    near = jnp.concatenate(
        [
            jnp.where(odd, two, one), rolling_ref[...], jnp.where(odd, one, two),
            jnp.where(upper, side_two, side_one), jnp.where(upper, side_one, side_two),
        ],
        axis=0,
    )
    ordered = dot_nn(near_order_ref[...], near).astype(BF16)
    qkv_two = dot_nn(ordered[:, :D], w_qkv_ref[1]).astype(BF16)
    blocks = position_bias(table_ref[0], reach_ref[...])
    across = near_order_ref.shape[0] // PLACES // 2
    biases = []
    for u in range(2):

        def keep_of(a2, u=u):
            place = row_first + (u * WIN_LAT - HALF_LAT + a2)
            place = jnp.where(place < 0, place + lat_count, place)
            return keep_ref[jnp.where(place >= lat_count, place - lat_count, place)]

        last_band = jnp.where((row_first + u * WIN_LAT) % lat_count == 0, 1, 0)
        biases += [masked(blocks, keep_of, last_band)] * across
    windows = [window_rows(qkv_two, w) for w in range(2 * across)]
    d_outs = [window_rows(ordered, w)[:, D:] for w in range(2 * across)]
    queries = [here[:, :INNER] for here in windows]
    stacks = stack_up([here[:, INNER:] for here in windows], spread, own)
    all_probs, outs = attend(queries, stacks, biases)
    d_windows = attend_back(d_outs, all_probs, queries, stacks, spread_back, own)
    rows_two = jnp.concatenate([jnp.concatenate(d_windows, axis=0), jnp.concatenate(outs, axis=0)], axis=1)
    unrolled = dot_nn(near_back_ref[...], rows_two).astype(BF16)
    heads_two = unrolled[:, 3 * INNER :]
    d_normed_two = dot_nt(unrolled[:, : 3 * INNER], w_qkv_ref[1]).astype(BF16)

    stream = wide_ref[:, D:]
    unit_two, inv_two = norm_stats(stream)
    d_branch, gain_two = norm_back(d_normed_two.astype(F32), unit_two, inv_two, gains_ref[1:2])
    cotangent = cot_ref[...]
    d_stream = (cotangent.astype(F32) + d_branch).astype(BF16)
    branch_two = dot_nn(heads_two, w_proj_ref[1]).astype(BF16)
    output_ref[...] = stream + branch_two.astype(F32)
    proj_one = dot_tn(heads_ref[...], d_stream)
    proj_two = dot_tn(heads_two, cotangent)
    kept_ref[:INNER] = jnp.where(upper, proj_two, proj_one).astype(BF16)
    sent_ref[:INNER] = jnp.where(upper, proj_one, proj_two).astype(BF16)

    d_heads = dot_nt(d_stream, w_proj_ref[0]).astype(BF16)
    d_outs = dot_nn(order_ref[...], d_heads).astype(BF16)
    qkv_one = qkv_ref[...]
    windows = [window_rows(qkv_one, w) for w in range(probs_ref.shape[0])]
    d_outs = [window_rows(d_outs, w) for w in range(probs_ref.shape[0])]
    stacks = stack_up([here[:, INNER:] for here in windows], spread, own)
    all_probs = [[probs_ref[w, g] for g in range(GROUPS)] for w in range(probs_ref.shape[0])]
    d_windows = attend_back(d_outs, all_probs, [here[:, :INNER] for here in windows], stacks, spread_back, own)
    d_qkv = dot_nn(order_back_ref[...], jnp.concatenate(d_windows, axis=0)).astype(BF16)
    d_normed = dot_nt(d_qkv, w_qkv_ref[0]).astype(BF16)
    unit_one, inv_one = norm_stats(wide_ref[:, :D])
    d_branch, gain_one = norm_back(d_normed.astype(F32), unit_one, inv_one, gains_ref[0:1])
    grad_ref[...] = (d_stream.astype(F32) + d_branch).astype(BF16)
    gain = jnp.concatenate(
        [row[:, 128 * j : 128 * (j + 1)] for row in (gain_one, gain_two) for j in range(D // 128)], axis=0
    )
    pair = jnp.concatenate([gain_pair(gain), jnp.zeros((2 * GAIN_ROWS, D - 128), BF16)], axis=1)
    kept_ref[INNER:] = pair
    sent_ref[INNER:] = pair


def gain_pair(gain):
    high = gain.astype(BF16).astype(F32)
    return jnp.concatenate([high, gain - high], axis=0).astype(BF16)


def pair_sum(pair):
    return pair[:GAIN_ROWS] + pair[GAIN_ROWS : 2 * GAIN_ROWS]


def core_sum_kernel(kept_ref, landed_ref, out_ref):
    total = kept_ref[...].astype(F32) + landed_ref[...].astype(F32)
    low = total[:INNER].astype(BF16)
    pair = gain_pair(pair_sum(total[INNER:, :128]))
    pieces, tall = out_ref.shape[0], out_ref.shape[1]
    for s in range(pieces):
        row, col = tall * (s // 2), D // 2 * (s % 2)
        out_ref[s, :, : D // 2] = low[row : row + tall, col : col + D // 2]
        out_ref[s, : 2 * GAIN_ROWS, D // 2 :] = pair
        if tall > 2 * GAIN_ROWS:
            out_ref[s, 2 * GAIN_ROWS :, D // 2 :] = jnp.zeros((tall - 2 * GAIN_ROWS, 128), BF16)


def added(parts_ref):
    total = parts_ref[0].astype(F32)
    for s in range(1, parts_ref.shape[0]):
        total = total + parts_ref[s].astype(F32)
    return total[:, : D // 2], pair_sum(total[:, D // 2 :])


def plane_sum_kernel(parts_ref, out_ref):
    proj, gain = added(parts_ref)
    low, pair = proj.astype(BF16), gain_pair(gain)
    tall = out_ref.shape[1]
    for s in range(out_ref.shape[0]):
        out_ref[s, :, : D // 2] = low
        out_ref[s, : 2 * GAIN_ROWS, D // 2 :] = pair
        if tall > 2 * GAIN_ROWS:
            out_ref[s, 2 * GAIN_ROWS :, D // 2 :] = jnp.zeros((tall - 2 * GAIN_ROWS, 128), BF16)


def depth_sum_kernel(scale, parts_ref, proj_ref, gains_ref):
    proj, gain = added(parts_ref)
    low = (proj * scale).astype(BF16)
    for s in range(proj_ref.shape[0]):
        proj_ref[s] = low
    gain = gain * scale
    per_row = D // 128
    for r in range(GAIN_ROWS):
        gains_ref[r // per_row : r // per_row + 1, 128 * (r % per_row) : 128 * (r % per_row + 1)] = gain[r : r + 1]


def join_kernel(core_ref, mine_ref, other_ref, out_ref):
    pieces, tall = mine_ref.shape[0], mine_ref.shape[1]
    upper = core_ref[0] == 1
    for s in range(pieces):
        row, col = tall * (s // 2), D // 2 * (s % 2)
        mine, other = mine_ref[s], other_ref[s]
        out_ref[0, row : row + tall, col : col + D // 2] = jnp.where(upper, other, mine)
        out_ref[1, row : row + tall, col : col + D // 2] = jnp.where(upper, mine, other)


def scalars(array):
    return array, pl.BlockSpec(memory_space=pltpu.SMEM)


def whole(array):
    return array, pl.BlockSpec(array.shape, functools.partial(lambda n, i: (0,) * n, array.ndim))


def in_hbm(array):
    return whole(pltpu.with_memory_space_constraint(array, pltpu.HBM))


def layer(array, index):
    spec = pl.BlockSpec((1,) + array.shape[1:], lambda i: (index,) + (0,) * (array.ndim - 1))
    return pltpu.with_memory_space_constraint(array, pltpu.HBM), spec


def hbm(*dims, dtype=BF16):
    return pltpu.HBM(dims, dtype)


def either(*dims, dtype=BF16):
    return jax.ShapeDtypeStruct(dims, dtype)


def call(kernel, outs, operands):
    arrays, specs = zip(*operands)
    out_specs = [pl.BlockSpec(o.shape, functools.partial(lambda n, i: (0,) * n, len(o.shape))) for o in outs]
    return pl.pallas_call(
        kernel,
        grid=(1,),
        in_specs=specs,
        out_specs=out_specs,
        out_shape=outs,
        compiler_params=pltpu.CompilerParams(vmem_limit_bytes=50 * 1024 * 1024),
    )(*arrays)


LON = ("z_lo", "x", "core")
LAT = ("z_hi", "y")
PLANE = ("x", "y")
DEPTH = ("z_lo", "z_hi")


def swapped(array, axes, side):
    length = lax.axis_size(axes)
    return lax.ppermute(array, axes, [(i, (i + (side if i % 2 else -side)) % length) for i in range(length)])


def local(tokens, land_mask, keep_rows, land_embed, norm_gains, w_qkv, w_proj, rel_bias, cotangent):
    rows, cols = tokens.shape[0], tokens.shape[1]
    cells, count = rows * cols, cols // WIN_LON
    band, wide = band_rows(cols), D + INNER
    scale_out = float(rows * lax.axis_size(LAT) * cols * lax.axis_size(LON)) ** (-0.5)
    row_first = scalars((lax.axis_index(LAT) * rows).astype(jnp.int32).reshape(1))
    odd = scalars((lax.axis_index(LAT) % 2).astype(jnp.int32).reshape(1))
    core = scalars(lax.axis_index("core").astype(jnp.int32).reshape(1))
    keep_in = scalars(keep_rows)
    order = own_windows(cols)
    order, order_back = in_hbm(fixed(order)), in_hbm(fixed(order.T))
    near_order, near_back = (in_hbm(fixed(m)) for m in near_windows(cols))
    spread = spread_matrix()
    spread, spread_back = in_hbm(fixed(spread)), in_hbm(fixed(spread.T))
    reach = in_hbm(fixed(reach_matrix()))
    cot_flat = in_hbm(cotangent.reshape(cells, D))

    wide_one, qkv_one, heads_one, probs_one, rolling, to_one, to_two = call(
        first_kernel,
        [
            hbm(cells, 2 * D, dtype=F32), hbm(count * PLACES, 3 * INNER), hbm(cells, INNER),
            hbm(count, GROUPS, TILES, 8, PLACES, dtype=F32), either(cells, wide), either(band, wide), either(band, wide),
        ],
        [
            odd, row_first, keep_in, in_hbm(tokens.reshape(cells, D)), in_hbm(land_mask), in_hbm(land_embed),
            in_hbm(norm_gains), layer(w_qkv, 0), in_hbm(w_proj), layer(rel_bias, 0), cot_flat,
            order, order_back, spread, reach,
        ],
    )

    one = swapped(to_one, LAT, 1)
    two = swapped(to_two, LAT, -1)
    to_one, to_two = call(
        functools.partial(edge_kernel, cols),
        [either(SIDE, wide), either(SIDE, wide)],
        [odd, core, whole(one), whole(rolling), whole(two)],
    )
    side_one = swapped(to_one, LON, 1)
    side_two = swapped(to_two, LON, -1)

    output, grad_tokens, kept, sent = call(
        second_kernel,
        [hbm(cells, D, dtype=F32), hbm(cells, D), either(INNER + 2 * GAIN_ROWS, D), either(INNER + 2 * GAIN_ROWS, D)],
        [
            odd, core, row_first, keep_in, whole(one), whole(rolling), whole(two), whole(side_one), whole(side_two),
            in_hbm(wide_one), in_hbm(qkv_one), in_hbm(heads_one), in_hbm(probs_one), cot_flat,
            in_hbm(norm_gains), in_hbm(w_qkv), in_hbm(w_proj), layer(rel_bias, 1),
            order, order_back, near_order, near_back, spread, spread_back, reach,
        ],
    )

    planes, depths, cores = lax.axis_size(PLANE), lax.axis_size(DEPTH), lax.axis_size("core")
    tall = 2 * INNER // planes
    swap = [(i, (i + 1) % cores) for i in range(cores)]
    landed = lax.ppermute(sent, "core", swap)
    (pieces,) = call(core_sum_kernel, [either(planes, tall, D // 2 + 128)], [whole(kept), whole(landed)])
    parts = lax.all_to_all(pieces, PLANE, 0, 0, tiled=True)
    (pieces,) = call(plane_sum_kernel, [either(depths, tall, D // 2 + 128)], [whole(parts)])
    parts = lax.all_to_all(pieces, DEPTH, 0, 0, tiled=True)
    pieces, grad_gains = call(
        functools.partial(depth_sum_kernel, scale_out),
        [either(planes, tall, D // 2), either(2, D, dtype=F32)],
        [whole(parts)],
    )
    mine = lax.all_to_all(pieces, PLANE, 0, 0, tiled=True)
    other = lax.ppermute(mine, "core", swap)
    (grad_proj,) = call(join_kernel, [either(2, INNER, D)], [core, whole(mine), whole(other)])
    return output.reshape(rows, cols, D), grad_tokens.reshape(rows, cols, D), grad_proj, grad_gains


def chip_axes(lon, lat):
    x = min(4, lon // 2)
    y = min(8, lat)
    return (lon // (2 * x), x, 2, lat // y, y)


def solution(mesh):
    sizes = chip_axes(mesh.shape["lon"], mesh.shape["lat"])
    fine = Mesh(mesh.devices.reshape(sizes), LON + LAT)
    grid = P(LAT, LON, None)
    in_specs = (grid, P(LAT, LON), P(), P(), P(), P(), P(), P(), grid)
    out_specs = (grid, grid, P(), P())
    return jax.shard_map(local, mesh=fine, in_specs=in_specs, out_specs=out_specs, check_vma=False)
```

```python
import functools

import jax
import jax.numpy as jnp
import numpy as np
from jax import lax
from jax.experimental import pallas as pl
from jax.experimental.pallas import tpu as pltpu
from jax.sharding import Mesh
from jax.sharding import PartitionSpec as P

D = 512
HEAD_DIM = 32
HEADS = 8
INNER = HEADS * HEAD_DIM
WIN_LAT = 6
WIN_LON = 12
HALF_LAT = WIN_LAT // 2
HALF_LON = WIN_LON // 2
WIN = WIN_LAT * WIN_LON
SPAN_LON = 2 * WIN_LON - 1
REACH = WIN_LAT * SPAN_LON
PLACES = 80
SIDE = 80
GROUP = 4
GROUPS = HEADS // GROUP
SHEET = GROUP * HEAD_DIM
TILES = WIN * GROUP // 8
LOG2E = 1.4426950408889634
STACK = WIN * GROUP
GAIN_ROWS = 8

NORM_EPS = 1e-05
SCALE = HEAD_DIM ** (-0.5)
SHUT = -1e30

F32 = jnp.float32
BF16 = jnp.bfloat16


def dot_nn(left, right):
    return lax.dot_general(left, right, (((1,), (0,)), ((), ())), preferred_element_type=F32)


def dot_nt(left, right):
    return lax.dot_general(left, right, (((1,), (1,)), ((), ())), preferred_element_type=F32)


def dot_tn(left, right):
    return lax.dot_general(left, right, (((0,), (0,)), ((), ())), preferred_element_type=F32)


def spread_matrix():
    spread = np.zeros((WIN, GROUP, PLACES), np.float32)
    for key in range(WIN):
        spread[key, :, key] = 1
    return spread.reshape(STACK, PLACES)


def reach_matrix():
    reach = np.zeros((REACH, WIN_LON, 128), np.float32)
    for e2 in range(WIN_LON):
        for a in range(WIN_LAT):
            for e in range(WIN_LON):
                reach[a * SPAN_LON + e - e2 + WIN_LON - 1, e2, e * WIN_LAT + a] = 1
    return reach.reshape(REACH, -1)


def own_windows(cols):
    order = np.zeros((cols // WIN_LON, PLACES, WIN_LAT * cols), np.float32)
    for w in range(cols // WIN_LON):
        for a in range(WIN_LAT):
            for e in range(WIN_LON):
                order[w, e * WIN_LAT + a, a * cols + w * WIN_LON + e] = 1
    return order.reshape(-1, WIN_LAT * cols)


def band_rows(cols):
    return -(-HALF_LAT * cols // 16) * 16


def near_place(i, j, cols):
    band = band_rows(cols)
    if 0 <= j < cols:
        return band - HALF_LAT * cols + (i + HALF_LAT) * cols + j
    first = 2 * band + WIN_LAT * cols + (0 if j < 0 else SIDE)
    return first + (i + HALF_LAT) * HALF_LON + (j + HALF_LON if j < 0 else j - cols)


def near_windows(cols):
    cells, across = WIN_LAT * cols, cols // WIN_LON + 1
    near = 2 * (band_rows(cols) + SIDE) + cells
    order = np.zeros((2, across, PLACES, near), np.float32)
    back = np.zeros((cells, 2, across, PLACES), np.float32)
    for u in range(2):
        for v in range(across):
            for a in range(WIN_LAT):
                for e in range(WIN_LON):
                    i, j = u * WIN_LAT + a - HALF_LAT, v * WIN_LON + e - HALF_LON
                    place = e * WIN_LAT + a
                    order[u, v, place, near_place(i, j, cols)] = 1
                    if 0 <= i < WIN_LAT and 0 <= j < cols:
                        back[i * cols + j, u, v, place] = 1
    return order.reshape(-1, near), back.reshape(cells, -1)


def fixed(matrix):
    return jnp.asarray(matrix, BF16)


def norm_stats(values):
    row_mean = jnp.sum(values, axis=-1, keepdims=True) * (1.0 / D)
    centred = values - row_mean
    row_var = jnp.sum(centred * centred, axis=-1, keepdims=True) * (1.0 / D)
    inv_std = lax.rsqrt(row_var + NORM_EPS)
    return centred * inv_std, inv_std


def norm_back(d_float, unit_rows, inv_std, gain_row):
    d_unit = d_float * gain_row
    mean_grad = jnp.sum(d_unit, axis=-1, keepdims=True) * (1.0 / D)
    mean_proj = jnp.sum(d_unit * unit_rows, axis=-1, keepdims=True) * (1.0 / D)
    d_input = inv_std * (d_unit - mean_grad - unit_rows * mean_proj)
    return d_input, jnp.sum(d_float * unit_rows, axis=0, keepdims=True)


def position_bias(table, reach):
    table = table * LOG2E
    shifted = jnp.concatenate(
        [
            table[g * GROUP : (g + 1) * GROUP, (WIN_LAT - 1 - a2) * SPAN_LON : (WIN_LAT - 1 - a2) * SPAN_LON + REACH]
            for g in range(GROUPS)
            for a2 in range(WIN_LAT)
        ],
        axis=0,
    )
    high = shifted.astype(BF16)
    rest = shifted - high.astype(F32)
    middle = rest.astype(BF16)
    low = (rest - middle.astype(F32)).astype(BF16)
    spread = dot_nn(high, reach) + (dot_nn(middle, reach) + dot_nn(low, reach))
    return [spread[:, 128 * e2 : 128 * e2 + PLACES] for e2 in range(WIN_LON)]


def masked(blocks, keep_of, split_rows):
    rows = WIN_LAT * GROUP
    place = lax.broadcasted_iota(jnp.int32, (rows, PLACES), 1)
    key_row = lax.broadcasted_iota(jnp.int32, (rows, PLACES), 0) // GROUP
    query_late = jnp.where(place % WIN_LAT >= HALF_LAT, 1, 0)
    key_late = jnp.where(key_row >= HALF_LAT, 1, 0)
    shut = jnp.where(query_late == key_late, 0, 1) * split_rows
    for a2 in range(WIN_LAT):
        shut = shut + jnp.where(key_row == a2, 1, 0) * jnp.where(keep_of(a2) == 1, 0, 1)
    tile = jnp.where(shut > 0, SHUT, 0.0).astype(F32)
    return [
        jnp.concatenate([block[g * rows : (g + 1) * rows] + tile for block in blocks], axis=0).reshape(TILES, 8, PLACES)
        for g in range(GROUPS)
    ]


def own_head():
    head = lax.broadcasted_iota(jnp.int32, (8, 2 * INNER), 0) % GROUP
    lane = lax.broadcasted_iota(jnp.int32, (8, 2 * INNER), 1)
    return jnp.where((lane // HEAD_DIM) % GROUP == head, 1.0, 0.0).astype(F32)[None]


def sheet(array, g):
    return array[:, g * SHEET : (g + 1) * SHEET]


def own_parts(stacked, own):
    return (stacked.reshape(TILES, 8, 2 * INNER) * own).reshape(STACK, 2 * INNER).astype(BF16)


def stack_up(key_values, spread, own):
    stacks = [own_parts(stacked, own) for stacked in [dot_nn(spread, each) for each in key_values]]
    return [(stack[:, :INNER], stack[:, INNER:]) for stack in stacks]


def over_keys(combine, tiles):
    return combine(tiles, jnp.concatenate([tiles[GROUP:], tiles[:GROUP]], axis=0))


def attend(queries, stacks, biases):
    both = [(w, g) for w in range(len(queries)) for g in range(GROUPS)]
    scores = [dot_nt(sheet(stacks[w][0], g), sheet(queries[w], g)) for w, g in both]
    scores = [
        one.reshape(TILES, 8, PLACES) * (SCALE * LOG2E) + biases[w][g] for one, (w, g) in zip(scores, both)
    ]
    tops = [over_keys(jnp.maximum, jnp.max(one, axis=0)) for one in scores]
    exps = [jnp.exp2(one - top) for one, top in zip(scores, tops)]
    shares = [1.0 / over_keys(jnp.add, jnp.sum(one, axis=0)) for one in exps]
    probs = [one * share for one, share in zip(exps, shares)]
    lows = [one.reshape(STACK, PLACES).astype(BF16) for one in probs]
    outs = [dot_tn(low, sheet(stacks[w][1], g)).astype(BF16) for low, (w, g) in zip(lows, both)]
    per_window = [slice(w * GROUPS, (w + 1) * GROUPS) for w in range(len(queries))]
    return [probs[here] for here in per_window], [jnp.concatenate(outs[here], axis=1) for here in per_window]


def attend_back(d_outs, probs, queries, stacks, spread_back, own):
    both = [(w, g) for w in range(len(queries)) for g in range(GROUPS)]
    d_probs = [dot_nt(sheet(stacks[w][1], g), sheet(d_outs[w], g)) for w, g in both]
    d_probs = [one.reshape(TILES, 8, PLACES) for one in d_probs]
    totals = [over_keys(jnp.add, jnp.sum(one * probs[w][g], axis=0)) for one, (w, g) in zip(d_probs, both)]
    d_lows = [
        (probs[w][g] * (one - total) * SCALE).reshape(STACK, PLACES).astype(BF16)
        for one, total, (w, g) in zip(d_probs, totals, both)
    ]
    lows = [probs[w][g].reshape(STACK, PLACES).astype(BF16) for w, g in both]
    d_values = [dot_nn(low, sheet(d_outs[w], g)) for low, (w, g) in zip(lows, both)]
    d_keys = [dot_nn(d_low, sheet(queries[w], g)) for d_low, (w, g) in zip(d_lows, both)]
    d_queries = [dot_tn(d_low, sheet(stacks[w][0], g)).astype(BF16) for d_low, (w, g) in zip(d_lows, both)]
    per_window = [slice(w * GROUPS, (w + 1) * GROUPS) for w in range(len(queries))]
    d_stacks = [own_parts(jnp.concatenate(d_keys[here] + d_values[here], axis=1), own) for here in per_window]
    d_rest = [dot_nn(spread_back, d_stack).astype(BF16) for d_stack in d_stacks]
    return [jnp.concatenate(d_queries[here] + [rest], axis=1) for here, rest in zip(per_window, d_rest)]


def window_rows(array, w):
    return array[w * PLACES : (w + 1) * PLACES]


def first_kernel(
    odd_ref, row_ref, keep_ref, tokens_ref, mask_ref, embed_ref, gains_ref, w_qkv_ref, w_proj_ref, table_ref, cot_ref,
    order_ref, order_back_ref, spread_ref, reach_ref,
    wide_ref, qkv_ref, heads_ref, probs_ref, rolling_ref, one_ref, two_ref,
):
    rows, cols = mask_ref.shape
    mask = mask_ref[...].astype(F32)
    spread_mask = jnp.concatenate([jnp.broadcast_to(mask[r : r + 1], (cols, cols)) for r in range(rows)], axis=0)
    cell = lax.broadcasted_iota(jnp.int32, (rows * cols, cols), 0)
    lane = lax.broadcasted_iota(jnp.int32, (rows * cols, cols), 1)
    land = jnp.sum(jnp.where(cell % cols == lane, spread_mask, 0.0), axis=1, keepdims=True)
    embedded = tokens_ref[...].astype(F32) + jnp.where(land == 1.0, embed_ref[1:2], embed_ref[0:1])
    wide_ref[:, :D] = embedded
    unit_one, _ = norm_stats(embedded)
    normed_one = (unit_one * gains_ref[0:1]).astype(BF16)
    ordered = dot_nn(order_ref[...], normed_one).astype(BF16)
    qkv = dot_nn(ordered, w_qkv_ref[0]).astype(BF16)
    qkv_ref[...] = qkv
    bias = masked(position_bias(table_ref[0], reach_ref[...]), lambda a2: keep_ref[row_ref[0] + a2], 0)
    spread, own = spread_ref[...], own_head()
    windows = [window_rows(qkv, w) for w in range(cols // WIN_LON)]
    stacks = stack_up([here[:, INNER:] for here in windows], spread, own)
    all_probs, outs = attend([here[:, :INNER] for here in windows], stacks, [bias] * len(windows))
    for w, probs in enumerate(all_probs):
        for g in range(GROUPS):
            probs_ref[w, g] = probs[g]
    heads = dot_nn(order_back_ref[...], jnp.concatenate(outs, axis=0)).astype(BF16)
    heads_ref[...] = heads
    branch = dot_nn(heads, w_proj_ref[0]).astype(BF16)
    stream = embedded + branch.astype(F32)
    wide_ref[:, D:] = stream
    unit_two, _ = norm_stats(stream)
    normed_two = (unit_two * gains_ref[1:2]).astype(BF16)
    d_heads_two = dot_nt(cot_ref[...], w_proj_ref[1]).astype(BF16)
    rolling = jnp.concatenate([normed_two, d_heads_two], axis=1)
    rolling_ref[...] = rolling
    band = one_ref.shape[0]
    upper, lower = rolling[:band], rolling[rows * cols - band :]
    odd = odd_ref[0] == 1
    one_ref[...] = jnp.where(odd, lower, upper)
    two_ref[...] = jnp.where(odd, upper, lower)


def edge_kernel(cols, odd_ref, core_ref, one_ref, rolling_ref, two_ref, to_one_ref, to_two_ref):
    band, cells = one_ref.shape[0], rolling_ref.shape[0]
    tall = jnp.concatenate([one_ref[...], rolling_ref[...], two_ref[...]], axis=0)
    shape = (SIDE, tall.shape[0])
    row = lax.broadcasted_iota(jnp.int32, shape, 0)
    place = lax.broadcasted_iota(jnp.int32, shape, 1)
    i = row // HALF_LON
    far = odd_ref[0] * (band + cells)
    first = jnp.where(i < HALF_LAT, band - HALF_LAT * cols + far, band - HALF_LAT * cols)
    first = jnp.where(i >= HALF_LAT + WIN_LAT, first - far, first)
    source = first + i * cols + row % HALF_LON
    source = jnp.where(i < 2 * WIN_LAT, source, -1)
    shift = (cols - HALF_LON) * core_ref[0]
    for out_ref, column in ((to_one_ref, shift), (to_two_ref, cols - HALF_LON - shift)):
        pick = jnp.where(place == jnp.where(source < 0, -1, source + column), 1.0, 0.0).astype(BF16)
        out_ref[...] = dot_nn(pick, tall).astype(BF16)


def second_kernel(
    odd_ref, core_ref, row_ref, keep_ref, one_ref, rolling_ref, two_ref, side_one_ref, side_two_ref,
    wide_ref, qkv_ref, heads_ref, probs_ref, cot_ref, gains_ref, w_qkv_ref, w_proj_ref, table_ref,
    order_ref, order_back_ref, near_order_ref, near_back_ref, spread_ref, spread_back_ref, reach_ref,
    output_ref, grad_ref, kept_ref, sent_ref,
):
    lat_count = keep_ref.shape[0]
    row_first = row_ref[0]
    spread, spread_back, own = spread_ref[...], spread_back_ref[...], own_head()
    odd, upper = odd_ref[0] == 1, core_ref[0] == 1
    one, two, side_one, side_two = one_ref[...], two_ref[...], side_one_ref[...], side_two_ref[...]
    near = jnp.concatenate(
        [
            jnp.where(odd, two, one), rolling_ref[...], jnp.where(odd, one, two),
            jnp.where(upper, side_two, side_one), jnp.where(upper, side_one, side_two),
        ],
        axis=0,
    )
    ordered = dot_nn(near_order_ref[...], near).astype(BF16)
    qkv_two = dot_nn(ordered[:, :D], w_qkv_ref[1]).astype(BF16)
    blocks = position_bias(table_ref[0], reach_ref[...])
    across = near_order_ref.shape[0] // PLACES // 2
    biases = []
    for u in range(2):

        def keep_of(a2, u=u):
            place = row_first + (u * WIN_LAT - HALF_LAT + a2)
            place = jnp.where(place < 0, place + lat_count, place)
            return keep_ref[jnp.where(place >= lat_count, place - lat_count, place)]

        last_band = jnp.where((row_first + u * WIN_LAT) % lat_count == 0, 1, 0)
        biases += [masked(blocks, keep_of, last_band)] * across
    windows = [window_rows(qkv_two, w) for w in range(2 * across)]
    d_outs = [window_rows(ordered, w)[:, D:] for w in range(2 * across)]
    queries = [here[:, :INNER] for here in windows]
    stacks = stack_up([here[:, INNER:] for here in windows], spread, own)
    all_probs, outs = attend(queries, stacks, biases)
    d_windows = attend_back(d_outs, all_probs, queries, stacks, spread_back, own)
    rows_two = jnp.concatenate([jnp.concatenate(d_windows, axis=0), jnp.concatenate(outs, axis=0)], axis=1)
    unrolled = dot_nn(near_back_ref[...], rows_two).astype(BF16)
    heads_two = unrolled[:, 3 * INNER :]
    d_normed_two = dot_nt(unrolled[:, : 3 * INNER], w_qkv_ref[1]).astype(BF16)

    stream = wide_ref[:, D:]
    unit_two, inv_two = norm_stats(stream)
    d_branch, gain_two = norm_back(d_normed_two.astype(F32), unit_two, inv_two, gains_ref[1:2])
    cotangent = cot_ref[...]
    d_stream = (cotangent.astype(F32) + d_branch).astype(BF16)
    branch_two = dot_nn(heads_two, w_proj_ref[1]).astype(BF16)
    output_ref[...] = stream + branch_two.astype(F32)
    proj_one = dot_tn(heads_ref[...], d_stream)
    proj_two = dot_tn(heads_two, cotangent)
    kept_ref[:INNER] = jnp.where(upper, proj_two, proj_one).astype(BF16)
    sent_ref[:INNER] = jnp.where(upper, proj_one, proj_two).astype(BF16)

    d_heads = dot_nt(d_stream, w_proj_ref[0]).astype(BF16)
    d_outs = dot_nn(order_ref[...], d_heads).astype(BF16)
    qkv_one = qkv_ref[...]
    windows = [window_rows(qkv_one, w) for w in range(probs_ref.shape[0])]
    d_outs = [window_rows(d_outs, w) for w in range(probs_ref.shape[0])]
    stacks = stack_up([here[:, INNER:] for here in windows], spread, own)
    all_probs = [[probs_ref[w, g] for g in range(GROUPS)] for w in range(probs_ref.shape[0])]
    d_windows = attend_back(d_outs, all_probs, [here[:, :INNER] for here in windows], stacks, spread_back, own)
    d_qkv = dot_nn(order_back_ref[...], jnp.concatenate(d_windows, axis=0)).astype(BF16)
    d_normed = dot_nt(d_qkv, w_qkv_ref[0]).astype(BF16)
    unit_one, inv_one = norm_stats(wide_ref[:, :D])
    d_branch, gain_one = norm_back(d_normed.astype(F32), unit_one, inv_one, gains_ref[0:1])
    grad_ref[...] = (d_stream.astype(F32) + d_branch).astype(BF16)
    gain = jnp.concatenate(
        [row[:, 128 * j : 128 * (j + 1)] for row in (gain_one, gain_two) for j in range(D // 128)], axis=0
    )
    pair = jnp.concatenate([gain_pair(gain), jnp.zeros((2 * GAIN_ROWS, D - 128), BF16)], axis=1)
    kept_ref[INNER:] = pair
    sent_ref[INNER:] = pair


def gain_pair(gain):
    high = gain.astype(BF16).astype(F32)
    return jnp.concatenate([high, gain - high], axis=0).astype(BF16)


def pair_sum(pair):
    return pair[:GAIN_ROWS] + pair[GAIN_ROWS : 2 * GAIN_ROWS]


def core_sum_kernel(kept_ref, landed_ref, out_ref):
    total = kept_ref[...].astype(F32) + landed_ref[...].astype(F32)
    low = total[:INNER].astype(BF16)
    pair = gain_pair(pair_sum(total[INNER:, :128]))
    pieces, tall = out_ref.shape[0], out_ref.shape[1]
    for s in range(pieces):
        fill_piece(out_ref, s, low[s * tall : (s + 1) * tall], pair)


def fill_piece(out_ref, s, low, pair):
    tall = out_ref.shape[1]
    out_ref[s, :, :D] = low
    out_ref[s, : 2 * GAIN_ROWS, D:] = pair
    if tall > 2 * GAIN_ROWS:
        out_ref[s, 2 * GAIN_ROWS :, D:] = jnp.zeros((tall - 2 * GAIN_ROWS, 128), BF16)


def added(parts_ref):
    total = parts_ref[0].astype(F32)
    for s in range(1, parts_ref.shape[0]):
        total = total + parts_ref[s].astype(F32)
    return total[:, :D], pair_sum(total[:, D:])


def near_sum_kernel(parts_ref, out_ref):
    proj, gain = added(parts_ref)
    low, pair = proj.astype(BF16), gain_pair(gain)
    for s in range(out_ref.shape[0]):
        fill_piece(out_ref, s, low, pair)


def far_sum_kernel(scale, parts_ref, proj_ref, gains_ref):
    proj, gain = added(parts_ref)
    low = (proj * scale).astype(BF16)
    for s in range(proj_ref.shape[0]):
        proj_ref[s] = low
    gain = gain * scale
    per_row = D // 128
    for r in range(GAIN_ROWS):
        gains_ref[r // per_row : r // per_row + 1, 128 * (r % per_row) : 128 * (r % per_row + 1)] = gain[r : r + 1]


def join_kernel(core_ref, mine_ref, other_ref, out_ref):
    upper = core_ref[0] == 1
    mine, other = mine_ref[...], other_ref[...]
    out_ref[0] = jnp.where(upper, other, mine)
    out_ref[1] = jnp.where(upper, mine, other)


def scalars(array):
    return pltpu.with_memory_space_constraint(array, pltpu.HBM), pl.BlockSpec(memory_space=pltpu.SMEM)


def whole(array):
    return array, pl.BlockSpec(array.shape, functools.partial(lambda n, i: (0,) * n, array.ndim))


def in_hbm(array):
    return whole(pltpu.with_memory_space_constraint(array, pltpu.HBM))


def layer(array, index):
    spec = pl.BlockSpec((1,) + array.shape[1:], lambda i: (index,) + (0,) * (array.ndim - 1))
    return pltpu.with_memory_space_constraint(array, pltpu.HBM), spec


def hbm(*dims, dtype=BF16):
    return pltpu.HBM(dims, dtype)


def either(*dims, dtype=BF16):
    return jax.ShapeDtypeStruct(dims, dtype)


def call(kernel, outs, operands):
    arrays, specs = zip(*operands)
    out_specs = [pl.BlockSpec(o.shape, functools.partial(lambda n, i: (0,) * n, len(o.shape))) for o in outs]
    return pl.pallas_call(
        kernel,
        grid=(1,),
        in_specs=specs,
        out_specs=out_specs,
        out_shape=outs,
        compiler_params=pltpu.CompilerParams(vmem_limit_bytes=30 * 1024 * 1024),
    )(*arrays)


LON = ("z_mid", "z_low", "x", "core")
LAT = ("z_hi", "y_hi", "y_low")
NEAR = ("z_low", "x", "y_low")
FAR = ("z_mid", "z_hi", "y_hi")


def swapped(array, axes, side):
    length = lax.axis_size(axes)
    return lax.ppermute(array, axes, [(i, (i + (side if i % 2 else -side)) % length) for i in range(length)])


def local(tokens, land_mask, keep_rows, land_embed, norm_gains, w_qkv, w_proj, rel_bias, cotangent):
    rows, cols = tokens.shape[0], tokens.shape[1]
    cells, count = rows * cols, cols // WIN_LON
    band, wide = band_rows(cols), D + INNER
    scale_out = float(rows * lax.axis_size(LAT) * cols * lax.axis_size(LON)) ** (-0.5)
    row_first = scalars((lax.axis_index(LAT) * rows).astype(jnp.int32).reshape(1))
    odd = scalars((lax.axis_index(LAT) % 2).astype(jnp.int32).reshape(1))
    core = scalars(lax.axis_index("core").astype(jnp.int32).reshape(1))
    keep_in = scalars(keep_rows)
    order = own_windows(cols)
    order, order_back = in_hbm(fixed(order)), in_hbm(fixed(order.T))
    near_order, near_back = (in_hbm(fixed(m)) for m in near_windows(cols))
    spread = spread_matrix()
    spread, spread_back = in_hbm(fixed(spread)), in_hbm(fixed(spread.T))
    reach = in_hbm(fixed(reach_matrix()))
    cot_flat = in_hbm(cotangent.reshape(cells, D))

    wide_one, qkv_one, heads_one, probs_one, rolling, to_one, to_two = call(
        first_kernel,
        [
            either(cells, 2 * D, dtype=F32), either(count * PLACES, 3 * INNER), either(cells, INNER),
            either(count, GROUPS, TILES, 8, PLACES, dtype=F32), either(cells, wide), either(band, wide), either(band, wide),
        ],
        [
            odd, row_first, keep_in, in_hbm(tokens.reshape(cells, D)), in_hbm(land_mask), in_hbm(land_embed),
            in_hbm(norm_gains), layer(w_qkv, 0), in_hbm(w_proj), layer(rel_bias, 0), cot_flat,
            order, order_back, spread, reach,
        ],
    )

    one = swapped(to_one, LAT, 1)
    two = swapped(to_two, LAT, -1)
    to_one, to_two = call(
        functools.partial(edge_kernel, cols),
        [either(SIDE, wide), either(SIDE, wide)],
        [odd, core, whole(one), whole(rolling), whole(two)],
    )
    side_one = swapped(to_one, LON, 1)
    side_two = swapped(to_two, LON, -1)

    output, grad_tokens, kept, sent = call(
        second_kernel,
        [hbm(cells, D, dtype=F32), hbm(cells, D), either(INNER + 2 * GAIN_ROWS, D), either(INNER + 2 * GAIN_ROWS, D)],
        [
            odd, core, row_first, keep_in, whole(one), whole(rolling), whole(two), whole(side_one), whole(side_two),
            whole(wide_one), whole(qkv_one), whole(heads_one), whole(probs_one), cot_flat,
            in_hbm(norm_gains), in_hbm(w_qkv), in_hbm(w_proj), layer(rel_bias, 1),
            order, order_back, near_order, near_back, spread, spread_back, reach,
        ],
    )

    near, far = lax.axis_size(NEAR), lax.axis_size(FAR)
    tall = INNER // near
    swap = [(0, 1), (1, 0)]
    landed = lax.ppermute(sent, "core", swap)
    (pieces,) = call(core_sum_kernel, [either(near, tall, D + 128)], [whole(kept), whole(landed)])
    parts = lax.all_to_all(pieces, NEAR, 0, 0, tiled=True)
    (pieces,) = call(near_sum_kernel, [either(far, tall, D + 128)], [whole(parts)])
    parts = lax.all_to_all(pieces, FAR, 0, 0, tiled=True)
    pieces, grad_gains = call(
        functools.partial(far_sum_kernel, scale_out),
        [either(near, tall, D), either(2, D, dtype=F32)],
        [whole(parts)],
    )
    mine = lax.all_to_all(pieces, NEAR, 0, 0, tiled=True).reshape(INNER, D)
    other = lax.ppermute(mine, "core", swap)
    (grad_proj,) = call(join_kernel, [either(2, INNER, D)], [core, whole(mine), whole(other)])
    return output.reshape(rows, cols, D), grad_tokens.reshape(rows, cols, D), grad_proj, grad_gains


def halved(length):
    return (length // 2, 2) if length % 2 == 0 else (length, 1)


def chip_axes(lon, lat):
    x = min(4, lon // 2)
    y = min(8, lat)
    return (*halved(lon // (2 * x)), x, 2, lat // y, *halved(y))


def solution(mesh):
    sizes = chip_axes(mesh.shape["lon"], mesh.shape["lat"])
    fine = Mesh(mesh.devices.reshape(sizes), LON + LAT)
    grid = P(LAT, LON, None)
    in_specs = (grid, P(LAT, LON), P(), P(), P(), P(), P(), P(), grid)
    out_specs = (grid, grid, P(), P())
    return jax.shard_map(local, mesh=fine, in_specs=in_specs, out_specs=out_specs, check_vma=False)
```

```python
import functools

import jax
import jax.numpy as jnp
import numpy as np
from jax import lax
from jax.experimental import pallas as pl
from jax.experimental.pallas import tpu as pltpu
from jax.sharding import Mesh
from jax.sharding import PartitionSpec as P

D = 512
HEAD_DIM = 32
HEADS = 8
INNER = HEADS * HEAD_DIM
WIN_LAT = 6
WIN_LON = 12
HALF_LAT = WIN_LAT // 2
HALF_LON = WIN_LON // 2
WIN = WIN_LAT * WIN_LON
SPAN_LON = 2 * WIN_LON - 1
REACH = WIN_LAT * SPAN_LON
PLACES = 80
SIDE = 80
GROUP = 4
GROUPS = HEADS // GROUP
SHEET = GROUP * HEAD_DIM
TILES = WIN * GROUP // 8
LOG2E = 1.4426950408889634
STACK = WIN * GROUP
GAIN_ROWS = 8

NORM_EPS = 1e-05
SCALE = HEAD_DIM ** (-0.5)
SHUT = -1e30

F32 = jnp.float32
BF16 = jnp.bfloat16


def dot_nn(left, right):
    return lax.dot_general(left, right, (((1,), (0,)), ((), ())), preferred_element_type=F32)


def dot_nt(left, right):
    return lax.dot_general(left, right, (((1,), (1,)), ((), ())), preferred_element_type=F32)


def dot_tn(left, right):
    return lax.dot_general(left, right, (((0,), (0,)), ((), ())), preferred_element_type=F32)


def spread_matrix():
    spread = np.zeros((WIN, GROUP, PLACES), np.float32)
    for key in range(WIN):
        spread[key, :, key] = 1
    return spread.reshape(STACK, PLACES)


def reach_matrix():
    reach = np.zeros((REACH, WIN_LON, 128), np.float32)
    for e2 in range(WIN_LON):
        for a in range(WIN_LAT):
            for e in range(WIN_LON):
                reach[a * SPAN_LON + e - e2 + WIN_LON - 1, e2, e * WIN_LAT + a] = 1
    return reach.reshape(REACH, -1)


def own_windows(cols):
    order = np.zeros((cols // WIN_LON, PLACES, WIN_LAT * cols), np.float32)
    for w in range(cols // WIN_LON):
        for a in range(WIN_LAT):
            for e in range(WIN_LON):
                order[w, e * WIN_LAT + a, a * cols + w * WIN_LON + e] = 1
    return order.reshape(-1, WIN_LAT * cols)


def band_rows(cols):
    return -(-HALF_LAT * cols // 16) * 16


def near_place(i, j, cols):
    band = band_rows(cols)
    if 0 <= j < cols:
        return band - HALF_LAT * cols + (i + HALF_LAT) * cols + j
    first = 2 * band + WIN_LAT * cols + (0 if j < 0 else SIDE)
    return first + (i + HALF_LAT) * HALF_LON + (j + HALF_LON if j < 0 else j - cols)


def near_windows(cols):
    cells, across = WIN_LAT * cols, cols // WIN_LON + 1
    near = 2 * (band_rows(cols) + SIDE) + cells
    order = np.zeros((2, across, PLACES, near), np.float32)
    back = np.zeros((cells, 2, across, PLACES), np.float32)
    for u in range(2):
        for v in range(across):
            for a in range(WIN_LAT):
                for e in range(WIN_LON):
                    i, j = u * WIN_LAT + a - HALF_LAT, v * WIN_LON + e - HALF_LON
                    place = e * WIN_LAT + a
                    order[u, v, place, near_place(i, j, cols)] = 1
                    if 0 <= i < WIN_LAT and 0 <= j < cols:
                        back[i * cols + j, u, v, place] = 1
    return order.reshape(-1, near), back.reshape(cells, -1)


def fixed(matrix):
    return jnp.asarray(matrix, BF16)


def norm_stats(values):
    row_mean = jnp.sum(values, axis=-1, keepdims=True) * (1.0 / D)
    centred = values - row_mean
    row_var = jnp.sum(centred * centred, axis=-1, keepdims=True) * (1.0 / D)
    inv_std = lax.rsqrt(row_var + NORM_EPS)
    return centred * inv_std, inv_std


def norm_back(d_float, unit_rows, inv_std, gain_row):
    d_unit = d_float * gain_row
    mean_grad = jnp.sum(d_unit, axis=-1, keepdims=True) * (1.0 / D)
    mean_proj = jnp.sum(d_unit * unit_rows, axis=-1, keepdims=True) * (1.0 / D)
    d_input = inv_std * (d_unit - mean_grad - unit_rows * mean_proj)
    return d_input, jnp.sum(d_float * unit_rows, axis=0, keepdims=True)


def position_bias(table, reach):
    table = table * LOG2E
    shifted = jnp.concatenate(
        [
            table[g * GROUP : (g + 1) * GROUP, (WIN_LAT - 1 - a2) * SPAN_LON : (WIN_LAT - 1 - a2) * SPAN_LON + REACH]
            for g in range(GROUPS)
            for a2 in range(WIN_LAT)
        ],
        axis=0,
    )
    high = shifted.astype(BF16)
    rest = shifted - high.astype(F32)
    middle = rest.astype(BF16)
    low = (rest - middle.astype(F32)).astype(BF16)
    spread = dot_nn(high, reach) + (dot_nn(middle, reach) + dot_nn(low, reach))
    return [spread[:, 128 * e2 : 128 * e2 + PLACES] for e2 in range(WIN_LON)]


def masked(blocks, keep_of, split_rows):
    rows = WIN_LAT * GROUP
    place = lax.broadcasted_iota(jnp.int32, (rows, PLACES), 1)
    key_row = lax.broadcasted_iota(jnp.int32, (rows, PLACES), 0) // GROUP
    query_late = jnp.where(place % WIN_LAT >= HALF_LAT, 1, 0)
    key_late = jnp.where(key_row >= HALF_LAT, 1, 0)
    shut = jnp.where(query_late == key_late, 0, 1) * split_rows
    for a2 in range(WIN_LAT):
        shut = shut + jnp.where(key_row == a2, 1, 0) * jnp.where(keep_of(a2) == 1, 0, 1)
    tile = jnp.where(shut > 0, SHUT, 0.0).astype(F32)
    return [
        jnp.concatenate([block[g * rows : (g + 1) * rows] + tile for block in blocks], axis=0).reshape(TILES, 8, PLACES)
        for g in range(GROUPS)
    ]


def own_head():
    head = lax.broadcasted_iota(jnp.int32, (8, 2 * INNER), 0) % GROUP
    lane = lax.broadcasted_iota(jnp.int32, (8, 2 * INNER), 1)
    return jnp.where((lane // HEAD_DIM) % GROUP == head, 1.0, 0.0).astype(F32)[None]


def sheet(array, g):
    return array[:, g * SHEET : (g + 1) * SHEET]


def own_parts(stacked, own):
    return (stacked.reshape(TILES, 8, 2 * INNER) * own).reshape(STACK, 2 * INNER).astype(BF16)


def stack_up(key_values, spread, own):
    stacks = [own_parts(stacked, own) for stacked in [dot_nn(spread, each) for each in key_values]]
    return [(stack[:, :INNER], stack[:, INNER:]) for stack in stacks]


def over_keys(combine, tiles):
    return combine(tiles, jnp.concatenate([tiles[GROUP:], tiles[:GROUP]], axis=0))


def attend(queries, stacks, biases):
    both = [(w, g) for w in range(len(queries)) for g in range(GROUPS)]
    scores = [dot_nt(sheet(stacks[w][0], g), sheet(queries[w], g)) for w, g in both]
    scores = [
        one.reshape(TILES, 8, PLACES) * (SCALE * LOG2E) + biases[w][g] for one, (w, g) in zip(scores, both)
    ]
    tops = [over_keys(jnp.maximum, jnp.max(one, axis=0)) for one in scores]
    exps = [jnp.exp2(one - top) for one, top in zip(scores, tops)]
    shares = [1.0 / over_keys(jnp.add, jnp.sum(one, axis=0)) for one in exps]
    probs = [one * share for one, share in zip(exps, shares)]
    lows = [one.reshape(STACK, PLACES).astype(BF16) for one in probs]
    outs = [dot_tn(low, sheet(stacks[w][1], g)).astype(BF16) for low, (w, g) in zip(lows, both)]
    per_window = [slice(w * GROUPS, (w + 1) * GROUPS) for w in range(len(queries))]
    return [probs[here] for here in per_window], [jnp.concatenate(outs[here], axis=1) for here in per_window]


def attend_back(d_outs, probs, queries, stacks, spread_back, own):
    both = [(w, g) for w in range(len(queries)) for g in range(GROUPS)]
    d_probs = [dot_nt(sheet(stacks[w][1], g), sheet(d_outs[w], g)) for w, g in both]
    d_probs = [one.reshape(TILES, 8, PLACES) for one in d_probs]
    totals = [over_keys(jnp.add, jnp.sum(one * probs[w][g], axis=0)) for one, (w, g) in zip(d_probs, both)]
    d_lows = [
        (probs[w][g] * (one - total) * SCALE).reshape(STACK, PLACES).astype(BF16)
        for one, total, (w, g) in zip(d_probs, totals, both)
    ]
    lows = [probs[w][g].reshape(STACK, PLACES).astype(BF16) for w, g in both]
    d_values = [dot_nn(low, sheet(d_outs[w], g)) for low, (w, g) in zip(lows, both)]
    d_keys = [dot_nn(d_low, sheet(queries[w], g)) for d_low, (w, g) in zip(d_lows, both)]
    d_queries = [dot_tn(d_low, sheet(stacks[w][0], g)).astype(BF16) for d_low, (w, g) in zip(d_lows, both)]
    per_window = [slice(w * GROUPS, (w + 1) * GROUPS) for w in range(len(queries))]
    d_stacks = [own_parts(jnp.concatenate(d_keys[here] + d_values[here], axis=1), own) for here in per_window]
    d_rest = [dot_nn(spread_back, d_stack).astype(BF16) for d_stack in d_stacks]
    return [jnp.concatenate(d_queries[here] + [rest], axis=1) for here, rest in zip(per_window, d_rest)]


def window_rows(array, w):
    return array[w * PLACES : (w + 1) * PLACES]


def first_kernel(
    odd_ref, row_ref, keep_ref, tokens_ref, mask_ref, embed_ref, gains_ref, w_qkv_ref, w_proj_ref, table_ref, cot_ref,
    order_ref, order_back_ref, spread_ref, reach_ref,
    wide_ref, qkv_ref, heads_ref, probs_ref, rolling_ref, one_ref, two_ref,
):
    rows, cols = mask_ref.shape
    mask = mask_ref[...].astype(F32)
    spread_mask = jnp.concatenate([jnp.broadcast_to(mask[r : r + 1], (cols, cols)) for r in range(rows)], axis=0)
    cell = lax.broadcasted_iota(jnp.int32, (rows * cols, cols), 0)
    lane = lax.broadcasted_iota(jnp.int32, (rows * cols, cols), 1)
    land = jnp.sum(jnp.where(cell % cols == lane, spread_mask, 0.0), axis=1, keepdims=True)
    embedded = tokens_ref[...].astype(F32) + jnp.where(land == 1.0, embed_ref[1:2], embed_ref[0:1])
    wide_ref[:, :D] = embedded
    unit_one, _ = norm_stats(embedded)
    normed_one = (unit_one * gains_ref[0:1]).astype(BF16)
    ordered = dot_nn(order_ref[...], normed_one).astype(BF16)
    qkv = dot_nn(ordered, w_qkv_ref[0]).astype(BF16)
    qkv_ref[...] = qkv
    bias = masked(position_bias(table_ref[0], reach_ref[...]), lambda a2: keep_ref[row_ref[0] + a2], 0)
    spread, own = spread_ref[...], own_head()
    windows = [window_rows(qkv, w) for w in range(cols // WIN_LON)]
    stacks = stack_up([here[:, INNER:] for here in windows], spread, own)
    all_probs, outs = attend([here[:, :INNER] for here in windows], stacks, [bias] * len(windows))
    for w, probs in enumerate(all_probs):
        for g in range(GROUPS):
            probs_ref[w, g] = probs[g]
    heads = dot_nn(order_back_ref[...], jnp.concatenate(outs, axis=0)).astype(BF16)
    heads_ref[...] = heads
    branch = dot_nn(heads, w_proj_ref[0]).astype(BF16)
    stream = embedded + branch.astype(F32)
    wide_ref[:, D:] = stream
    unit_two, _ = norm_stats(stream)
    normed_two = (unit_two * gains_ref[1:2]).astype(BF16)
    d_heads_two = dot_nt(cot_ref[...], w_proj_ref[1]).astype(BF16)
    rolling = jnp.concatenate([normed_two, d_heads_two], axis=1)
    rolling_ref[...] = rolling
    band = one_ref.shape[0]
    upper, lower = rolling[:band], rolling[rows * cols - band :]
    odd = odd_ref[0] == 1
    one_ref[...] = jnp.where(odd, lower, upper)
    two_ref[...] = jnp.where(odd, upper, lower)


def turn_kernel(after_ref, w_qkv_ref, w_proj_ref, qkv_back_ref, proj_back_ref):
    qkv_back_ref[0] = w_qkv_ref[0].T
    qkv_back_ref[1] = w_qkv_ref[1].T
    proj_back_ref[...] = w_proj_ref[0].T


def edge_kernel(cols, odd_ref, core_ref, one_ref, rolling_ref, two_ref, to_one_ref, to_two_ref):
    band, cells = one_ref.shape[0], rolling_ref.shape[0]
    tall = jnp.concatenate([one_ref[...], rolling_ref[...], two_ref[...]], axis=0)
    shape = (SIDE, tall.shape[0])
    row = lax.broadcasted_iota(jnp.int32, shape, 0)
    place = lax.broadcasted_iota(jnp.int32, shape, 1)
    i = row // HALF_LON
    far = odd_ref[0] * (band + cells)
    first = jnp.where(i < HALF_LAT, band - HALF_LAT * cols + far, band - HALF_LAT * cols)
    first = jnp.where(i >= HALF_LAT + WIN_LAT, first - far, first)
    source = first + i * cols + row % HALF_LON
    source = jnp.where(i < 2 * WIN_LAT, source, -1)
    shift = (cols - HALF_LON) * core_ref[0]
    for out_ref, column in ((to_one_ref, shift), (to_two_ref, cols - HALF_LON - shift)):
        pick = jnp.where(place == jnp.where(source < 0, -1, source + column), 1.0, 0.0).astype(BF16)
        out_ref[...] = dot_nn(pick, tall).astype(BF16)


def second_kernel(
    odd_ref, core_ref, row_ref, keep_ref, one_ref, rolling_ref, two_ref, side_one_ref, side_two_ref,
    wide_ref, qkv_ref, heads_ref, probs_ref, cot_ref, gains_ref, w_qkv_ref, qkv_back_ref, w_proj_ref, proj_back_ref, table_ref,
    order_ref, order_back_ref, near_order_ref, near_back_ref, spread_ref, spread_back_ref, reach_ref,
    output_ref, grad_ref, kept_ref, sent_ref,
):
    lat_count = keep_ref.shape[0]
    row_first = row_ref[0]
    spread, spread_back, own = spread_ref[...], spread_back_ref[...], own_head()
    odd, upper = odd_ref[0] == 1, core_ref[0] == 1
    one, two, side_one, side_two = one_ref[...], two_ref[...], side_one_ref[...], side_two_ref[...]
    near = jnp.concatenate(
        [
            jnp.where(odd, two, one), rolling_ref[...], jnp.where(odd, one, two),
            jnp.where(upper, side_two, side_one), jnp.where(upper, side_one, side_two),
        ],
        axis=0,
    )
    ordered = dot_nn(near_order_ref[...], near).astype(BF16)
    qkv_two = dot_nn(ordered[:, :D], w_qkv_ref[0]).astype(BF16)
    blocks = position_bias(table_ref[0], reach_ref[...])
    across = near_order_ref.shape[0] // PLACES // 2
    biases = []
    for u in range(2):

        def keep_of(a2, u=u):
            place = row_first + (u * WIN_LAT - HALF_LAT + a2)
            place = jnp.where(place < 0, place + lat_count, place)
            return keep_ref[jnp.where(place >= lat_count, place - lat_count, place)]

        last_band = jnp.where((row_first + u * WIN_LAT) % lat_count == 0, 1, 0)
        biases += [masked(blocks, keep_of, last_band)] * across
    windows = [window_rows(qkv_two, w) for w in range(2 * across)]
    d_outs = [window_rows(ordered, w)[:, D:] for w in range(2 * across)]
    queries = [here[:, :INNER] for here in windows]
    stacks = stack_up([here[:, INNER:] for here in windows], spread, own)
    all_probs, outs = attend(queries, stacks, biases)
    d_windows = attend_back(d_outs, all_probs, queries, stacks, spread_back, own)
    rows_two = jnp.concatenate([jnp.concatenate(d_windows, axis=0), jnp.concatenate(outs, axis=0)], axis=1)
    unrolled = dot_nn(near_back_ref[...], rows_two).astype(BF16)
    heads_two = unrolled[:, 3 * INNER :]
    d_normed_two = dot_nn(unrolled[:, : 3 * INNER], qkv_back_ref[1]).astype(BF16)

    stream = wide_ref[:, D:]
    unit_two, inv_two = norm_stats(stream)
    d_branch, gain_two = norm_back(d_normed_two.astype(F32), unit_two, inv_two, gains_ref[1:2])
    cotangent = cot_ref[...]
    d_stream = (cotangent.astype(F32) + d_branch).astype(BF16)
    branch_two = dot_nn(heads_two, w_proj_ref[0]).astype(BF16)
    output_ref[...] = stream + branch_two.astype(F32)
    proj_one = dot_tn(heads_ref[...], d_stream)
    proj_two = dot_tn(heads_two, cotangent)
    kept_ref[:INNER] = jnp.where(upper, proj_two, proj_one).astype(BF16)
    sent_ref[:INNER] = jnp.where(upper, proj_one, proj_two).astype(BF16)

    d_heads = dot_nn(d_stream, proj_back_ref[...]).astype(BF16)
    d_outs = dot_nn(order_ref[...], d_heads).astype(BF16)
    qkv_one = qkv_ref[...]
    windows = [window_rows(qkv_one, w) for w in range(probs_ref.shape[0])]
    d_outs = [window_rows(d_outs, w) for w in range(probs_ref.shape[0])]
    stacks = stack_up([here[:, INNER:] for here in windows], spread, own)
    all_probs = [[probs_ref[w, g] for g in range(GROUPS)] for w in range(probs_ref.shape[0])]
    d_windows = attend_back(d_outs, all_probs, [here[:, :INNER] for here in windows], stacks, spread_back, own)
    d_qkv = dot_nn(order_back_ref[...], jnp.concatenate(d_windows, axis=0)).astype(BF16)
    d_normed = dot_nn(d_qkv, qkv_back_ref[0]).astype(BF16)
    unit_one, inv_one = norm_stats(wide_ref[:, :D])
    d_branch, gain_one = norm_back(d_normed.astype(F32), unit_one, inv_one, gains_ref[0:1])
    grad_ref[...] = (d_stream.astype(F32) + d_branch).astype(BF16)
    gain = jnp.concatenate(
        [row[:, 128 * j : 128 * (j + 1)] for row in (gain_one, gain_two) for j in range(D // 128)], axis=0
    )
    pair = jnp.concatenate([gain_pair(gain), jnp.zeros((2 * GAIN_ROWS, D - 128), BF16)], axis=1)
    kept_ref[INNER:] = pair
    sent_ref[INNER:] = pair


def gain_pair(gain):
    high = gain.astype(BF16).astype(F32)
    return jnp.concatenate([high, gain - high], axis=0).astype(BF16)


def pair_sum(pair):
    return pair[:GAIN_ROWS] + pair[GAIN_ROWS : 2 * GAIN_ROWS]


def core_sum_kernel(kept_ref, landed_ref, out_ref):
    total = kept_ref[...].astype(F32) + landed_ref[...].astype(F32)
    low = total[:INNER].astype(BF16)
    pair = gain_pair(pair_sum(total[INNER:, :128]))
    pieces, tall = out_ref.shape[0], out_ref.shape[1]
    for s in range(pieces):
        fill_piece(out_ref, s, low[s * tall : (s + 1) * tall], pair)


def fill_piece(out_ref, s, low, pair):
    tall = out_ref.shape[1]
    out_ref[s, :, :D] = low
    out_ref[s, : 2 * GAIN_ROWS, D:] = pair
    if tall > 2 * GAIN_ROWS:
        out_ref[s, 2 * GAIN_ROWS :, D:] = jnp.zeros((tall - 2 * GAIN_ROWS, 128), BF16)


def added(parts_ref):
    total = parts_ref[0].astype(F32)
    for s in range(1, parts_ref.shape[0]):
        total = total + parts_ref[s].astype(F32)
    return total[:, :D], pair_sum(total[:, D:])


def near_sum_kernel(parts_ref, out_ref):
    proj, gain = added(parts_ref)
    low, pair = proj.astype(BF16), gain_pair(gain)
    for s in range(out_ref.shape[0]):
        fill_piece(out_ref, s, low, pair)


def far_sum_kernel(scale, parts_ref, proj_ref, gains_ref):
    proj, gain = added(parts_ref)
    low = (proj * scale).astype(BF16)
    for s in range(proj_ref.shape[0]):
        proj_ref[s] = low
    gains_ref[...] = gain * scale


def join_kernel(core_ref, mine_ref, other_ref, gain_ref, out_ref, gains_ref):
    gain, per_row = gain_ref[...], D // 128
    for r in range(GAIN_ROWS):
        gains_ref[r // per_row : r // per_row + 1, 128 * (r % per_row) : 128 * (r % per_row + 1)] = gain[r : r + 1]
    upper = core_ref[0] == 1
    mine, other = mine_ref[...], other_ref[...]
    out_ref[0] = jnp.where(upper, other, mine)
    out_ref[1] = jnp.where(upper, mine, other)


def scalars(array):
    return pltpu.with_memory_space_constraint(array, pltpu.HBM), pl.BlockSpec(memory_space=pltpu.SMEM)


def whole(array):
    return array, pl.BlockSpec(array.shape, functools.partial(lambda n, i: (0,) * n, array.ndim))


def in_hbm(array):
    return whole(pltpu.with_memory_space_constraint(array, pltpu.HBM))


def layer(array, index):
    spec = pl.BlockSpec((1,) + array.shape[1:], lambda i: (index,) + (0,) * (array.ndim - 1))
    return pltpu.with_memory_space_constraint(array, pltpu.HBM), spec


def hbm(*dims, dtype=BF16):
    return pltpu.HBM(dims, dtype)


def either(*dims, dtype=BF16):
    return jax.ShapeDtypeStruct(dims, dtype)


def call(kernel, outs, operands):
    arrays, specs = zip(*operands)
    out_specs = [pl.BlockSpec(o.shape, functools.partial(lambda n, i: (0,) * n, len(o.shape))) for o in outs]
    return pl.pallas_call(
        kernel,
        grid=(1,),
        in_specs=specs,
        out_specs=out_specs,
        out_shape=outs,
        compiler_params=pltpu.CompilerParams(vmem_limit_bytes=30 * 1024 * 1024),
    )(*arrays)


LON = ("z_mid", "z_low", "x", "core")
LAT = ("z_hi", "y_hi", "y_low")
NEAR = ("z_low", "x", "y_low")
FAR = ("z_mid", "z_hi", "y_hi")


def swapped(array, axes, side):
    length = lax.axis_size(axes)
    return lax.ppermute(array, axes, [(i, (i + (side if i % 2 else -side)) % length) for i in range(length)])


def local(tokens, land_mask, keep_rows, land_embed, norm_gains, w_qkv, w_proj, rel_bias, cotangent):
    rows, cols = tokens.shape[0], tokens.shape[1]
    cells, count = rows * cols, cols // WIN_LON
    band, wide = band_rows(cols), D + INNER
    scale_out = float(rows * lax.axis_size(LAT) * cols * lax.axis_size(LON)) ** (-0.5)
    row_first = scalars((lax.axis_index(LAT) * rows).astype(jnp.int32).reshape(1))
    odd = scalars((lax.axis_index(LAT) % 2).astype(jnp.int32).reshape(1))
    core = scalars(lax.axis_index("core").astype(jnp.int32).reshape(1))
    keep_in = scalars(keep_rows)
    order = own_windows(cols)
    order, order_back = in_hbm(fixed(order)), in_hbm(fixed(order.T))
    near_order, near_back = (in_hbm(fixed(m)) for m in near_windows(cols))
    spread = spread_matrix()
    spread, spread_back = in_hbm(fixed(spread)), in_hbm(fixed(spread.T))
    reach = in_hbm(fixed(reach_matrix()))
    cot_flat = in_hbm(cotangent.reshape(cells, D))

    wide_one, qkv_one, heads_one, probs_one, rolling, to_one, to_two = call(
        first_kernel,
        [
            either(cells, 2 * D, dtype=F32), either(count * PLACES, 3 * INNER), either(cells, INNER),
            either(count, GROUPS, TILES, 8, PLACES, dtype=F32), either(cells, wide), either(band, wide), either(band, wide),
        ],
        [
            odd, row_first, keep_in, in_hbm(tokens.reshape(cells, D)), in_hbm(land_mask), in_hbm(land_embed),
            in_hbm(norm_gains), layer(w_qkv, 0), in_hbm(w_proj), layer(rel_bias, 0), cot_flat,
            order, order_back, spread, reach,
        ],
    )

    one = swapped(to_one, LAT, 1)
    two = swapped(to_two, LAT, -1)
    qkv_back, proj_back = call(
        turn_kernel,
        [either(2, 3 * INNER, D), either(D, INNER)],
        [(to_two, pl.BlockSpec(memory_space=pl.ANY)), in_hbm(w_qkv), in_hbm(w_proj)],
    )
    to_one, to_two = call(
        functools.partial(edge_kernel, cols),
        [either(SIDE, wide), either(SIDE, wide)],
        [odd, core, whole(one), whole(rolling), whole(two)],
    )
    side_one = swapped(to_one, LON, 1)
    side_two = swapped(to_two, LON, -1)

    output, grad_tokens, kept, sent = call(
        second_kernel,
        [hbm(cells, D, dtype=F32), hbm(cells, D), either(INNER + 2 * GAIN_ROWS, D), either(INNER + 2 * GAIN_ROWS, D)],
        [
            odd, core, row_first, keep_in, whole(one), whole(rolling), whole(two), whole(side_one), whole(side_two),
            whole(wide_one), whole(qkv_one), whole(heads_one), whole(probs_one), cot_flat,
            in_hbm(norm_gains), layer(w_qkv, 1), whole(qkv_back), layer(w_proj, 1), whole(proj_back), layer(rel_bias, 1),
            order, order_back, near_order, near_back, spread, spread_back, reach,
        ],
    )

    near, far = lax.axis_size(NEAR), lax.axis_size(FAR)
    tall = INNER // near
    swap = [(0, 1), (1, 0)]
    landed = lax.ppermute(sent, "core", swap)
    (pieces,) = call(core_sum_kernel, [either(near, tall, D + 128)], [whole(kept), whole(landed)])
    parts = lax.all_to_all(pieces, NEAR, 0, 0, tiled=True)
    (pieces,) = call(near_sum_kernel, [either(far, tall, D + 128)], [whole(parts)])
    parts = lax.all_to_all(pieces, FAR, 0, 0, tiled=True)
    pieces, gain = call(
        functools.partial(far_sum_kernel, scale_out),
        [either(near, tall, D), either(GAIN_ROWS, 128, dtype=F32)],
        [whole(parts)],
    )
    mine = lax.all_to_all(pieces, NEAR, 0, 0, tiled=True).reshape(INNER, D)
    other = lax.ppermute(mine, "core", swap)
    grad_proj, grad_gains = call(
        join_kernel, [hbm(2, INNER, D), hbm(2, D, dtype=F32)], [core, whole(mine), whole(other), whole(gain)]
    )
    return output.reshape(rows, cols, D), grad_tokens.reshape(rows, cols, D), grad_proj, grad_gains


def halved(length):
    return (length // 2, 2) if length % 2 == 0 else (length, 1)


def chip_axes(lon, lat):
    x = min(4, lon // 2)
    y = min(8, lat)
    return (*halved(lon // (2 * x)), x, 2, lat // y, *halved(y))


def solution(mesh):
    sizes = chip_axes(mesh.shape["lon"], mesh.shape["lat"])
    fine = Mesh(mesh.devices.reshape(sizes), LON + LAT)
    grid = P(LAT, LON, None)
    in_specs = (grid, P(LAT, LON), P(), P(), P(), P(), P(), P(), grid)
    out_specs = (grid, grid, P(), P())
    return jax.shard_map(local, mesh=fine, in_specs=in_specs, out_specs=out_specs, check_vma=False)
```

```python
import functools

import jax
import jax.numpy as jnp
import numpy as np
from jax import lax
from jax.experimental import pallas as pl
from jax.experimental.pallas import tpu as pltpu
from jax.sharding import Mesh
from jax.sharding import PartitionSpec as P

D = 512
HEAD_DIM = 32
HEADS = 8
INNER = HEADS * HEAD_DIM
WIN_LAT = 6
WIN_LON = 12
HALF_LAT = WIN_LAT // 2
HALF_LON = WIN_LON // 2
WIN = WIN_LAT * WIN_LON
SPAN_LON = 2 * WIN_LON - 1
REACH = WIN_LAT * SPAN_LON
PLACES = 80
SIDE = 80
GROUP = 4
GROUPS = HEADS // GROUP
SHEET = GROUP * HEAD_DIM
TILES = WIN * GROUP // 8
LOG2E = 1.4426950408889634
STACK = WIN * GROUP
GAIN_ROWS = 8

NORM_EPS = 1e-05
SCALE = HEAD_DIM ** (-0.5)
SHUT = -1e30

F32 = jnp.float32
BF16 = jnp.bfloat16


def dot_nn(left, right):
    return lax.dot_general(left, right, (((1,), (0,)), ((), ())), preferred_element_type=F32)


def dot_nt(left, right):
    return lax.dot_general(left, right, (((1,), (1,)), ((), ())), preferred_element_type=F32)


def dot_tn(left, right):
    return lax.dot_general(left, right, (((0,), (0,)), ((), ())), preferred_element_type=F32)


def spread_matrix():
    spread = np.zeros((WIN, GROUP, PLACES), np.float32)
    for key in range(WIN):
        spread[key, :, key] = 1
    return spread.reshape(STACK, PLACES)


def reach_matrix():
    reach = np.zeros((REACH, WIN_LON, 128), np.float32)
    for e2 in range(WIN_LON):
        for a in range(WIN_LAT):
            for e in range(WIN_LON):
                reach[a * SPAN_LON + e - e2 + WIN_LON - 1, e2, e * WIN_LAT + a] = 1
    return reach.reshape(REACH, -1)


def own_windows(cols):
    order = np.zeros((cols // WIN_LON, PLACES, WIN_LAT * cols), np.float32)
    for w in range(cols // WIN_LON):
        for a in range(WIN_LAT):
            for e in range(WIN_LON):
                order[w, e * WIN_LAT + a, a * cols + w * WIN_LON + e] = 1
    return order.reshape(-1, WIN_LAT * cols)


def band_rows(cols):
    return -(-HALF_LAT * cols // 16) * 16


def near_place(i, j, cols):
    band = band_rows(cols)
    if 0 <= j < cols:
        return band - HALF_LAT * cols + (i + HALF_LAT) * cols + j
    first = 2 * band + WIN_LAT * cols + (0 if j < 0 else SIDE)
    return first + (i + HALF_LAT) * HALF_LON + (j + HALF_LON if j < 0 else j - cols)


def near_windows(cols):
    cells, across = WIN_LAT * cols, cols // WIN_LON + 1
    near = 2 * (band_rows(cols) + SIDE) + cells
    order = np.zeros((2, across, PLACES, near), np.float32)
    back = np.zeros((cells, 2, across, PLACES), np.float32)
    for u in range(2):
        for v in range(across):
            for a in range(WIN_LAT):
                for e in range(WIN_LON):
                    i, j = u * WIN_LAT + a - HALF_LAT, v * WIN_LON + e - HALF_LON
                    place = e * WIN_LAT + a
                    order[u, v, place, near_place(i, j, cols)] = 1
                    if 0 <= i < WIN_LAT and 0 <= j < cols:
                        back[i * cols + j, u, v, place] = 1
    return order.reshape(-1, near), back.reshape(cells, -1)


def fixed(matrix):
    return jnp.asarray(matrix, BF16)


def norm_stats(values):
    row_mean = jnp.sum(values, axis=-1, keepdims=True) * (1.0 / D)
    centred = values - row_mean
    row_var = jnp.sum(centred * centred, axis=-1, keepdims=True) * (1.0 / D)
    inv_std = lax.rsqrt(row_var + NORM_EPS)
    return centred * inv_std, inv_std


def norm_back(d_float, unit_rows, inv_std, gain_row):
    d_unit = d_float * gain_row
    mean_grad = jnp.sum(d_unit, axis=-1, keepdims=True) * (1.0 / D)
    mean_proj = jnp.sum(d_unit * unit_rows, axis=-1, keepdims=True) * (1.0 / D)
    d_input = inv_std * (d_unit - mean_grad - unit_rows * mean_proj)
    return d_input, jnp.sum(d_float * unit_rows, axis=0, keepdims=True)


def position_bias(table, reach):
    table = table * LOG2E
    shifted = jnp.concatenate(
        [
            table[g * GROUP : (g + 1) * GROUP, (WIN_LAT - 1 - a2) * SPAN_LON : (WIN_LAT - 1 - a2) * SPAN_LON + REACH]
            for g in range(GROUPS)
            for a2 in range(WIN_LAT)
        ],
        axis=0,
    )
    high = shifted.astype(BF16)
    rest = shifted - high.astype(F32)
    middle = rest.astype(BF16)
    low = (rest - middle.astype(F32)).astype(BF16)
    spread = dot_nn(high, reach) + (dot_nn(middle, reach) + dot_nn(low, reach))
    return [spread[:, 128 * e2 : 128 * e2 + PLACES] for e2 in range(WIN_LON)]


def masked(blocks, keep_of, split_rows):
    rows = WIN_LAT * GROUP
    place = lax.broadcasted_iota(jnp.int32, (rows, PLACES), 1)
    key_row = lax.broadcasted_iota(jnp.int32, (rows, PLACES), 0) // GROUP
    query_late = jnp.where(place % WIN_LAT >= HALF_LAT, 1, 0)
    key_late = jnp.where(key_row >= HALF_LAT, 1, 0)
    shut = jnp.where(query_late == key_late, 0, 1) * split_rows
    for a2 in range(WIN_LAT):
        shut = shut + jnp.where(key_row == a2, 1, 0) * jnp.where(keep_of(a2) == 1, 0, 1)
    tile = jnp.where(shut > 0, SHUT, 0.0).astype(F32)
    return [
        jnp.concatenate([block[g * rows : (g + 1) * rows] + tile for block in blocks], axis=0).reshape(TILES, 8, PLACES)
        for g in range(GROUPS)
    ]


def own_head():
    head = lax.broadcasted_iota(jnp.int32, (8, 2 * INNER), 0) % GROUP
    lane = lax.broadcasted_iota(jnp.int32, (8, 2 * INNER), 1)
    return jnp.where((lane // HEAD_DIM) % GROUP == head, 1.0, 0.0).astype(F32)[None]


def sheet(array, g):
    return array[:, g * SHEET : (g + 1) * SHEET]


def own_parts(stacked, own):
    return (stacked.reshape(TILES, 8, 2 * INNER) * own).reshape(STACK, 2 * INNER).astype(BF16)


def stack_up(key_values, spread, own):
    stacks = [own_parts(stacked, own) for stacked in [dot_nn(spread, each) for each in key_values]]
    return [(stack[:, :INNER], stack[:, INNER:]) for stack in stacks]


def over_keys(combine, tiles):
    return combine(tiles, jnp.concatenate([tiles[GROUP:], tiles[:GROUP]], axis=0))


def attend(queries, stacks, biases):
    both = [(w, g) for w in range(len(queries)) for g in range(GROUPS)]
    scores = [dot_nt(sheet(stacks[w][0], g), sheet(queries[w], g)) for w, g in both]
    scores = [
        one.reshape(TILES, 8, PLACES) * (SCALE * LOG2E) + biases[w][g] for one, (w, g) in zip(scores, both)
    ]
    tops = [over_keys(jnp.maximum, jnp.max(one, axis=0)) for one in scores]
    exps = [jnp.exp2(one - top) for one, top in zip(scores, tops)]
    shares = [1.0 / over_keys(jnp.add, jnp.sum(one, axis=0)) for one in exps]
    probs = [one * share for one, share in zip(exps, shares)]
    lows = [one.reshape(STACK, PLACES).astype(BF16) for one in probs]
    outs = [dot_tn(low, sheet(stacks[w][1], g)).astype(BF16) for low, (w, g) in zip(lows, both)]
    per_window = [slice(w * GROUPS, (w + 1) * GROUPS) for w in range(len(queries))]
    return [probs[here] for here in per_window], [jnp.concatenate(outs[here], axis=1) for here in per_window]


def attend_back(d_outs, probs, queries, stacks, spread_back, own):
    both = [(w, g) for w in range(len(queries)) for g in range(GROUPS)]
    d_probs = [dot_nt(sheet(stacks[w][1], g), sheet(d_outs[w], g)) for w, g in both]
    d_probs = [one.reshape(TILES, 8, PLACES) for one in d_probs]
    totals = [over_keys(jnp.add, jnp.sum(one * probs[w][g], axis=0)) for one, (w, g) in zip(d_probs, both)]
    d_lows = [
        (probs[w][g] * (one - total) * SCALE).reshape(STACK, PLACES).astype(BF16)
        for one, total, (w, g) in zip(d_probs, totals, both)
    ]
    lows = [probs[w][g].reshape(STACK, PLACES).astype(BF16) for w, g in both]
    d_values = [dot_nn(low, sheet(d_outs[w], g)) for low, (w, g) in zip(lows, both)]
    d_keys = [dot_nn(d_low, sheet(queries[w], g)) for d_low, (w, g) in zip(d_lows, both)]
    d_queries = [dot_tn(d_low, sheet(stacks[w][0], g)).astype(BF16) for d_low, (w, g) in zip(d_lows, both)]
    per_window = [slice(w * GROUPS, (w + 1) * GROUPS) for w in range(len(queries))]
    d_stacks = [own_parts(jnp.concatenate(d_keys[here] + d_values[here], axis=1), own) for here in per_window]
    d_rest = [dot_nn(spread_back, d_stack).astype(BF16) for d_stack in d_stacks]
    return [jnp.concatenate(d_queries[here] + [rest], axis=1) for here, rest in zip(per_window, d_rest)]


def window_rows(array, w):
    return array[w * PLACES : (w + 1) * PLACES]


def first_kernel(
    odd_ref, row_ref, keep_ref, tokens_ref, mask_ref, embed_ref, gains_ref, w_qkv_ref, w_proj_ref, table_ref, cot_ref,
    order_ref, order_back_ref, spread_ref, reach_ref,
    wide_ref, qkv_ref, heads_ref, probs_ref, rolling_ref, one_ref, two_ref,
):
    rows, cols = mask_ref.shape
    mask = mask_ref[...].astype(F32)
    spread_mask = jnp.concatenate([jnp.broadcast_to(mask[r : r + 1], (cols, cols)) for r in range(rows)], axis=0)
    cell = lax.broadcasted_iota(jnp.int32, (rows * cols, cols), 0)
    lane = lax.broadcasted_iota(jnp.int32, (rows * cols, cols), 1)
    land = jnp.sum(jnp.where(cell % cols == lane, spread_mask, 0.0), axis=1, keepdims=True)
    embedded = tokens_ref[...].astype(F32) + jnp.where(land == 1.0, embed_ref[1:2], embed_ref[0:1])
    wide_ref[:, :D] = embedded
    unit_one, _ = norm_stats(embedded)
    normed_one = (unit_one * gains_ref[0:1]).astype(BF16)
    ordered = dot_nn(order_ref[...], normed_one).astype(BF16)
    qkv = dot_nn(ordered, w_qkv_ref[0]).astype(BF16)
    qkv_ref[...] = qkv
    bias = masked(position_bias(table_ref[0], reach_ref[...]), lambda a2: keep_ref[row_ref[0] + a2], 0)
    spread, own = spread_ref[...], own_head()
    windows = [window_rows(qkv, w) for w in range(cols // WIN_LON)]
    stacks = stack_up([here[:, INNER:] for here in windows], spread, own)
    all_probs, outs = attend([here[:, :INNER] for here in windows], stacks, [bias] * len(windows))
    for w, probs in enumerate(all_probs):
        for g in range(GROUPS):
            probs_ref[w, g] = probs[g]
    heads = dot_nn(order_back_ref[...], jnp.concatenate(outs, axis=0)).astype(BF16)
    heads_ref[...] = heads
    branch = dot_nn(heads, w_proj_ref[0]).astype(BF16)
    stream = embedded + branch.astype(F32)
    wide_ref[:, D:] = stream
    unit_two, _ = norm_stats(stream)
    normed_two = (unit_two * gains_ref[1:2]).astype(BF16)
    d_heads_two = dot_nt(cot_ref[...], w_proj_ref[1]).astype(BF16)
    rolling = jnp.concatenate([normed_two, d_heads_two], axis=1)
    rolling_ref[...] = rolling
    band = one_ref.shape[0]
    upper, lower = rolling[:band], rolling[rows * cols - band :]
    odd = odd_ref[0] == 1
    one_ref[...] = jnp.where(odd, lower, upper)
    two_ref[...] = jnp.where(odd, upper, lower)


def turn_kernel(after_ref, w_qkv_ref, w_proj_ref, qkv_back_ref, proj_back_ref):
    qkv_back_ref[0] = w_qkv_ref[0].T
    qkv_back_ref[1] = w_qkv_ref[1].T
    proj_back_ref[...] = w_proj_ref[0].T


def edge_kernel(cols, odd_ref, core_ref, one_ref, rolling_ref, two_ref, after_ref, to_one_ref, to_two_ref):
    band, cells = one_ref.shape[0], rolling_ref.shape[0]
    tall = jnp.concatenate([one_ref[...], rolling_ref[...], two_ref[...]], axis=0)
    shape = (SIDE, tall.shape[0])
    row = lax.broadcasted_iota(jnp.int32, shape, 0)
    place = lax.broadcasted_iota(jnp.int32, shape, 1)
    i = row // HALF_LON
    far = odd_ref[0] * (band + cells)
    first = jnp.where(i < HALF_LAT, band - HALF_LAT * cols + far, band - HALF_LAT * cols)
    first = jnp.where(i >= HALF_LAT + WIN_LAT, first - far, first)
    source = first + i * cols + row % HALF_LON
    source = jnp.where(i < 2 * WIN_LAT, source, -1)
    shift = (cols - HALF_LON) * core_ref[0]
    for out_ref, column in ((to_one_ref, shift), (to_two_ref, cols - HALF_LON - shift)):
        pick = jnp.where(place == jnp.where(source < 0, -1, source + column), 1.0, 0.0).astype(BF16)
        out_ref[...] = dot_nn(pick, tall).astype(BF16)


def second_kernel(
    odd_ref, core_ref, row_ref, keep_ref, one_ref, rolling_ref, two_ref, side_one_ref, side_two_ref,
    wide_ref, qkv_ref, heads_ref, probs_ref, cot_ref, gains_ref, w_qkv_ref, qkv_back_ref, w_proj_ref, proj_back_ref, table_ref,
    order_ref, order_back_ref, near_order_ref, near_back_ref, spread_ref, spread_back_ref, reach_ref,
    output_ref, grad_ref, kept_ref, sent_ref,
):
    lat_count = keep_ref.shape[0]
    row_first = row_ref[0]
    spread, spread_back, own = spread_ref[...], spread_back_ref[...], own_head()
    odd, upper = odd_ref[0] == 1, core_ref[0] == 1
    one, two, side_one, side_two = one_ref[...], two_ref[...], side_one_ref[...], side_two_ref[...]
    near = jnp.concatenate(
        [
            jnp.where(odd, two, one), rolling_ref[...], jnp.where(odd, one, two),
            jnp.where(upper, side_two, side_one), jnp.where(upper, side_one, side_two),
        ],
        axis=0,
    )
    ordered = dot_nn(near_order_ref[...], near).astype(BF16)
    qkv_two = dot_nn(ordered[:, :D], w_qkv_ref[0]).astype(BF16)
    blocks = position_bias(table_ref[0], reach_ref[...])
    across = near_order_ref.shape[0] // PLACES // 2
    biases = []
    for u in range(2):

        def keep_of(a2, u=u):
            place = row_first + (u * WIN_LAT - HALF_LAT + a2)
            place = jnp.where(place < 0, place + lat_count, place)
            return keep_ref[jnp.where(place >= lat_count, place - lat_count, place)]

        last_band = jnp.where((row_first + u * WIN_LAT) % lat_count == 0, 1, 0)
        biases += [masked(blocks, keep_of, last_band)] * across
    windows = [window_rows(qkv_two, w) for w in range(2 * across)]
    d_outs = [window_rows(ordered, w)[:, D:] for w in range(2 * across)]
    queries = [here[:, :INNER] for here in windows]
    stacks = stack_up([here[:, INNER:] for here in windows], spread, own)
    all_probs, outs = attend(queries, stacks, biases)
    d_windows = attend_back(d_outs, all_probs, queries, stacks, spread_back, own)
    rows_two = jnp.concatenate([jnp.concatenate(d_windows, axis=0), jnp.concatenate(outs, axis=0)], axis=1)
    unrolled = dot_nn(near_back_ref[...], rows_two).astype(BF16)
    heads_two = unrolled[:, 3 * INNER :]
    d_normed_two = dot_nn(unrolled[:, : 3 * INNER], qkv_back_ref[1]).astype(BF16)

    stream = wide_ref[:, D:]
    unit_two, inv_two = norm_stats(stream)
    d_branch, gain_two = norm_back(d_normed_two.astype(F32), unit_two, inv_two, gains_ref[1:2])
    cotangent = cot_ref[...]
    d_stream = (cotangent.astype(F32) + d_branch).astype(BF16)
    branch_two = dot_nn(heads_two, w_proj_ref[0]).astype(BF16)
    output_ref[...] = stream + branch_two.astype(F32)
    proj_one = dot_tn(heads_ref[...], d_stream)
    proj_two = dot_tn(heads_two, cotangent)
    kept_ref[:INNER] = jnp.where(upper, proj_two, proj_one).astype(BF16)
    sent_ref[:INNER] = jnp.where(upper, proj_one, proj_two).astype(BF16)

    d_heads = dot_nn(d_stream, proj_back_ref[...]).astype(BF16)
    d_outs = dot_nn(order_ref[...], d_heads).astype(BF16)
    qkv_one = qkv_ref[...]
    windows = [window_rows(qkv_one, w) for w in range(probs_ref.shape[0])]
    d_outs = [window_rows(d_outs, w) for w in range(probs_ref.shape[0])]
    stacks = stack_up([here[:, INNER:] for here in windows], spread, own)
    all_probs = [[probs_ref[w, g] for g in range(GROUPS)] for w in range(probs_ref.shape[0])]
    d_windows = attend_back(d_outs, all_probs, [here[:, :INNER] for here in windows], stacks, spread_back, own)
    d_qkv = dot_nn(order_back_ref[...], jnp.concatenate(d_windows, axis=0)).astype(BF16)
    d_normed = dot_nn(d_qkv, qkv_back_ref[0]).astype(BF16)
    unit_one, inv_one = norm_stats(wide_ref[:, :D])
    d_branch, gain_one = norm_back(d_normed.astype(F32), unit_one, inv_one, gains_ref[0:1])
    grad_ref[...] = (d_stream.astype(F32) + d_branch).astype(BF16)
    gain = jnp.concatenate(
        [row[:, 128 * j : 128 * (j + 1)] for row in (gain_one, gain_two) for j in range(D // 128)], axis=0
    )
    pair = jnp.concatenate([gain_pair(gain), jnp.zeros((2 * GAIN_ROWS, D - 128), BF16)], axis=1)
    kept_ref[INNER:] = pair
    sent_ref[INNER:] = pair


def gain_pair(gain):
    high = gain.astype(BF16).astype(F32)
    return jnp.concatenate([high, gain - high], axis=0).astype(BF16)


def pair_sum(pair):
    return pair[:GAIN_ROWS] + pair[GAIN_ROWS : 2 * GAIN_ROWS]


def core_sum_kernel(kept_ref, landed_ref, out_ref):
    total = kept_ref[...].astype(F32) + landed_ref[...].astype(F32)
    low = total[:INNER].astype(BF16)
    pair = gain_pair(pair_sum(total[INNER:, :128]))
    pieces, tall = out_ref.shape[0], out_ref.shape[1]
    for s in range(pieces):
        fill_piece(out_ref, s, low[s * tall : (s + 1) * tall], pair)


def fill_piece(out_ref, s, low, pair):
    tall = out_ref.shape[1]
    out_ref[s, :, :D] = low
    out_ref[s, : 2 * GAIN_ROWS, D:] = pair
    if tall > 2 * GAIN_ROWS:
        out_ref[s, 2 * GAIN_ROWS :, D:] = jnp.zeros((tall - 2 * GAIN_ROWS, 128), BF16)


def added(parts_ref):
    total = parts_ref[0].astype(F32)
    for s in range(1, parts_ref.shape[0]):
        total = total + parts_ref[s].astype(F32)
    return total[:, :D], pair_sum(total[:, D:])


def near_sum_kernel(parts_ref, out_ref):
    proj, gain = added(parts_ref)
    low, pair = proj.astype(BF16), gain_pair(gain)
    for s in range(out_ref.shape[0]):
        fill_piece(out_ref, s, low, pair)


def far_sum_kernel(scale, parts_ref, proj_ref, gains_ref):
    proj, gain = added(parts_ref)
    low = (proj * scale).astype(BF16)
    for s in range(proj_ref.shape[0]):
        proj_ref[s] = low
    gains_ref[...] = gain * scale


def join_kernel(core_ref, mine_ref, other_ref, gain_ref, out_ref, gains_ref):
    gain, per_row = gain_ref[...], D // 128
    for r in range(GAIN_ROWS):
        gains_ref[r // per_row : r // per_row + 1, 128 * (r % per_row) : 128 * (r % per_row + 1)] = gain[r : r + 1]
    upper = core_ref[0] == 1
    mine, other = mine_ref[...], other_ref[...]
    out_ref[0] = jnp.where(upper, other, mine)
    out_ref[1] = jnp.where(upper, mine, other)


def scalars(array):
    return pltpu.with_memory_space_constraint(array, pltpu.HBM), pl.BlockSpec(memory_space=pltpu.SMEM)


def whole(array):
    return array, pl.BlockSpec(array.shape, functools.partial(lambda n, i: (0,) * n, array.ndim))


def in_hbm(array):
    return whole(pltpu.with_memory_space_constraint(array, pltpu.HBM))


def layer(array, index):
    spec = pl.BlockSpec((1,) + array.shape[1:], lambda i: (index,) + (0,) * (array.ndim - 1))
    return pltpu.with_memory_space_constraint(array, pltpu.HBM), spec


def hbm(*dims, dtype=BF16):
    return pltpu.HBM(dims, dtype)


def either(*dims, dtype=BF16):
    return jax.ShapeDtypeStruct(dims, dtype)


def call(kernel, outs, operands):
    arrays, specs = zip(*operands)
    out_specs = [pl.BlockSpec(o.shape, functools.partial(lambda n, i: (0,) * n, len(o.shape))) for o in outs]
    return pl.pallas_call(
        kernel,
        grid=(1,),
        in_specs=specs,
        out_specs=out_specs,
        out_shape=outs,
        compiler_params=pltpu.CompilerParams(vmem_limit_bytes=30 * 1024 * 1024),
    )(*arrays)


LON = ("z_mid", "z_low", "x", "core")
LAT = ("z_hi", "y_hi", "y_low")
NEAR = ("z_low", "x", "y_low")
FAR = ("z_mid", "z_hi", "y_hi")


def swapped(array, axes, side):
    length = lax.axis_size(axes)
    return lax.ppermute(array, axes, [(i, (i + (side if i % 2 else -side)) % length) for i in range(length)])


def local(tokens, land_mask, keep_rows, land_embed, norm_gains, w_qkv, w_proj, rel_bias, cotangent):
    rows, cols = tokens.shape[0], tokens.shape[1]
    cells, count = rows * cols, cols // WIN_LON
    band, wide = band_rows(cols), D + INNER
    scale_out = float(rows * lax.axis_size(LAT) * cols * lax.axis_size(LON)) ** (-0.5)
    row_first = scalars((lax.axis_index(LAT) * rows).astype(jnp.int32).reshape(1))
    odd = scalars((lax.axis_index(LAT) % 2).astype(jnp.int32).reshape(1))
    core = scalars(lax.axis_index("core").astype(jnp.int32).reshape(1))
    keep_in = scalars(keep_rows)
    order = own_windows(cols)
    order, order_back = in_hbm(fixed(order)), in_hbm(fixed(order.T))
    near_order, near_back = (in_hbm(fixed(m)) for m in near_windows(cols))
    spread = spread_matrix()
    spread, spread_back = in_hbm(fixed(spread)), in_hbm(fixed(spread.T))
    reach = in_hbm(fixed(reach_matrix()))
    cot_flat = in_hbm(cotangent.reshape(cells, D))

    wide_one, qkv_one, heads_one, probs_one, rolling, to_one, to_two = call(
        first_kernel,
        [
            either(cells, 2 * D, dtype=F32), either(count * PLACES, 3 * INNER), either(cells, INNER),
            either(count, GROUPS, TILES, 8, PLACES, dtype=F32), either(cells, wide), either(band, wide), either(band, wide),
        ],
        [
            odd, row_first, keep_in, in_hbm(tokens.reshape(cells, D)), in_hbm(land_mask), in_hbm(land_embed),
            in_hbm(norm_gains), layer(w_qkv, 0), in_hbm(w_proj), layer(rel_bias, 0), cot_flat,
            order, order_back, spread, reach,
        ],
    )

    one = swapped(to_one, LAT, 1)
    two = swapped(to_two, LAT, -1)
    qkv_back, proj_back = call(
        turn_kernel,
        [either(2, 3 * INNER, D), either(D, INNER)],
        [(to_two, pl.BlockSpec(memory_space=pl.ANY)), in_hbm(w_qkv), in_hbm(w_proj)],
    )
    to_one, to_two = call(
        functools.partial(edge_kernel, cols),
        [either(SIDE, wide), either(SIDE, wide)],
        [odd, core, whole(one), whole(rolling), whole(two), (proj_back, pl.BlockSpec(memory_space=pl.ANY))],
    )
    side_one = swapped(to_one, LON, 1)
    side_two = swapped(to_two, LON, -1)

    output, grad_tokens, kept, sent = call(
        second_kernel,
        [hbm(cells, D, dtype=F32), hbm(cells, D), either(INNER + 2 * GAIN_ROWS, D), either(INNER + 2 * GAIN_ROWS, D)],
        [
            odd, core, row_first, keep_in, whole(one), whole(rolling), whole(two), whole(side_one), whole(side_two),
            whole(wide_one), whole(qkv_one), whole(heads_one), whole(probs_one), cot_flat,
            in_hbm(norm_gains), layer(w_qkv, 1), whole(qkv_back), layer(w_proj, 1), whole(proj_back), layer(rel_bias, 1),
            order, order_back, near_order, near_back, spread, spread_back, reach,
        ],
    )

    near, far = lax.axis_size(NEAR), lax.axis_size(FAR)
    tall = INNER // near
    swap = [(0, 1), (1, 0)]
    landed = lax.ppermute(sent, "core", swap)
    (pieces,) = call(core_sum_kernel, [either(near, tall, D + 128)], [whole(kept), whole(landed)])
    parts = lax.all_to_all(pieces, NEAR, 0, 0, tiled=True)
    (pieces,) = call(near_sum_kernel, [either(far, tall, D + 128)], [whole(parts)])
    parts = lax.all_to_all(pieces, FAR, 0, 0, tiled=True)
    pieces, gain = call(
        functools.partial(far_sum_kernel, scale_out),
        [either(near, tall, D), either(GAIN_ROWS, 128, dtype=F32)],
        [whole(parts)],
    )
    mine = lax.all_to_all(pieces, NEAR, 0, 0, tiled=True).reshape(INNER, D)
    other = lax.ppermute(mine, "core", swap)
    grad_proj, grad_gains = call(
        join_kernel, [hbm(2, INNER, D), hbm(2, D, dtype=F32)], [core, whole(mine), whole(other), whole(gain)]
    )
    return output.reshape(rows, cols, D), grad_tokens.reshape(rows, cols, D), grad_proj, grad_gains


def halved(length):
    return (length // 2, 2) if length % 2 == 0 else (length, 1)


def chip_axes(lon, lat):
    x = min(4, lon // 2)
    y = min(8, lat)
    return (*halved(lon // (2 * x)), x, 2, lat // y, *halved(y))


def solution(mesh):
    sizes = chip_axes(mesh.shape["lon"], mesh.shape["lat"])
    fine = Mesh(mesh.devices.reshape(sizes), LON + LAT)
    grid = P(LAT, LON, None)
    in_specs = (grid, P(LAT, LON), P(), P(), P(), P(), P(), P(), grid)
    out_specs = (grid, grid, P(), P())
    return jax.shard_map(local, mesh=fine, in_specs=in_specs, out_specs=out_specs, check_vma=False)
```
